32 devices in a mesh: fsdp: 2 (over x), ctx: 4 (over y, core), tp: 4 (over z).
Axes of the slice: x: 2, y: 2, z: 4, core: 2. Of those that a mesh axis runs over, the one named last changes fastest.
Arguments:
- layer_input: bfloat16 [8, 1024, 768], P('fsdp', 'ctx'), may hold values from -6 to 6
- gain_attn: bfloat16 [768], P('fsdp'), may hold values from 0.5 to 1.5
- query_weight: bfloat16 [768, 768], P('fsdp', 'tp'), may hold values from -0.21875 to 0.21875
- key_weight: bfloat16 [768, 768], P('fsdp', 'tp'), may hold values from -0.21875 to 0.21875
- value_weight: bfloat16 [768, 768], P('fsdp', 'tp'), may hold values from -0.21875 to 0.21875
- output_weight: bfloat16 [768, 768], P('tp', 'fsdp'), may hold values from -1.75 to 1.75
- gain_ffn: bfloat16 [768], P('fsdp'), may hold values from 0.5 to 1.5
- router: bfloat16 [768, 8], P('fsdp'), may hold values from -0.15625 to 0.15625
- exp_gate: bfloat16 [8, 768, 2048], P(None, 'fsdp', 'tp'), may hold values from -0.21875 to 0.21875
- exp_up: bfloat16 [8, 768, 2048], P(None, 'fsdp', 'tp'), may hold values from -0.21875 to 0.21875
- exp_down: bfloat16 [8, 2048, 768], P(None, 'tp', 'fsdp'), may hold values from -0.5 to 0.5
- shared_gate_weight: bfloat16 [768, 2048], P('fsdp', 'tp'), may hold values from -0.21875 to 0.21875
- shared_up_weight: bfloat16 [768, 2048], P('fsdp', 'tp'), may hold values from -0.21875 to 0.21875
- shared_down_weight: bfloat16 [2048, 768], P('tp', 'fsdp'), may hold values from -0.125 to 0.125
- routes: int32 [8, 1024, 2], P('fsdp', 'ctx'), may hold values from 0 to 7, all different within a row; in each aligned block of 256 rows (0 to 255, 256 to 511, ..., all dimensions but the last counted through in order) at most 80 rows name the same one
- prefix: int32 [8], P('fsdp'), may hold values from 102 to 512
- cotangent: bfloat16 [8, 1024, 768], P('fsdp', 'ctx'), may hold values from -6 to 6
Outputs:
- activations: bfloat16 [8, 1024, 768], P('fsdp', 'ctx')
- grad_input: float32 [8, 1024, 768], P('fsdp', 'ctx')
- grad_gain_attn: float32 [768], P(('fsdp', 'ctx'))
- grad_w_query: float32 [768, 768], P(('fsdp', 'ctx'), 'tp')
- grad_w_key: float32 [768, 768], P(('fsdp', 'ctx'), 'tp')
- grad_w_value: float32 [768, 768], P(('fsdp', 'ctx'), 'tp')
- grad_w_out: float32 [768, 768], P('tp', ('fsdp', 'ctx'))
- grad_gain_ffn: float32 [768], P(('fsdp', 'ctx'))
- grad_router: float32 [768, 8], P(('fsdp', 'ctx'))
- grad_exp_gate: float32 [8, 768, 2048], P(None, ('fsdp', 'ctx'), 'tp')
- grad_exp_up: float32 [8, 768, 2048], P(None, ('fsdp', 'ctx'), 'tp')
- grad_exp_down: float32 [8, 2048, 768], P(None, 'tp', ('fsdp', 'ctx'))
- grad_shared_gate: float32 [768, 2048], P(('fsdp', 'ctx'), 'tp')
- grad_shared_up: float32 [768, 2048], P(('fsdp', 'ctx'), 'tp')
- grad_shared_down: float32 [2048, 768], P('tp', ('fsdp', 'ctx'))
The draws below stay inside these ranges and needn't reach their ends.
Inputs may be any that keep to these rules, and one draw needn't show every extreme that they name: `routes`: A token's two experts differ. In each aligned block of 256 rows (the tokens of one sequence on one index of ctx) no expert is named by more than 80 rows, a bound that some block reaches.
All inputs are finite; a program needn't handle non-finite values.
Results may differ from the reference program's by a relative error of at most 0.02.
Values may be sent and summed in bfloat16 or wider, within the bound.
No kernel may reach another device: no remote copies, remote signals or barrier semaphores. Data moves between devices by JAX's collectives and lax.ppermute only.
A program may use at most 320 MiB of HBM per device.

```python
import math
import jax
import jax.numpy as jnp
import numpy as np
from jax import lax

MODEL_DIM = 768
HEADS = 12
HD = 64
FF = 2048
EXPERT_COUNT = 8
EXPERT_SLOTS = 80
LEN = 1024
QLEN = 256
SEQS = 8
N_CTX = 4


def place_ends(values, stream_key, least, high):
    spot = [jax.random.randint(jax.random.fold_in(stream_key, axis), (), 0, length) for axis, length in enumerate(values.shape)]
    main_axis = values.shape.index(max(values.shape))
    next_to = spot[:main_axis] + [(spot[main_axis] + 1) % values.shape[main_axis]] + spot[main_axis + 1:]
    return values.at[tuple(spot)].set(least).at[tuple(next_to)].set(high)


def raised(entries, key, source, target, shards_of, factor):
    def block_of(position):
        return (jnp.arange(entries.shape[position]) // (entries.shape[position] // shards_of)).reshape((-1,) + (1,) * (entries.ndim - 1 - position))

    near = jax.random.permutation(key, shards_of)[block_of(target)]
    other_side = (block_of(target) + shards_of // 2) % shards_of
    return jnp.where((block_of(source) == near) | (block_of(source) == other_side), factor * entries, entries)


def block_scale(key, shape, cuts, smallest, high):
    factor_of, own = 1.0, jax.random.fold_in(key, 6)
    for axis_at, blocks in cuts:
        draws = jnp.exp(jax.random.uniform(jax.random.fold_in(own, axis_at), (blocks,), jnp.float32, smallest / len(cuts), high / len(cuts)))
        factor_of = factor_of * jnp.repeat(draws, shape[axis_at] // blocks).reshape([-1 if axis == axis_at else 1 for axis in range(len(shape))])
    return factor_of


def assign_block(rng, own, number, rows, number_of, top, reach, skew):
    sequence = jax.random.permutation(rng, number_of)
    heavy_load, usual = portions_of(number_of, rows * top, reach, skew, True), portions_of(number_of, rows * top, reach, skew, False)
    places = jnp.arange(number_of)

    def named(sizes, rotation):
        used = int((sizes > 0).sum())
        fixed = max(1, used // 4)
        moved = fixed + (places - fixed + rotation * (used - fixed)) % max(1, number_of - fixed)
        return jnp.zeros((number_of,), jnp.int32).at[sequence[jnp.where(places < fixed, places, moved)]].set(jnp.asarray(sizes, jnp.int32))

    sizes = jnp.where(number % 4 == 0, named(heavy_load, number // 4), named(usual, number - number // 4 - 1))
    mixed = jax.random.permutation(jax.random.fold_in(own, 3), number_of)
    giver, receiver = mixed[0:number_of // 2 * 2:2], mixed[1:number_of // 2 * 2:2]
    slack = jnp.minimum(sizes[giver] - 1, reach - sizes[receiver]) // 2
    slack = jnp.where((giver == sequence[0]) | (receiver == sequence[0]) | (sizes[receiver] == 0), 0, jnp.maximum(slack, 0))
    moved = jax.random.randint(jax.random.fold_in(own, 4), (number_of // 2,), 0, 1 << 20) % (slack + 1)
    sizes = sizes.at[giver].add(-moved).at[receiver].add(moved)
    members = jnp.searchsorted(jnp.cumsum(sizes), jnp.arange(rows * top), side="right").astype(jnp.int32)
    listing = members.reshape(top, rows).T
    listing = listing[jax.random.permutation(jax.random.fold_in(own, 1), rows)]
    rotation = jax.random.randint(jax.random.fold_in(own, 2), (rows, 1), 0, top)
    return jnp.take_along_axis(listing, (jnp.arange(top)[None, :] + rotation) % top, axis=1)


def portions_of(number_of, total, most, skew, full):
    portions = [(1 << 20) // math.isqrt(grade ** skew) + 1 for grade in range(1, number_of + 1)]
    largest = most if full else min(most, max(-(-total // number_of), total * portions[0] // sum(portions)))
    least = 1 if total - largest >= number_of - 1 else 0
    holding, spare = [largest] + [least] * (number_of - 1), total - largest - least * (number_of - 1)
    while spare > 0:
        candidates = [i for i in range(1, number_of) if holding[i] < largest] or [i for i in range(1, number_of) if holding[i] < most]
        whole, left = sum([portions[i] for i in candidates]), spare
        for i in candidates:
            extra = min(most - holding[i], max(1, left * portions[i] // whole), spare)
            holding[i] = holding[i] + extra
            spare = spare - extra
    return np.array(holding)


def scatter_about(rng, extent, deviation, bound, cuts=(), kind=jnp.bfloat16):
    entries = deviation * jax.random.normal(rng, extent, jnp.float32)
    if cuts:
        entries = entries * block_scale(rng, extent, cuts, -0.22, 0.18)
    return jnp.clip(entries, -bound, bound).astype(kind)


def noise_with(key, extent, spread, most, cuts, heavy, held_as=jnp.bfloat16):
    drawn = spread * jax.random.normal(key, extent, jnp.float32)
    if cuts:
        drawn = drawn * block_scale(key, extent, cuts, -0.22, 0.18)
    return jnp.clip(raised(drawn, jax.random.fold_in(key, 3), *heavy), -most, most).astype(held_as)


def setup_inputs(seed: int = 0) -> dict:
    key_list = jax.random.split(jax.random.key(seed), 18)
    layer_input = noise_with(key_list[0], (SEQS, LEN, MODEL_DIM), 1.0, 6.0, ((0, 2), (1, 4)), (0, 2, 2, 2.0))
    gain_attn = jnp.clip(1.0 + 0.1 * jax.random.normal(key_list[1], (MODEL_DIM,), jnp.float32), 0.5, 1.5).astype(jnp.bfloat16)
    query_weight = scatter_about(key_list[2], (MODEL_DIM, HEADS * HD), MODEL_DIM ** -0.5, 0.21875, ((0, 2), (1, 4)))
    key_weight = scatter_about(key_list[3], (MODEL_DIM, HEADS * HD), MODEL_DIM ** -0.5, 0.21875, ((0, 2), (1, 4)))
    value_weight = scatter_about(key_list[4], (MODEL_DIM, HEADS * HD), MODEL_DIM ** -0.5, 0.21875, ((0, 2), (1, 4)))
    output_weight = scatter_about(key_list[5], (HEADS * HD, MODEL_DIM), (max(HEADS * HD // 64, 1)) ** -0.5, 1.75, ((0, 4), (1, 2)))
    gain_ffn = jnp.clip(1.0 + 0.1 * jax.random.normal(key_list[6], (MODEL_DIM,), jnp.float32), 0.5, 1.5).astype(jnp.bfloat16)
    router = scatter_about(key_list[7], (MODEL_DIM, EXPERT_COUNT), (16 * MODEL_DIM // 9) ** -0.5, 0.15625, ((0, 2),))
    exp_gate = scatter_about(key_list[8], (EXPERT_COUNT, MODEL_DIM, FF), MODEL_DIM ** -0.5, 0.21875, ((1, 2), (2, 4)))
    exp_up = scatter_about(key_list[9], (EXPERT_COUNT, MODEL_DIM, FF), MODEL_DIM ** -0.5, 0.21875, ((1, 2), (2, 4)))
    exp_down = scatter_about(key_list[10], (EXPERT_COUNT, FF, MODEL_DIM), (FF // 16) ** -0.5, 0.5, ((1, 4), (2, 2)))
    shared_gate_weight = scatter_about(key_list[11], (MODEL_DIM, FF), MODEL_DIM ** -0.5, 0.21875, ((0, 2), (1, 4)))
    shared_up_weight = scatter_about(key_list[12], (MODEL_DIM, FF), MODEL_DIM ** -0.5, 0.21875, ((0, 2), (1, 4)))
    shared_down_weight = scatter_about(key_list[13], (FF, MODEL_DIM), FF ** -0.5, 0.125, ((0, 4), (1, 2)))
    routes_keys = jax.random.split(jax.random.fold_in(key_list[14], 1), SEQS * LEN // QLEN)
    routes_turns = jax.random.permutation(jax.random.fold_in(key_list[14], 3), SEQS * LEN // QLEN)
    routes = jax.vmap(lambda own, number: assign_block(jax.random.fold_in(key_list[14], 2), own, number, QLEN, EXPERT_COUNT, 2, EXPERT_SLOTS, 1))(routes_keys, routes_turns).reshape((SEQS, LEN, 2))
    prefix = place_ends(jax.random.randint(key_list[15], (SEQS,), LEN // 10, LEN // 2 + 1), jax.random.fold_in(key_list[15], 1), LEN // 10, (LEN // 2 + 1) - 1).astype(jnp.int32)
    cotangent = noise_with(key_list[16], (SEQS, LEN, MODEL_DIM), 1.0, 6.0, ((0, 2), (1, 4)), (0, 2, 2, 2.0))
    return dict(layer_input=layer_input, gain_attn=gain_attn, query_weight=query_weight, key_weight=key_weight, value_weight=value_weight, output_weight=output_weight, gain_ffn=gain_ffn, router=router, exp_gate=exp_gate, exp_up=exp_up, exp_down=exp_down, shared_gate_weight=shared_gate_weight, shared_up_weight=shared_up_weight, shared_down_weight=shared_down_weight, routes=routes, prefix=prefix, cotangent=cotangent)


EPS = 1e-06

@jax.custom_vjp
def reduced_precision(v):
    return lax.optimization_barrier(v.astype(jnp.bfloat16)).astype(jnp.float32)

@jax.custom_vjp
def reduced_backward(v):
    return v

def low_keep(v):
    return (reduced_precision(v), None)

def low_pass(kept, grad):
    return (grad,)

def back_keep(v):
    return (v, None)

def back_low(kept, grad):
    return (reduced_precision(grad),)
reduced_precision.defvjp(low_keep, low_pass)
reduced_backward.defvjp(back_keep, back_low)

def einsum_product(form, left, right):
    return jnp.einsum(form, left, right, precision=lax.Precision.HIGHEST)

def rms_scale(value_rows):
    return lax.rsqrt(lax.optimization_barrier(jnp.mean(value_rows * value_rows, -1, keepdims=True)) + EPS)

def rope_tables(positions, half):
    inverse = jnp.exp(jnp.arange(half, dtype=jnp.float32) * (-math.log(10000.0) / half))
    angles = positions.astype(jnp.float32)[:, None] * inverse[None, :]
    return (jnp.cos(angles), jnp.sin(angles))

def rotate(value_rows, cosine, sine):
    half = value_rows.shape[-1] // 2
    first = value_rows[..., :half]
    second = value_rows[..., half:]
    cosine = cosine[:, None, :]
    sine = sine[:, None, :]
    return jnp.concatenate([first * cosine - second * sine, second * cosine + first * sine], axis=-1)

def attend(pieces):
    query_rows, key_rows, value_rows, start = pieces
    sequence_length = query_rows.shape[0]
    scores = reduced_backward(einsum_product('ihd,jhd->hij', query_rows, key_rows) * HD ** (-0.5))
    places = jnp.arange(sequence_length, dtype=jnp.int32)
    seen = (places[None, :] <= places[:, None]) | (places[None, :] < start)
    scores = jnp.where(seen[None], scores, -1e+30)
    peak = lax.optimization_barrier(jnp.max(scores, -1, keepdims=True))
    expo = jnp.exp(scores - peak)
    probs = expo / lax.optimization_barrier(jnp.sum(expo, -1, keepdims=True))
    return einsum_product('hij,jhd->ihd', reduced_precision(probs), value_rows)

def block_forward(layer_inputs, gain_attn, query_weight, key_weight, value_weight, output_weight, gain_ffn, router, exp_gate, exp_up, exp_down, shared_gate_weight, shared_up_weight, shared_down_weight, route_group, prefix_group):
    slot_count = layer_inputs.shape[0]
    sequence_length = layer_inputs.shape[1]
    first_normed = reduced_precision(layer_inputs * rms_scale(layer_inputs) * gain_attn)
    split_into_heads = (slot_count, sequence_length, HEADS, HD)
    cosine, sine = rope_tables(jnp.arange(sequence_length, dtype=jnp.int32), HD // 2)
    query_rows = reduced_backward(einsum_product('jqn,nr->jqr', first_normed, query_weight)).reshape(split_into_heads)
    key_rows = reduced_backward(einsum_product('jqn,nr->jqr', first_normed, key_weight)).reshape(split_into_heads)
    value_rows = reduced_precision(reduced_backward(einsum_product('jqn,nr->jqr', first_normed, value_weight))).reshape(split_into_heads)
    query_rows = reduced_precision(rotate(query_rows, cosine, sine))
    key_rows = reduced_precision(rotate(key_rows, cosine, sine))
    attention_result = lax.map(jax.checkpoint(attend), (query_rows, key_rows, value_rows, prefix_group))
    attention_result = reduced_precision(reduced_backward(attention_result)).reshape(slot_count, sequence_length, HEADS * HD)
    middle_state = layer_inputs + reduced_backward(einsum_product('zpg,gv->zpv', attention_result, output_weight))
    second_normed = reduced_precision(middle_state * rms_scale(middle_state) * gain_ffn)
    router_logits = reduced_backward(einsum_product('jqn,nr->jqr', second_normed, router))
    expo = jnp.exp(router_logits)
    gates = expo / lax.optimization_barrier(jnp.sum(expo, -1, keepdims=True))
    block_list = slot_count * N_CTX
    rows_per_block = sequence_length // N_CTX
    flat_routes = route_group.reshape(block_list, rows_per_block * 2).astype(jnp.int32)
    hot = (flat_routes[:, :, None] == jnp.arange(EXPERT_COUNT, dtype=jnp.int32)[None, None, :]).astype(jnp.int32)
    place = lax.optimization_barrier(jnp.sum((jnp.cumsum(hot, axis=1) - hot) * hot, -1)).astype(jnp.int32)
    slots = flat_routes * EXPERT_SLOTS + place
    picker = (slots[:, None, :] == jnp.arange(EXPERT_COUNT * EXPERT_SLOTS, dtype=jnp.int32)[None, :, None]).astype(jnp.float32)
    picker = picker.reshape(block_list, EXPERT_COUNT, EXPERT_SLOTS, rows_per_block, 2)
    dispatch_matrix = lax.optimization_barrier(jnp.sum(picker, -1))
    expert_input = einsum_product('jpxs,jsy->pjxy', dispatch_matrix, second_normed.reshape(block_list, rows_per_block, MODEL_DIM)).reshape(EXPERT_COUNT, block_list * EXPERT_SLOTS, MODEL_DIM)
    gate_act = reduced_backward(einsum_product('end,edf->enf', expert_input, exp_gate))
    up_act = reduced_backward(einsum_product('end,edf->enf', expert_input, exp_up))
    expert_hid = reduced_precision(jax.nn.silu(gate_act) * up_act)
    expert_output = reduced_backward(einsum_product('enf,efd->end', expert_hid, exp_down)).reshape(EXPERT_COUNT, block_list, EXPERT_SLOTS, MODEL_DIM)
    chosen = jnp.take_along_axis(gates.reshape(block_list, rows_per_block, EXPERT_COUNT), route_group.reshape(block_list, rows_per_block, 2).astype(jnp.int32), axis=-1)
    combine_weights = einsum_product('becqt,bqt->becq', picker, chosen)
    expert_mixture = einsum_product('jrhw,rjht->jwt', combine_weights, expert_output).reshape(slot_count, sequence_length, MODEL_DIM)
    shared_gate_act = reduced_backward(einsum_product('awn,nh->awh', second_normed, shared_gate_weight))
    shared_up_act = reduced_backward(einsum_product('awn,nh->awh', second_normed, shared_up_weight))
    shared_hidden = reduced_precision(jax.nn.silu(shared_gate_act) * shared_up_act)
    shared_output = reduced_backward(einsum_product('kyn,nt->kyt', shared_hidden, shared_down_weight))
    return middle_state + expert_mixture + shared_output

def reference(layer_input, gain_attn, query_weight, key_weight, value_weight, output_weight, gain_ffn, router, exp_gate, exp_up, exp_down, shared_gate_weight, shared_up_weight, shared_down_weight, routes, prefix, cotangent):
    weights = tuple((item.astype(jnp.float32) for item in (gain_attn, query_weight, key_weight, value_weight, output_weight, gain_ffn, router, exp_gate, exp_up, exp_down, shared_gate_weight, shared_up_weight, shared_down_weight)))
    group = math.gcd(SEQS, max(1, 4096 // LEN))
    rounds = SEQS // group
    layer_inputs = layer_input.astype(jnp.float32).reshape(rounds, group, LEN, MODEL_DIM)
    upstream = cotangent.astype(jnp.float32).reshape(rounds, group, LEN, MODEL_DIM)
    route_groups = routes.reshape(rounds, group, LEN, 2)
    prefix_groups = prefix.reshape(rounds, group)

    def one_group(totals, pieces):
        inputs_group, upstream_group, routes_group, prefixes = pieces

        def forward(block_in, *params):
            return block_forward(block_in, *params, routes_group, prefixes)
        result, pullback = jax.vjp(forward, inputs_group, *weights)
        grads = pullback(upstream_group)
        totals = tuple((total + grad for total, grad in zip(totals, grads[1:])))
        return (totals, (result.astype(jnp.bfloat16), grads[0]))
    zeros = tuple((jnp.zeros_like(item) for item in weights))
    totals, (results, input_grads) = lax.scan(one_group, zeros, (layer_inputs, upstream, route_groups, prefix_groups))
    return (results.reshape(SEQS, LEN, MODEL_DIM), input_grads.reshape(SEQS, LEN, MODEL_DIM), totals[0], totals[1], totals[2], totals[3], totals[4], totals[5], totals[6], totals[7], totals[8], totals[9], totals[10], totals[11], totals[12])
```

```python
import functools
import math

import jax
import jax.numpy as jnp
from jax import lax
from jax.experimental import pallas as pl
from jax.experimental.pallas import tpu as pltpu
from jax.sharding import PartitionSpec as P

HD = 64
SLOTS = 80
EPS = 1e-06
F32 = jnp.float32
BF16 = jnp.bfloat16
VMEM_BYTES = 56 * 1024 * 1024


def mm(a, b):
    return lax.dot_general(a, b, (((1,), (0,)), ((), ())), preferred_element_type=F32)


def mm_nt(a, b):
    return lax.dot_general(a, b, (((1,), (1,)), ((), ())), preferred_element_type=F32)


def mm_tn(a, b):
    return lax.dot_general(a, b, (((0,), (0,)), ((), ())), preferred_element_type=F32)


def params(steps=1):
    return pltpu.CompilerParams(
        dimension_semantics=("arbitrary",) * steps, vmem_limit_bytes=VMEM_BYTES
    )


def rotation(width):
    row = lax.broadcasted_iota(jnp.int32, (width, width), 0)
    col = lax.broadcasted_iota(jnp.int32, (width, width), 1)
    first = (col % HD) < HD // 2
    minus = first & (row == col + HD // 2)
    plus = jnp.logical_not(first) & (row == col - HD // 2)
    return jnp.where(minus, -1.0, jnp.where(plus, 1.0, 0.0)).astype(BF16)


def row_scale(value):
    return lax.rsqrt(jnp.mean(value * value, -1, keepdims=True) + EPS)


def qkv_kernel(scal, x_ref, own_ref, oth_ref, cos_ref, sin_ref, n1_ref, q_ref, kv_ref, w_ref, small_ref, swap):
    half = own_ref.shape[0]

    @pl.when(pl.program_id(0) == 0)
    def _():
        mine = pl.multiple_of(scal[0] * half, half)
        other = pl.multiple_of((1 - scal[0]) * half, half)
        w_ref[pl.ds(mine, half), :] = own_ref[...]
        w_ref[pl.ds(other, half), :] = oth_ref[...]
        swap[...] = mm(w_ref[...], rotation(w_ref.shape[1])).astype(BF16)
        turned = jnp.transpose(w_ref[:, 128:256].astype(F32))
        small_ref[...] = turned[64:80, :]

    x = x_ref[0].astype(F32)
    n1 = (x * row_scale(x) * small_ref[8:9, :]).astype(BF16)
    n1_ref[0] = n1
    turned = mm(n1, w_ref[...]) * cos_ref[...] + mm(n1, swap[...]) * sin_ref[...]
    q_ref[0] = turned[:, :192].astype(BF16)
    kv_ref[0] = turned[:, 256:640].astype(BF16)


def visible(scal, prefix, keys, rows):
    key_pos = lax.broadcasted_iota(jnp.int32, (keys, rows), 0) ^ (scal[1] * rows)
    row_pos = lax.broadcasted_iota(jnp.int32, (keys, rows), 1) + scal[1] * rows
    return (key_pos <= row_pos) | (key_pos < prefix[pl.program_id(0)])


def only_head(rows, head):
    lane = lax.broadcasted_iota(jnp.int32, rows.shape, 1)
    return jnp.where((lane >= head * HD) & (lane < (head + 1) * HD), rows, jnp.zeros_like(rows))


def attn_fwd_kernel(scal, prefix, q_ref, kv0, kv1, kv2, kv3, o_ref, lse_ref):
    q = q_ref[0]
    rows, width = q.shape
    heads = width // HD
    kv = jnp.concatenate([kv0[0], kv1[0], kv2[0], kv3[0]], axis=0)
    k = kv[:, :width]
    value_t = jnp.transpose(kv[:, width:].astype(F32)).astype(BF16)
    seen = visible(scal, prefix, kv.shape[0], rows)
    outs = []
    for head in range(heads):
        scores = mm_nt(k, only_head(q, head) * (HD ** -0.5))
        scores = jnp.where(seen, scores, -1e30)
        peak = jnp.max(scores, 0, keepdims=True)
        expo = jnp.exp(scores - peak)
        total = jnp.sum(expo, 0, keepdims=True)
        probs = (expo * (1.0 / total)).astype(BF16)
        outs.append(mm(value_t[head * HD:(head + 1) * HD], probs))
        lse_ref[0, head:head + 1, :] = peak + jnp.log(total)
    o = jnp.transpose(jnp.concatenate(outs, axis=0))
    o_ref[0] = jnp.concatenate([o[: rows // 2], o[rows // 2:]], axis=1).astype(BF16)


def post_kernel(scal, o_ref, wo_ref, x_ref, small_ref, routes_ref, n2_ref, h2_ref, gates_ref, slots_ref, wo):
    step = pl.program_id(0)
    zs, width = wo_ref.shape[1], wo_ref.shape[2]
    half = wo_ref.shape[3]

    @pl.when(step == 0)
    def _():
        for z in range(zs):
            for side in range(2):
                wo[z * width:(z + 1) * width, side * half:(side + 1) * half] = wo_ref[side, z]

    low = jnp.zeros((o_ref.shape[2], 2 * half), F32)
    high = low
    for z in range(zs):
        block = o_ref[z, 0]
        weights = wo[z * width:(z + 1) * width, :]
        low += mm(block[:, :width], weights)
        high += mm(block[:, width:], weights)
    h2 = x_ref[0].astype(F32) + jnp.concatenate([low, high], axis=0)
    n2 = (h2 * row_scale(h2) * small_ref[9:10, :]).astype(BF16)
    n2_ref[0] = n2

    @pl.when(step == scal[2])
    def _():
        h2_ref[...] = h2

    expo = jnp.exp(mm_nt(small_ref[0:8, :].astype(BF16), n2))
    gates_ref[0] = expo / jnp.sum(expo, 0, keepdims=True)
    rows = n2.shape[0]
    expert = lax.broadcasted_iota(jnp.int32, (8, rows), 0)
    named = (routes_ref[0, 0:1, :] == expert) | (routes_ref[0, 1:2, :] == expert)
    before = lax.broadcasted_iota(jnp.int32, (rows, rows), 0) < lax.broadcasted_iota(jnp.int32, (rows, rows), 1)
    place = mm(named.astype(BF16), before.astype(BF16))
    slots_ref[0] = jnp.where(named, place.astype(jnp.int32), -1)


def silu_parts(value):
    sigma = 1.0 / (1.0 + jnp.exp(-value))
    return sigma, value * sigma


def split_blocks(core, value, blocks):
    rows = value.shape[0] // (2 * blocks)
    value = value.astype(BF16).reshape(blocks, 2, rows, value.shape[1])
    first = core == 0
    return jnp.where(first, value[:, 0], value[:, 1]), jnp.where(first, value[:, 1], value[:, 0])


def put_grads(core, keep_ref, send_ref, index, value):
    keep, send = split_blocks(core, value, keep_ref.shape[0])
    at = slice(index * keep.shape[1], (index + 1) * keep.shape[1])
    keep_ref[:, 0, at, :] = keep
    send_ref[:, 0, at, :] = send


def shared_kernel(
    scal, n2_ref, dy_ref, go_ref, uo_ref, do_ref, g0, g1, g2, g3, u0, u1, u2, u3, d0, d1, d2, d3,
    ys_ref, dn_ref, keep_ref, send_ref, wg, wu, wd, hs_s, da_s, db_s,
):
    step = pl.program_id(0)
    seqs, rows, width = n2_ref.shape
    half = go_ref.shape[0]
    hidden = go_ref.shape[1]

    @pl.when(step == 0)
    def _():
        mine = pl.multiple_of(scal[0] * half, half)
        other = (1 - scal[0]) * half
        wg[pl.ds(mine, half), :] = go_ref[...]
        wu[pl.ds(mine, half), :] = uo_ref[...]
        wd[:, pl.ds(mine, half)] = do_ref[...]
        for piece, (g, u, d) in enumerate(((g0, u0, d0), (g1, u1, d1), (g2, u2, d2), (g3, u3, d3))):
            quarter = scal[3] ^ piece
            at = pl.multiple_of(other + quarter * (half // 4), half // 4)
            wg[pl.ds(at, half // 4), :] = g[...]
            wu[pl.ds(at, half // 4), :] = u[...]
            at = pl.multiple_of(quarter * (hidden // 4), hidden // 4)
            wd[pl.ds(at, hidden // 4), pl.ds(pl.multiple_of(other, half), half)] = d[...]

    @pl.when(step < seqs)
    def _():
        n2 = n2_ref[step]
        dy = dy_ref[step]
        gate = mm(n2, wg[...])
        up = mm(n2, wu[...])
        sigma, silu = silu_parts(gate)
        hid = (silu * up).astype(BF16)
        ys_ref[0] = mm(hid, wd[...]).astype(BF16)
        back = mm_nt(dy, wd[...])
        da = (back * up * (sigma * (1.0 + gate * (1.0 - sigma)))).astype(BF16)
        db = (back * silu).astype(BF16)
        dn_ref[0] = (mm_nt(da, wg[...]) + mm_nt(db, wu[...])).astype(BF16)
        at = pl.ds(pl.multiple_of(step * rows, rows), rows)
        hs_s[at, :] = hid
        da_s[at, :] = da
        db_s[at, :] = db

    @pl.when(step == seqs)
    def _():
        n2 = n2_ref[...].reshape(seqs * rows, width)
        put_grads(scal[4], keep_ref, send_ref, 0, mm_tn(n2, da_s[...]))
        put_grads(scal[4], keep_ref, send_ref, 1, mm_tn(n2, db_s[...]))
        put_grads(scal[4], keep_ref, send_ref, 2, mm_tn(dy_ref[...].reshape(seqs * rows, width), hs_s[...]))


def moe_kernel(
    scal, n2_ref, dy_ref, slots_ref, gates_ref, ys_ref, dn_in_ref, go_ref, uo_ref, do_ref,
    g0, g1, g2, g3, u0, u1, u2, u3, d0, d1, d2, d3, keep_in, send_in,
    y_ref, dn_ref, keep_ref, send_ref, wg, wu, wd, pick_s, ye_s, dx_s, xe_s, dy_s, de_s, gs_s, dprob_s,
):
    step = pl.program_id(0)
    seqs, rows, width = n2_ref.shape
    half = go_ref.shape[1]
    experts = slots_ref.shape[1]

    @pl.when(step < experts)
    def _():
        piece = step // 2
        expert = 2 * (piece ^ scal[3]) + step % 2
        mine = pl.multiple_of(scal[0] * half, half)
        other = pl.multiple_of((1 - scal[0]) * half, half)
        wg[pl.ds(mine, half), :] = go_ref[0]
        wu[pl.ds(mine, half), :] = uo_ref[0]
        wd[:, pl.ds(mine, half)] = do_ref[0]
        for index, (g, u, d) in enumerate(((g0, u0, d0), (g1, u1, d1), (g2, u2, d2), (g3, u3, d3))):
            @pl.when(piece == index)
            def _(g=g, u=u, d=d):
                wg[pl.ds(other, half), :] = g[...]
                wu[pl.ds(other, half), :] = u[...]
                wd[:, pl.ds(other, half)] = d[...]

        slot_at = pl.ds(pl.multiple_of(step * SLOTS, 16), SLOTS)
        slot = lax.broadcasted_iota(jnp.int32, (SLOTS, rows), 0)
        for s in range(seqs):
            at = slice(s * SLOTS, (s + 1) * SLOTS)
            hit = slots_ref[s, pl.ds(expert, 1), :] == slot
            gate_slot = jnp.sum(jnp.where(hit, gates_ref[s, pl.ds(expert, 1), :], 0.0), 1, keepdims=True)
            pick = hit.astype(BF16)
            pick_s[s, slot_at, :] = pick
            xe_s[at, :] = mm(pick, n2_ref[s]).astype(BF16)
            upstream = mm(pick, dy_ref[s])
            dy_s[at, :] = upstream.astype(BF16)
            de_s[at, :] = (gate_slot * upstream).astype(BF16)
            gs_s[at, :] = jnp.broadcast_to(gate_slot, (SLOTS, 128))

        xe = xe_s[...]
        gate = mm(xe, wg[...])
        up = mm(xe, wu[...])
        sigma, silu = silu_parts(gate)
        hid = (silu * up).astype(BF16)
        ye = mm(hid, wd[...])
        dots = jnp.sum(ye * dy_s[...].astype(F32), 1, keepdims=True)
        ye = (ye * gs_s[:, 0:1]).astype(BF16)
        for s in range(seqs):
            at = slice(s * SLOTS, (s + 1) * SLOTS)
            ye_s[s, slot_at, :] = ye[at]
            hit = slots_ref[s, pl.ds(expert, 1), :] == slot
            dprob_s[s, pl.ds(expert, 1), :] = jnp.sum(jnp.where(hit, dots[at], 0.0), 0, keepdims=True)
        back = mm_nt(de_s[...], wd[...])
        da = (back * up * (sigma * (1.0 + gate * (1.0 - sigma)))).astype(BF16)
        db = (back * silu).astype(BF16)
        dx = (mm_nt(da, wg[...]) + mm_nt(db, wu[...])).astype(BF16)
        for s in range(seqs):
            dx_s[s, slot_at, :] = dx[s * SLOTS:(s + 1) * SLOTS]
        put_grads(scal[4], keep_ref, send_ref, 0, mm_tn(xe_s[...], da))
        put_grads(scal[4], keep_ref, send_ref, 1, mm_tn(xe_s[...], db))
        put_grads(scal[4], keep_ref, send_ref, 2, mm_tn(de_s[...], hid))

    @pl.when(step >= experts)
    def _():
        s = step - experts
        pick = pick_s[s]
        y_ref[0] = (ys_ref[0].astype(F32) + mm_tn(pick, ye_s[s])).astype(BF16)
        dn_ref[0, 0:rows, :] = (dn_in_ref[0].astype(F32) + mm_tn(pick, dx_s[s])).astype(BF16)
        tail = jnp.concatenate([dprob_s[s], jnp.zeros((dn_ref.shape[1] - rows - experts, rows), F32)], axis=0)
        tail = jnp.concatenate([tail, jnp.zeros((tail.shape[0], width - rows), F32)], axis=1)
        dn_ref[0, rows:, :] = tail.astype(BF16)


def norm_back(grad_out, value, scale, gain):
    weighted = grad_out * gain
    return scale * weighted - value * (scale * scale * scale) * jnp.mean(weighted * value, -1, keepdims=True)


def mid_kernel(scal, dn_ref, gates_ref, h2_ref, n2_ref, dy_ref, small_ref, wo_ref, dh2_ref, do_ref, low_ref, sums_ref, wo):
    rows = h2_ref.shape[0]
    zs, width, half = wo_ref.shape[1:]
    for z in range(zs):
        for side in range(2):
            wo[z * width:(z + 1) * width, side * half:(side + 1) * half] = wo_ref[side, z]
    gates = gates_ref[0]
    dprob = dn_ref[0, rows:rows + 8, 0:rows].astype(F32)
    dlogits = (gates * (dprob - jnp.sum(dprob * gates, 0, keepdims=True))).astype(BF16)
    dn2 = dn_ref[0, 0:rows, :].astype(F32) + mm_tn(dlogits, small_ref[0:8, :].astype(BF16))
    h2 = h2_ref[...]
    scale = row_scale(h2)
    sums_ref[0:8, :] = mm(dlogits, n2_ref[0])
    sums_ref[8:16, :] = jnp.zeros((8, h2.shape[1]), F32)
    sums_ref[9:10, :] = jnp.sum(dn2 * h2 * scale, 0, keepdims=True)
    dh2 = dy_ref[0].astype(F32) + norm_back(dn2, h2, scale, small_ref[9:10, :])
    dh2_ref[...] = dh2
    low = dh2.astype(BF16)
    low_ref[...] = low
    for z in range(zs):
        do = mm_nt(low, wo[z * width:(z + 1) * width, :])
        do_ref[z] = jnp.concatenate([do[: rows // 2], do[rows // 2:]], axis=1).astype(BF16)


def attn_bwd_kernel(
    scal, prefix, q_ref, kv0, kv1, kv2, kv3, lse_ref, do_ref, cos_ref, sin_ref, dq_ref, e0, e1, e2, e3
):
    q = q_ref[0]
    rows, width = q.shape
    heads = width // HD
    kv = jnp.concatenate([kv0[0], kv1[0], kv2[0], kv3[0]], axis=0)
    k = kv[:, :width]
    v = kv[:, width:]
    key_t = jnp.transpose(k.astype(F32)).astype(BF16)
    do = jnp.concatenate([do_ref[0][:, :width], do_ref[0][:, width:]], axis=0)
    seen = visible(scal, prefix, kv.shape[0], rows)
    cosine, sine = cos_ref[...], sin_ref[...]
    turned, ds_all, probs_all, q_all, do_all = [], [], [], [], []
    for head in range(heads):
        q_head = only_head(q, head) * (HD ** -0.5)
        do_head = only_head(do, head)
        scores = mm_nt(k, q_head)
        probs = jnp.where(seen, jnp.exp(scores - lse_ref[0, head:head + 1, :]), 0.0)
        dp = mm_nt(v, do_head)
        ds = (probs * (dp - jnp.sum(dp * probs, 0, keepdims=True))).astype(BF16)
        dq = mm(key_t[head * HD:(head + 1) * HD], ds) * (HD ** -0.5)
        first, second = dq[: HD // 2], dq[HD // 2:]
        turned += [first * cosine + second * sine, second * cosine - first * sine]
        ds_all.append(ds)
        probs_all.append(probs.astype(BF16))
        q_all.append(q_head)
        do_all.append(do_head)
    dq_ref[0] = jnp.transpose(jnp.concatenate(turned, axis=0)).astype(BF16)
    dk = mm(jnp.concatenate(ds_all, axis=1), jnp.concatenate(q_all, axis=0))
    dv = mm(jnp.concatenate(probs_all, axis=1), jnp.concatenate(do_all, axis=0))
    dkv = jnp.concatenate([dk, dv], axis=1).astype(BF16)
    for piece, out in enumerate((e0, e1, e2, e3)):
        out[0] = dkv[piece * rows:(piece + 1) * rows]


def last_kernel(scal, dq_ref, a_ref, b_ref, c_ref, n1_ref, w_ref, cos_ref, sin_ref, dh_ref, o_ref, dn1_ref, keep_ref, send_ref, all_s, o_s):
    step = pl.program_id(0)
    steps, rows, width = n1_ref.shape
    head_cols = dq_ref.shape[2]
    packed = w_ref.shape[1]
    at = pl.ds(pl.multiple_of(step * rows, rows), rows)
    dkv = a_ref[0].astype(F32) + b_ref[0].astype(F32) + c_ref[0].astype(F32)
    swung = dkv * sin_ref[:, 256:]
    high = swung.astype(BF16)
    low = (swung - high.astype(F32)).astype(BF16)
    turn = rotation(dkv.shape[1])
    dkv = dkv * cos_ref[:, 256:] + mm_nt(high, turn) + mm_nt(low, turn)
    all_s[at, :head_cols] = dq_ref[0]
    all_s[at, head_cols:256] = jnp.zeros((rows, 256 - head_cols), BF16)
    all_s[at, 256:] = dkv.astype(BF16)
    dn1_ref[0] = mm_nt(all_s[at, :], w_ref[...]).astype(BF16)
    block = o_ref[0]
    o_s[at, :] = jnp.concatenate([block[:, :head_cols], block[:, head_cols:]], axis=0)

    @pl.when(step == steps - 1)
    def _():
        blocks = keep_ref.shape[0]
        n1 = n1_ref[...].reshape(steps * rows, width)
        keep_ref[:, :, 0:packed], send_ref[:, :, 0:packed] = split_blocks(scal[4], mm_tn(n1, all_s[...]), blocks)
        out_t = mm_tn(dh_ref[...].reshape(steps * rows, width), o_s[...])
        rest = keep_ref.shape[2] - packed - head_cols
        out_t = jnp.concatenate([out_t, jnp.zeros((width, rest), F32)], axis=1)
        keep_ref[:, :, packed:], send_ref[:, :, packed:] = split_blocks(scal[4], out_t, blocks)


def end_kernel(scal, dn1_ref, dh2_ref, x_ref, small_ref, sums_in, gi_ref, sums_ref):
    x = x_ref[0].astype(F32)
    dn1 = dn1_ref[0].astype(F32)
    scale = row_scale(x)
    sums_ref[...] = sums_in[...]
    sums_ref[8:9, :] = jnp.sum(dn1 * x * scale, 0, keepdims=True)
    gi_ref[...] = (dh2_ref[...] + norm_back(dn1, x, scale, small_ref[8:9, :])).astype(BF16)


def whole(shape):
    return pl.BlockSpec(shape, lambda *_: (0,) * len(shape))


def by_step(shape):
    return pl.BlockSpec((1,) + shape, lambda i, *_: (i,) + (0,) * len(shape))


def call(kernel, grid, in_specs, out_specs, out_shape, scratch=(), prefetch=1, aliases=None, flops=0, nbytes=0):
    return pl.pallas_call(
        kernel,
        grid_spec=pltpu.PrefetchScalarGridSpec(
            num_scalar_prefetch=prefetch,
            grid=grid,
            in_specs=in_specs,
            out_specs=out_specs,
            scratch_shapes=scratch,
        ),
        out_shape=out_shape,
        input_output_aliases=aliases or {},
        compiler_params=params(len(grid)),
        cost_estimate=pl.CostEstimate(flops=int(flops), bytes_accessed=int(nbytes), transcendentals=0),
    )


def shape_of(shape, dtype=BF16):
    return jax.ShapeDtypeStruct(shape, dtype)


def body(
    fsdp_size,
    layer_input,
    gain_attn,
    query_weight,
    key_weight,
    value_weight,
    output_weight,
    gain_ffn,
    router,
    exp_gate,
    exp_up,
    exp_down,
    shared_gate_weight,
    shared_up_weight,
    shared_down_weight,
    routes,
    prefix,
    cotangent,
):
    seqs, rows, width = layer_input.shape
    experts = exp_gate.shape[0]
    hidden = exp_gate.shape[2]
    head_cols = query_weight.shape[1]
    half = width // 2
    paired = fsdp_size == 2
    ctx = lax.axis_index("ctx")
    tp = lax.axis_index("tp")
    ctx_size = lax.axis_size("ctx")
    tp_size = lax.axis_size("tp")
    side = lax.axis_index("fsdp") if paired else jnp.int32(0)
    weight_ctx = ctx if paired else jnp.int32(0)
    blocks = fsdp_size * ctx_size
    direct = paired and ctx_size == 4
    core = ctx % 2 if direct else jnp.int32(0)
    scal = jnp.stack([side, ctx, tp, weight_ctx, core]).astype(jnp.int32)

    def over_x(value):
        return lax.ppermute(value, "fsdp", [(0, 1), (1, 0)])

    def over_ctx(value, bit):
        return lax.ppermute(value, "ctx", [(i, i ^ bit) for i in range(ctx_size)])

    columns = jnp.concatenate(
        [
            query_weight,
            router,
            gain_attn[:, None],
            gain_ffn[:, None],
            jnp.zeros((query_weight.shape[0], 54), BF16),
            key_weight,
            value_weight,
        ],
        axis=1,
    )
    if paired:
        columns_own, columns_other = columns, over_x(columns)
    else:
        columns = lax.all_gather(columns, "fsdp", axis=0, tiled=True)
        columns_own, columns_other = columns[:half], columns[half:]

    if paired:
        def quarter(stack, shared):
            mine = lax.dynamic_slice_in_dim(stack, 2 * ctx, 2, 0).reshape(-1, stack.shape[2])
            part = shared.shape[0] // 4
            return jnp.concatenate([mine, lax.dynamic_slice_in_dim(shared, part * ctx, part, 0)], axis=0)

        def pieces(stack, shared):
            first = over_x(quarter(stack, shared))
            return first

        gate_0 = pieces(exp_gate, shared_gate_weight)
        up_0 = pieces(exp_up, shared_up_weight)
        down_0 = pieces(exp_down, shared_down_weight)
        own = (exp_gate, exp_up, exp_down, shared_gate_weight, shared_up_weight, shared_down_weight)
    else:
        gate_all = lax.all_gather(exp_gate, "fsdp", axis=1, tiled=True)
        up_all = lax.all_gather(exp_up, "fsdp", axis=1, tiled=True)
        down_all = lax.all_gather(exp_down, "fsdp", axis=2, tiled=True)
        sg_all = lax.all_gather(shared_gate_weight, "fsdp", axis=0, tiled=True)
        su_all = lax.all_gather(shared_up_weight, "fsdp", axis=0, tiled=True)
        sd_all = lax.all_gather(shared_down_weight, "fsdp", axis=1, tiled=True)
        own = (gate_all[:, :half], up_all[:, :half], down_all[:, :, :half], sg_all[:half], su_all[:half], sd_all[:, :half])

        def split(stack, shared):
            part = shared.shape[0] // 4
            return [
                jnp.concatenate(
                    [stack[2 * p:2 * p + 2].reshape(-1, stack.shape[2]), shared[p * part:(p + 1) * part]], axis=0
                )
                for p in range(4)
            ]

        gates_p = split(gate_all[:, half:], sg_all[half:])
        ups_p = split(up_all[:, half:], su_all[half:])
        downs_p = split(down_all[:, :, half:], sd_all[:, half:])

    out_pieces = lax.all_gather(output_weight, ("fsdp", "tp"), axis=0)
    out_pieces = out_pieces.reshape(fsdp_size, tp_size, head_cols, output_weight.shape[1])
    if not paired:
        out_pieces = jnp.transpose(out_pieces, (1, 2, 0, 3)).reshape(tp_size, head_cols, 2, half)
        out_pieces = jnp.transpose(out_pieces, (2, 0, 1, 3))

    positions = (ctx * rows + jnp.arange(rows, dtype=jnp.int32)).astype(F32)
    inverse = jnp.exp(jnp.arange(HD // 2, dtype=F32) * (-math.log(10000.0) / (HD // 2)))
    angles = positions[:, None] * inverse[None, :]
    cosine, sine = jnp.cos(angles), jnp.sin(angles)
    heads = head_cols // HD

    def table(value, rest):
        turned = jnp.tile(value, (1, 2 * heads))
        plain = jnp.full((rows, head_cols), rest, F32)
        return jnp.concatenate([turned, plain[:, :64], turned, plain], axis=1)

    cos_table, sin_table = table(cosine, 1.0), table(sine, 0.0)
    packed = cos_table.shape[1]

    n1, q, kv, w_qkv, small = call(
        qkv_kernel,
        (seqs,),
        [
            by_step((rows, width)),
            whole((half, packed)),
            whole((half, packed)),
            whole((rows, packed)),
            whole((rows, packed)),
        ],
        [
            by_step((rows, width)),
            by_step((rows, head_cols)),
            by_step((rows, 2 * head_cols)),
            whole((width, packed)),
            whole((16, width)),
        ],
        [
            shape_of((seqs, rows, width)),
            shape_of((seqs, rows, head_cols)),
            shape_of((seqs, rows, 2 * head_cols)),
            shape_of((width, packed)),
            shape_of((16, width), F32),
        ],
        [pltpu.VMEM((width, packed), BF16)],
        flops=4 * seqs * rows * width * packed,
        nbytes=8e6,
    )(scal, layer_input, columns_own, columns_other, cos_table, sin_table)

    kv_0 = kv
    kv_2 = over_ctx(kv_0, 2)
    kv_1 = over_ctx(kv_0, 1)
    kv_3 = over_ctx(kv_2, 1)
    kvs = (kv_0, kv_1, kv_2, kv_3)

    if paired:
        gate_2, up_2, down_2 = over_ctx(gate_0, 2), over_ctx(up_0, 2), over_ctx(down_0, 2)
        gates_p = (gate_0, over_ctx(gate_0, 1), gate_2, over_ctx(gate_2, 1))
        ups_p = (up_0, over_ctx(up_0, 1), up_2, over_ctx(up_2, 1))
        downs_p = (down_0, over_ctx(down_0, 1), down_2, over_ctx(down_2, 1))

    o, lse = call(
        attn_fwd_kernel,
        (seqs,),
        [by_step((rows, head_cols))] + [by_step((rows, 2 * head_cols))] * 4,
        [by_step((rows // 2, 2 * head_cols)), by_step((8, rows))],
        [shape_of((seqs, rows // 2, 2 * head_cols)), shape_of((seqs, 8, rows), F32)],
        prefetch=2,
        flops=4 * seqs * heads * rows * rows * ctx_size * 256,
        nbytes=4e6,
    )(scal, prefix, q, *kvs)

    o_all = lax.all_gather(o, "tp", axis=0)
    routes_t = jnp.pad(jnp.transpose(routes, (0, 2, 1)), ((0, 0), (0, 6), (0, 0)))
    n2, h2, gates, slots = call(
        post_kernel,
        (seqs,),
        [
            pl.BlockSpec((tp_size, 1, rows // 2, 2 * head_cols), lambda i, *_: (0, i, 0, 0)),
            whole((2, tp_size, head_cols, half)),
            by_step((rows, width)),
            whole((16, width)),
            by_step((8, rows)),
        ],
        [by_step((rows, width)), whole((rows, width)), by_step((8, rows)), by_step((8, rows))],
        [
            shape_of((seqs, rows, width)),
            shape_of((rows, width), F32),
            shape_of((seqs, 8, rows), F32),
            shape_of((seqs, 8, rows), jnp.int32),
        ],
        [pltpu.VMEM((width, width), BF16)],
        flops=2 * seqs * rows * width * width,
        nbytes=8e6,
    )(scal, o_all, out_pieces, layer_input, small, routes_t)

    part_rows = 3 * (width // 8)
    full = whole((seqs, rows, width))
    shared_down_rows = hidden // 4
    grads_shape = shape_of((4, experts + 1, part_rows, hidden))
    upper = pl.BlockSpec((half // 4, hidden), lambda *_: (8, 0))
    lower = pl.BlockSpec((shared_down_rows, half), lambda *_: (8, 0))
    row_out = pl.BlockSpec((1, rows, width), lambda i, *_: (jnp.minimum(i, seqs - 1), 0, 0))
    shared_grads = pl.BlockSpec((4, 1, part_rows, hidden), lambda *_: (0, experts, 0, 0))
    ys, dn_shared, keep, send = call(
        shared_kernel,
        (seqs + 1,),
        [full, full, whole((half, hidden)), whole((half, hidden)), whole((hidden, half))]
        + [upper] * 8
        + [lower] * 4,
        [row_out, row_out, shared_grads, shared_grads],
        [shape_of((seqs, rows, width)), shape_of((seqs, rows, width)), grads_shape, grads_shape],
        [pltpu.VMEM((width, hidden), BF16)] * 2
        + [pltpu.VMEM((hidden, width), BF16)]
        + [pltpu.VMEM((seqs * rows, hidden), BF16)] * 3,
        flops=18 * seqs * rows * width * hidden,
        nbytes=14e6,
    )(scal, n2, cotangent, *own[3:], *gates_p, *ups_p, *downs_p)

    def expert_of(i, scal):
        i = jnp.minimum(i, experts - 1)
        return 2 * ((i // 2) ^ scal[3]) + i % 2

    def own_spec(shape):
        return pl.BlockSpec((1,) + shape, lambda i, scal: (expert_of(i, scal), 0, 0))

    def piece_specs(shape):
        return [
            pl.BlockSpec(shape, lambda i, scal, p=p: (jnp.clip(i - 2 * p, 0, 1), 0)) for p in range(4)
        ]

    late = pl.BlockSpec((1, rows, width), lambda i, *_: (jnp.maximum(i - experts, 0), 0, 0))
    dn_rows = rows + 16
    expert_grads = pl.BlockSpec((4, 1, part_rows, hidden), lambda i, scal: (0, expert_of(i, scal), 0, 0))
    y, dn, keep, send = call(
        moe_kernel,
        (experts + seqs,),
        [full, full, whole((seqs, 8, rows)), whole((seqs, 8, rows)), late, late]
        + [own_spec((half, hidden)), own_spec((half, hidden)), own_spec((hidden, half))]
        + piece_specs((half, hidden)) * 2
        + piece_specs((hidden, half))
        + [pl.BlockSpec(memory_space=pl.ANY)] * 2,
        [
            late,
            pl.BlockSpec((1, dn_rows, width), lambda i, *_: (jnp.maximum(i - experts, 0), 0, 0)),
            expert_grads,
            expert_grads,
        ],
        [shape_of((seqs, rows, width)), shape_of((seqs, dn_rows, width)), grads_shape, grads_shape],
        [pltpu.VMEM((width, hidden), BF16)] * 2
        + [pltpu.VMEM((hidden, width), BF16)]
        + [pltpu.VMEM((seqs, experts * SLOTS, rows), BF16)]
        + [pltpu.VMEM((seqs, experts * SLOTS, width), BF16)] * 2
        + [pltpu.VMEM((seqs * SLOTS, width), BF16)] * 3
        + [pltpu.VMEM((seqs * SLOTS, 128), F32), pltpu.VMEM((seqs, 8, rows), F32)],
        aliases={22: 2, 23: 3},
        flops=18 * seqs * experts * SLOTS * width * hidden,
        nbytes=50e6,
    )(scal, n2, cotangent, slots, gates, ys, dn_shared, *own[:3], *gates_p, *ups_p, *downs_p, keep, send)

    dn_own = lax.psum_scatter(dn, "tp", scatter_dimension=0, tiled=True)
    mine = pl.BlockSpec((1, rows, width), lambda i, scal: (scal[2], 0, 0))
    dh2, do, dh2_low, sums = call(
        mid_kernel,
        (1,),
        [
            whole((1, dn_rows, width)),
            pl.BlockSpec((1, 8, rows), lambda i, scal: (scal[2], 0, 0)),
            whole((rows, width)),
            mine,
            mine,
            whole((16, width)),
            whole((2, tp_size, head_cols, half)),
        ],
        [
            whole((rows, width)),
            whole((tp_size, rows // 2, 2 * head_cols)),
            whole((rows, width)),
            whole((16, width)),
        ],
        [
            shape_of((rows, width), F32),
            shape_of((tp_size, rows // 2, 2 * head_cols)),
            shape_of((rows, width)),
            shape_of((16, width), F32),
        ],
        [pltpu.VMEM((width, width), BF16)],
        flops=2 * rows * width * width,
        nbytes=5e6,
    )(scal, dn_own, gates, h2, n2, cotangent, small, out_pieces)
    do = lax.all_to_all(do, "tp", 0, 0, tiled=True)
    dh2_all = lax.all_gather(dh2_low, "tp", axis=0)

    y_own = lax.psum_scatter(y, "tp", scatter_dimension=0, tiled=True)
    activations = lax.all_gather((h2 + y_own[0].astype(F32)).astype(BF16), "tp", axis=0)

    part = width // blocks
    along_x, along_y = side, ctx // 2

    def pick(value, x, y, first, last):
        value = value.reshape((2, 2) + value.shape[1:])[:, :, first:last]
        if y is not None:
            value = lax.dynamic_index_in_dim(value, y, 1, False)
        if x is not None:
            value = lax.dynamic_index_in_dim(value, x, 0, False)
        return value.astype(F32)

    def scatter(keep, got, first, last, y_first):
        def both(x, y):
            return pick(keep, x, y, first, last) + pick(got, x, y, first, last)

        if y_first:
            far = over_ctx(both(None, 1 - along_y).astype(BF16), 2)
            away = both(1 - along_x, along_y) + lax.dynamic_index_in_dim(far, 1 - along_x, 0, False).astype(F32)
            here = both(along_x, along_y) + lax.dynamic_index_in_dim(far, along_x, 0, False).astype(F32)
            return here + over_x(away.astype(BF16)).astype(F32)
        far = over_x(both(1 - along_x, None).astype(BF16))
        away = both(along_x, 1 - along_y) + lax.dynamic_index_in_dim(far, 1 - along_y, 0, False).astype(F32)
        here = both(along_x, along_y) + lax.dynamic_index_in_dim(far, along_y, 0, False).astype(F32)
        return here + over_ctx(away.astype(BF16), 2).astype(F32)

    def scatter_plain(keep, send):
        both = jnp.stack([keep, send], axis=1)
        count, cols = both.shape[2], both.shape[4]
        both = jnp.transpose(both, (0, 1, 3, 2, 4)).reshape(blocks, part, count, cols)
        both = jnp.transpose(both, (0, 2, 1, 3)).reshape(blocks, count * part, cols)
        both = lax.psum_scatter(both, ("fsdp", "ctx"), scatter_dimension=0, tiled=True)
        return both.reshape(count, part, cols).astype(F32)

    if direct:
        got = over_ctx(send, 1)
        cut = experts // 2
        low_part = scatter(keep, got, 0, cut, True).reshape(cut, 3, part, hidden)
        high_part = scatter(keep, got, cut, experts + 1, False).reshape(experts + 1 - cut, 3, part, hidden)
        grads_exp = [jnp.concatenate([low_part[:, i], high_part[:-1, i]], axis=0) for i in range(3)]
        grads_shared = high_part[-1]
    else:
        shape = (4, (experts + 1) * 3, width // 8, hidden)
        grads = scatter_plain(keep.reshape(shape), send.reshape(shape)).reshape(experts + 1, 3, part, hidden)
        grads_exp = [grads[:experts, i] for i in range(3)]
        grads_shared = grads[experts]

    cos_t, sin_t = jnp.transpose(cosine), jnp.transpose(sine)
    kv_block = by_step((rows, 2 * head_cols))
    dq, e0, e1, e2, e3 = call(
        attn_bwd_kernel,
        (seqs,),
        [by_step((rows, head_cols))]
        + [kv_block] * 4
        + [by_step((8, rows)), by_step((rows // 2, 2 * head_cols)), whole((HD // 2, rows)), whole((HD // 2, rows))],
        [by_step((rows, head_cols))] + [kv_block] * 4,
        [shape_of((seqs, rows, head_cols))] + [shape_of((seqs, rows, 2 * head_cols))] * 4,
        prefetch=2,
        flops=10 * seqs * heads * rows * rows * ctx_size * 256,
        nbytes=10e6,
    )(scal, prefix, q, *kvs, lse, do, cos_t, sin_t)
    from_core_1 = over_ctx(e1, 1)
    from_core_3 = over_ctx(e3, 1)
    far = (e2.astype(F32) + from_core_3.astype(F32)).astype(BF16)
    from_y = over_ctx(far, 2)

    dn1, keep, send = call(
        last_kernel,
        (seqs,),
        [
            by_step((rows, head_cols)),
            kv_block,
            kv_block,
            kv_block,
            whole((seqs, rows, width)),
            whole((width, packed)),
            whole((rows, packed)),
            whole((rows, packed)),
            whole((seqs, rows, width)),
            by_step((rows // 2, 2 * head_cols)),
        ],
        [by_step((rows, width)), whole((4, width // 8, 896)), whole((4, width // 8, 896))],
        [shape_of((seqs, rows, width)), shape_of((4, width // 8, 896)), shape_of((4, width // 8, 896))],
        [pltpu.VMEM((seqs * rows, packed), BF16), pltpu.VMEM((seqs * rows, head_cols), BF16)],
        flops=4 * seqs * rows * width * packed + 2 * seqs * rows * width * head_cols,
        nbytes=12e6,
    )(scal, dq, e0, from_core_1, from_y, n1, w_qkv, cos_table, sin_table, dh2_all, o)
    dn1_own = lax.psum_scatter(dn1, "tp", scatter_dimension=0, tiled=True)
    keep, send = keep[:, None], send[:, None]
    if direct:
        grads_attn = scatter(keep, over_ctx(send, 1), 0, 1, True)[0]
    else:
        grads_attn = scatter_plain(keep, send)[0]

    gi, sums = call(
        end_kernel,
        (1,),
        [whole((1, rows, width)), whole((rows, width)), mine, whole((16, width)), whole((16, width))],
        [whole((rows, width)), whole((16, width))],
        [shape_of((rows, width)), shape_of((16, width), F32)],
        nbytes=3e6,
    )(scal, dn1_own, dh2, layer_input, small, sums)
    grad_input = lax.all_gather(gi, "tp", axis=0).astype(F32)
    if direct and tp_size == 4:
        sums = sums + over_ctx(sums, 1)
        sums = sums + over_ctx(sums, 2)
        sums = sums + over_x(sums)
        for bit in (1, 2):
            sums = sums + lax.ppermute(sums, "tp", [(i, i ^ bit) for i in range(tp_size)])
    else:
        sums = lax.psum(sums, ("fsdp", "ctx", "tp"))
    block = lax.axis_index("fsdp") * ctx_size + ctx
    sums = lax.dynamic_slice_in_dim(sums, block * part, part, 1)

    return (
        activations.reshape(layer_input.shape),
        grad_input.reshape(layer_input.shape),
        sums[8],
        grads_attn[:, :head_cols],
        grads_attn[:, 256:256 + head_cols],
        grads_attn[:, 256 + head_cols:256 + 2 * head_cols],
        jnp.transpose(grads_attn[:, packed:packed + head_cols]),
        sums[9],
        jnp.transpose(sums[0:8]),
        grads_exp[0],
        grads_exp[1],
        jnp.transpose(grads_exp[2], (0, 2, 1)),
        grads_shared[0],
        grads_shared[1],
        jnp.transpose(grads_shared[2]),
    )


def solution(mesh):
    placed = (
        P("fsdp", "ctx", None),
        P("fsdp"),
        P("fsdp", "tp"),
        P("fsdp", "tp"),
        P("fsdp", "tp"),
        P("tp", "fsdp"),
        P("fsdp"),
        P("fsdp", None),
        P(None, "fsdp", "tp"),
        P(None, "fsdp", "tp"),
        P(None, "tp", "fsdp"),
        P("fsdp", "tp"),
        P("fsdp", "tp"),
        P("tp", "fsdp"),
        P("fsdp", "ctx", None),
        P("fsdp"),
        P("fsdp", "ctx", None),
    )
    return jax.shard_map(
        functools.partial(body, mesh.shape["fsdp"]),
        mesh=mesh,
        in_specs=placed,
        out_specs=(
            P("fsdp", "ctx", None),
            P("fsdp", "ctx", None),
            P(("fsdp", "ctx")),
            P(("fsdp", "ctx"), "tp"),
            P(("fsdp", "ctx"), "tp"),
            P(("fsdp", "ctx"), "tp"),
            P("tp", ("fsdp", "ctx")),
            P(("fsdp", "ctx")),
            P(("fsdp", "ctx"), None),
            P(None, ("fsdp", "ctx"), "tp"),
            P(None, ("fsdp", "ctx"), "tp"),
            P(None, "tp", ("fsdp", "ctx")),
            P(("fsdp", "ctx"), "tp"),
            P(("fsdp", "ctx"), "tp"),
            P("tp", ("fsdp", "ctx")),
        ),
        check_vma=False,
    )
```

```python
import functools
import math

import jax
import jax.numpy as jnp
from jax import lax
from jax.experimental import pallas as pl
from jax.experimental.pallas import tpu as pltpu
from jax.sharding import PartitionSpec as P

HD = 64
SLOTS = 80
EPS = 1e-06
F32 = jnp.float32
BF16 = jnp.bfloat16
VMEM_BYTES = 56 * 1024 * 1024


def mm(a, b):
    return lax.dot_general(a, b, (((1,), (0,)), ((), ())), preferred_element_type=F32)


def mm_nt(a, b):
    return lax.dot_general(a, b, (((1,), (1,)), ((), ())), preferred_element_type=F32)


def mm_tn(a, b):
    return lax.dot_general(a, b, (((0,), (0,)), ((), ())), preferred_element_type=F32)


def params(steps=1):
    return pltpu.CompilerParams(
        dimension_semantics=("arbitrary",) * steps, vmem_limit_bytes=VMEM_BYTES
    )


def rotation(width):
    row = lax.broadcasted_iota(jnp.int32, (width, width), 0)
    col = lax.broadcasted_iota(jnp.int32, (width, width), 1)
    first = (col % HD) < HD // 2
    minus = first & (row == col + HD // 2)
    plus = jnp.logical_not(first) & (row == col - HD // 2)
    return jnp.where(minus, -1.0, jnp.where(plus, 1.0, 0.0)).astype(BF16)


def row_scale(value):
    return lax.rsqrt(jnp.mean(value * value, -1, keepdims=True) + EPS)


def qkv_kernel(scal, x_ref, own_ref, oth_ref, cos_ref, sin_ref, n1_ref, q_ref, kv_ref, all_ref, w_ref, small_ref, swap):
    half = own_ref.shape[0]

    @pl.when(pl.program_id(0) == 0)
    def _():
        mine = pl.multiple_of(scal[0] * half, half)
        other = pl.multiple_of((1 - scal[0]) * half, half)
        w_ref[pl.ds(mine, half), :] = own_ref[...]
        w_ref[pl.ds(other, half), :] = oth_ref[...]
        swap[...] = mm(w_ref[...], rotation(w_ref.shape[1])).astype(BF16)
        turned = jnp.transpose(w_ref[:, 128:256].astype(F32))
        small_ref[...] = turned[64:80, :]

    x = x_ref[0].astype(F32)
    n1 = (x * row_scale(x) * small_ref[8:9, :]).astype(BF16)
    n1_ref[0] = n1
    turned = (mm(n1, w_ref[...]) * cos_ref[...] + mm(n1, swap[...]) * sin_ref[...]).astype(BF16)
    q_ref[0] = turned[:, :192]
    kv_ref[0] = turned[:, 256:640]
    all_ref[0] = turned


def visible(scal, prefix, keys, rows):
    key_pos = lax.broadcasted_iota(jnp.int32, (keys, rows), 0) ^ (scal[1] * rows)
    row_pos = lax.broadcasted_iota(jnp.int32, (keys, rows), 1) + scal[1] * rows
    return (key_pos <= row_pos) | (key_pos < prefix)


def only_head(rows, head):
    lane = lax.broadcasted_iota(jnp.int32, rows.shape, 1)
    return jnp.where((lane >= head * HD) & (lane < (head + 1) * HD), rows, jnp.zeros_like(rows))


def softmax(scores, seen):
    scores = jnp.where(seen, scores, -1e30)
    expo = jnp.exp(scores - jnp.max(scores, 0, keepdims=True))
    return expo * (1.0 / jnp.sum(expo, 0, keepdims=True))


def attn_fwd_kernel(scal, prefix, q_ref, kv0, kv1, kv2, kv3, o_ref):
    q = q_ref[0]
    rows, width = q.shape
    heads = width // HD
    kv = jnp.concatenate([kv0[0], kv1[0], kv2[0], kv3[0]], axis=0)
    k = kv[:, :width]
    value_t = jnp.transpose(kv[:, width:].astype(F32)).astype(BF16)
    seen = visible(scal, prefix[pl.program_id(0)], kv.shape[0], rows)
    outs = []
    for head in range(heads):
        probs = softmax(mm_nt(k, only_head(q, head) * (HD ** -0.5)), seen).astype(BF16)
        outs.append(mm(value_t[head * HD:(head + 1) * HD], probs))
    o = jnp.transpose(jnp.concatenate(outs, axis=0))
    o_ref[0] = jnp.concatenate([o[: rows // 2], o[rows // 2:]], axis=1).astype(BF16)


def fill_out_weights(scal, wo, wo_ref):
    pieces, _, width, half = wo_ref.shape
    for piece in range(pieces):
        for index, side in enumerate((scal[0], 1 - scal[0])):
            at = pl.ds(pl.multiple_of(side * half, half), half)
            wo[piece * width:(piece + 1) * width, at] = wo_ref[piece, index]


def post_kernel(scal, o_ref, wo_ref, x_ref, small_ref, routes_ref, n2_ref, h2_ref, gates_ref, slots_ref, wo):
    step = pl.program_id(0)
    width = wo_ref.shape[2]

    @pl.when(step == 0)
    def _():
        fill_out_weights(scal, wo, wo_ref)

    low = jnp.zeros((o_ref.shape[2], wo.shape[1]), F32)
    high = low
    for piece in range(o_ref.shape[0]):
        block = o_ref[piece, 0]
        weights = wo[piece * width:(piece + 1) * width, :]
        low += mm(block[:, :width], weights)
        high += mm(block[:, width:], weights)
    h2 = x_ref[0].astype(F32) + jnp.concatenate([low, high], axis=0)
    n2 = (h2 * row_scale(h2) * small_ref[9:10, :]).astype(BF16)
    n2_ref[0] = n2

    @pl.when(step == scal[2])
    def _():
        h2_ref[...] = h2

    expo = jnp.exp(mm_nt(small_ref[0:8, :].astype(BF16), n2))
    gates_ref[0] = expo / jnp.sum(expo, 0, keepdims=True)
    rows = n2.shape[0]
    expert = lax.broadcasted_iota(jnp.int32, (8, rows), 0)
    named = (routes_ref[0, 0:1, :] == expert) | (routes_ref[0, 1:2, :] == expert)
    before = lax.broadcasted_iota(jnp.int32, (rows, rows), 0) < lax.broadcasted_iota(jnp.int32, (rows, rows), 1)
    place = mm(named.astype(BF16), before.astype(BF16))
    slots_ref[0] = jnp.where(named, place.astype(jnp.int32), -1)


def silu_parts(value):
    sigma = 1.0 / (1.0 + jnp.exp(-value))
    return sigma, value * sigma


def split_blocks(core, value, blocks):
    rows = value.shape[0] // (2 * blocks)
    value = value.astype(BF16).reshape(blocks, 2, rows, value.shape[1])
    first = core == 0
    return jnp.where(first, value[:, 0], value[:, 1]), jnp.where(first, value[:, 1], value[:, 0])


def put_grads(core, keep_ref, send_ref, index, value):
    keep, send = split_blocks(core, value, keep_ref.shape[0])
    at = slice(index * keep.shape[1], (index + 1) * keep.shape[1])
    keep_ref[:, 0, at, :] = keep
    send_ref[:, 0, at, :] = send


def shared_kernel(
    scal, n2_ref, dy_ref, go_ref, uo_ref, do_ref, g0, g1, g2, g3, u0, u1, u2, u3, d0, d1, d2, d3,
    ys_ref, dn_ref, hid_ref, da_ref, db_ref, wg, wu, wd,
):
    step = pl.program_id(0)
    half = go_ref.shape[0]
    hidden = go_ref.shape[1]

    @pl.when(step == 0)
    def _():
        mine = pl.multiple_of(scal[0] * half, half)
        other = (1 - scal[0]) * half
        wg[pl.ds(mine, half), :] = go_ref[...]
        wu[pl.ds(mine, half), :] = uo_ref[...]
        wd[:, pl.ds(mine, half)] = do_ref[...]
        for piece, (g, u, d) in enumerate(((g0, u0, d0), (g1, u1, d1), (g2, u2, d2), (g3, u3, d3))):
            quarter = scal[3] ^ piece
            at = pl.multiple_of(other + quarter * (half // 4), half // 4)
            wg[pl.ds(at, half // 4), :] = g[...]
            wu[pl.ds(at, half // 4), :] = u[...]
            at = pl.multiple_of(quarter * (hidden // 4), hidden // 4)
            wd[pl.ds(at, hidden // 4), pl.ds(pl.multiple_of(other, half), half)] = d[...]

    n2 = n2_ref[0]
    dy = dy_ref[0]
    gate = mm(n2, wg[...])
    up = mm(n2, wu[...])
    sigma, silu = silu_parts(gate)
    hid = (silu * up).astype(BF16)
    ys_ref[0] = mm(hid, wd[...]).astype(BF16)
    back = mm_nt(dy, wd[...])
    da = (back * up * (sigma * (1.0 + gate * (1.0 - sigma)))).astype(BF16)
    db = (back * silu).astype(BF16)
    dn_ref[0] = (mm_nt(da, wg[...]) + mm_nt(db, wu[...])).astype(BF16)
    hid_ref[0] = hid
    da_ref[0] = da
    db_ref[0] = db


def shared_grads_kernel(scal, n2_ref, dy_ref, hid_ref, da_ref, db_ref, keep_ref, send_ref):
    n2, dy, hid, da, db = [
        ref[...].reshape(-1, ref.shape[-1]) for ref in (n2_ref, dy_ref, hid_ref, da_ref, db_ref)
    ]
    put_grads(scal[4], keep_ref, send_ref, 0, mm_tn(n2, da))
    put_grads(scal[4], keep_ref, send_ref, 1, mm_tn(n2, db))
    put_grads(scal[4], keep_ref, send_ref, 2, mm_tn(dy, hid))


def moe_kernel(
    scal, n2_ref, dy_ref, slots_ref, gates_ref, ys_ref, dn_in_ref, go_ref, uo_ref, do_ref,
    g0, g1, g2, g3, u0, u1, u2, u3, v0, v1, v2, v3, d0, d1, d2, d3,
    y_ref, dn_ref, keep_ref, send_ref, wg, wu, wd, pick_s, ye_s, dx_s, xe_s, dy_s, de_s, gs_s, dprob_s,
):
    step = pl.program_id(0)
    seqs, rows, width = n2_ref.shape
    half = go_ref.shape[1]
    experts = slots_ref.shape[1]

    @pl.when(step < experts)
    def _():
        piece = step // 2
        expert = 2 * (piece ^ scal[3]) + step % 2
        mine = pl.multiple_of(scal[0] * half, half)
        other = pl.multiple_of((1 - scal[0]) * half, half)
        wg[pl.ds(mine, half), :] = go_ref[0]
        wu[pl.ds(mine, half), :] = uo_ref[0]
        wd[:, pl.ds(mine, half)] = do_ref[0]
        arrived = ((g0, u0, v0, d0), (g1, u1, v1, d1), (g2, u2, v2, d2), (g3, u3, v3, d3))
        for index, (g, u, v, d) in enumerate(arrived):
            @pl.when(piece == index)
            def _(g=g, d=d):
                wg[pl.ds(other, half), :] = g[...]
                wd[:, pl.ds(other, half)] = d[...]

            for odd, ref in enumerate((u, v)):
                @pl.when((piece == index) & (step % 2 == odd))
                def _(ref=ref):
                    wu[pl.ds(other, half), :] = ref[...]

        slot_at = pl.ds(pl.multiple_of(step * SLOTS, 16), SLOTS)
        slot = lax.broadcasted_iota(jnp.int32, (SLOTS, rows), 0)
        for s in range(seqs):
            at = slice(s * SLOTS, (s + 1) * SLOTS)
            hit = slots_ref[s, pl.ds(expert, 1), :] == slot
            gate_slot = jnp.sum(jnp.where(hit, gates_ref[s, pl.ds(expert, 1), :], 0.0), 1, keepdims=True)
            pick = hit.astype(BF16)
            pick_s[s, slot_at, :] = pick
            xe_s[at, :] = mm(pick, n2_ref[s]).astype(BF16)
            upstream = mm(pick, dy_ref[s])
            dy_s[at, :] = upstream.astype(BF16)
            de_s[at, :] = (gate_slot * upstream).astype(BF16)
            gs_s[at, :] = jnp.broadcast_to(gate_slot, (SLOTS, 128))

        xe = xe_s[...]
        gate = mm(xe, wg[...])
        up = mm(xe, wu[...])
        sigma, silu = silu_parts(gate)
        hid = (silu * up).astype(BF16)
        ye = mm(hid, wd[...])
        dots = jnp.sum(ye * dy_s[...].astype(F32), 1, keepdims=True)
        ye = (ye * gs_s[:, 0:1]).astype(BF16)
        for s in range(seqs):
            at = slice(s * SLOTS, (s + 1) * SLOTS)
            ye_s[s, slot_at, :] = ye[at]
            hit = slots_ref[s, pl.ds(expert, 1), :] == slot
            dprob_s[s, pl.ds(expert, 1), :] = jnp.sum(jnp.where(hit, dots[at], 0.0), 0, keepdims=True)
        back = mm_nt(de_s[...], wd[...])
        da = (back * up * (sigma * (1.0 + gate * (1.0 - sigma)))).astype(BF16)
        db = (back * silu).astype(BF16)
        dx = (mm_nt(da, wg[...]) + mm_nt(db, wu[...])).astype(BF16)
        for s in range(seqs):
            dx_s[s, slot_at, :] = dx[s * SLOTS:(s + 1) * SLOTS]
        put_grads(scal[4], keep_ref, send_ref, 0, mm_tn(xe_s[...], da))
        put_grads(scal[4], keep_ref, send_ref, 1, mm_tn(xe_s[...], db))
        put_grads(scal[4], keep_ref, send_ref, 2, mm_tn(de_s[...], hid))

    @pl.when(step >= experts)
    def _():
        s = step - experts
        pick = pick_s[s]
        y_ref[0] = (ys_ref[0].astype(F32) + mm_tn(pick, ye_s[s])).astype(BF16)
        dn_ref[0, 0:rows, :] = (dn_in_ref[0].astype(F32) + mm_tn(pick, dx_s[s])).astype(BF16)
        tail = jnp.concatenate([dprob_s[s], jnp.zeros((dn_ref.shape[1] - rows - experts, rows), F32)], axis=0)
        tail = jnp.concatenate([tail, jnp.zeros((tail.shape[0], width - rows), F32)], axis=1)
        dn_ref[0, rows:, :] = tail.astype(BF16)


def norm_back(grad_out, value, scale, gain):
    weighted = grad_out * gain
    return scale * weighted - value * (scale * scale * scale) * jnp.mean(weighted * value, -1, keepdims=True)


def mid_kernel(scal, dn_ref, gates_ref, h2_ref, n2_ref, dy_ref, small_ref, wo_ref, dh2_ref, do_ref, low_ref, sums_ref, wo):
    rows = h2_ref.shape[0]
    pieces, _, width, _ = wo_ref.shape
    fill_out_weights(scal, wo, wo_ref)
    parts = dn_ref[0].astype(F32)
    gates = gates_ref[0]
    dprob = parts[rows:rows + 8, 0:rows]
    dlogits = (gates * (dprob - jnp.sum(dprob * gates, 0, keepdims=True))).astype(BF16)
    dn2 = parts[0:rows, :] + mm_tn(dlogits, small_ref[0:8, :].astype(BF16))
    h2 = h2_ref[...]
    scale = row_scale(h2)
    sums_ref[0:8, :] = mm(dlogits, n2_ref[0])
    sums_ref[8:16, :] = jnp.zeros((8, h2.shape[1]), F32)
    sums_ref[9:10, :] = jnp.sum(dn2 * h2 * scale, 0, keepdims=True)
    dh2 = dy_ref[0].astype(F32) + norm_back(dn2, h2, scale, small_ref[9:10, :])
    dh2_ref[...] = dh2
    low = dh2.astype(BF16)
    low_ref[...] = low
    for piece in range(pieces):
        do = mm_nt(low, wo[piece * width:(piece + 1) * width, :])
        do_ref[piece] = jnp.concatenate([do[: rows // 2], do[rows // 2:]], axis=1).astype(BF16)


def attn_bwd_kernel(
    scal, prefix, q_ref, kv0, kv1, kv2, kv3, do_ref, cos_ref, sin_ref, dq_ref, e0, e1, e2, e3
):
    rows, width = dq_ref.shape[1:]
    q = q_ref[0][:, :width]
    heads = width // HD
    kv = jnp.concatenate([kv0[0], kv1[0], kv2[0], kv3[0]], axis=0)
    k = kv[:, :width]
    v = kv[:, width:]
    key_t = jnp.transpose(k.astype(F32)).astype(BF16)
    do = jnp.concatenate([do_ref[0][:, :width], do_ref[0][:, width:]], axis=0)
    seen = visible(scal, prefix[scal[2]], kv.shape[0], rows)
    cosine, sine = cos_ref[...], sin_ref[...]
    turned, ds_all, probs_all, q_all, do_all = [], [], [], [], []
    for head in range(heads):
        q_head = only_head(q, head) * (HD ** -0.5)
        do_head = only_head(do, head)
        probs = softmax(mm_nt(k, q_head), seen)
        dp = mm_nt(v, do_head)
        ds = (probs * (dp - jnp.sum(dp * probs, 0, keepdims=True))).astype(BF16)
        dq = mm(key_t[head * HD:(head + 1) * HD], ds) * (HD ** -0.5)
        first, second = dq[: HD // 2], dq[HD // 2:]
        turned += [first * cosine + second * sine, second * cosine - first * sine]
        ds_all.append(ds)
        probs_all.append(probs.astype(BF16))
        q_all.append(q_head)
        do_all.append(do_head)
    dq_ref[0] = jnp.transpose(jnp.concatenate(turned, axis=0)).astype(BF16)
    dk = mm(jnp.concatenate(ds_all, axis=1), jnp.concatenate(q_all, axis=0))
    dv = mm(jnp.concatenate(probs_all, axis=1), jnp.concatenate(do_all, axis=0))
    dkv = jnp.concatenate([dk, dv], axis=1).astype(BF16)
    for piece, out in enumerate((e0, e1, e2, e3)):
        out[0] = dkv[piece * rows:(piece + 1) * rows]


def swing_kernel(a_ref, b_ref, c_ref, cos_ref, sin_ref, out_ref):
    dkv = a_ref[0].astype(F32) + b_ref[0].astype(F32) + c_ref[0].astype(F32)
    swung = dkv * sin_ref[:, 256:]
    high = swung.astype(BF16)
    low = (swung - high.astype(F32)).astype(BF16)
    turn = rotation(dkv.shape[1])
    out_ref[0] = (dkv * cos_ref[:, 256:] + mm_nt(high, turn) + mm_nt(low, turn)).astype(BF16)


def end_kernel(scal, dq_ref, dkv_ref, w0, w1, w2, w3, dh2_ref, x_ref, small_ref, sums_in, gi_ref, sums_ref, w, total):
    step = pl.program_id(0)
    quarter = w0.shape[1]
    head_cols = dq_ref.shape[2]
    for piece, ref in enumerate((w0, w1, w2, w3)):
        at = pl.multiple_of((scal[1] ^ piece) * quarter, quarter)
        w[pl.ds(at, quarter), :] = ref[0]
    part = mm_nt(dq_ref[0], w[:, :head_cols]) + mm_nt(dkv_ref[0], w[:, 256:])

    @pl.when(step == 0)
    def _():
        total[...] = part

    @pl.when(step > 0)
    def _():
        total[...] += part

    @pl.when(step == pl.num_programs(0) - 1)
    def _():
        x = x_ref[0].astype(F32)
        dn1 = total[...]
        scale = row_scale(x)
        sums_ref[...] = sums_in[...]
        sums_ref[8:9, :] = jnp.sum(dn1 * x * scale, 0, keepdims=True)
        gi_ref[...] = (dh2_ref[...] + norm_back(dn1, x, scale, small_ref[8:9, :])).astype(BF16)


def first_grads_kernel(scal, n1_ref, dq_ref, low_ref, o_ref, keep_ref, send_ref):
    head_cols = dq_ref.shape[2]
    block = o_ref[0, 0]
    o = jnp.concatenate([block[:, :head_cols], block[:, head_cols:]], axis=0)
    grads = jnp.concatenate([mm_tn(n1_ref[0], dq_ref[0]), mm_tn(low_ref[...], o)], axis=1)
    keep_ref[:, 0], send_ref[:, 0] = split_blocks(scal[4], grads, keep_ref.shape[0])


def second_grads_kernel(scal, n1_ref, dkv_ref, sums_ref, keep_ref, send_ref):
    step = pl.program_id(0)
    last = pl.num_programs(0) - 1

    @pl.when(step < last)
    def _():
        keep_ref[:, 0], send_ref[:, 0] = split_blocks(scal[4], mm_tn(n1_ref[0], dkv_ref[0]), keep_ref.shape[0])

    @pl.when(step == last)
    def _():
        sums = sums_ref[...]
        sums = jnp.concatenate([sums, jnp.zeros((keep_ref.shape[3] - sums.shape[0], sums.shape[1]), F32)], axis=0)
        keep_ref[:, 0], send_ref[:, 0] = split_blocks(scal[4], jnp.transpose(sums), keep_ref.shape[0])


def whole(shape):
    return pl.BlockSpec(shape, lambda *_: (0,) * len(shape))


def by_step(shape):
    return pl.BlockSpec((1,) + shape, lambda i, *_: (i,) + (0,) * len(shape))


def call(kernel, grid, in_specs, out_specs, out_shape, scratch=(), prefetch=1, aliases=None):
    return pl.pallas_call(
        kernel,
        grid_spec=pltpu.PrefetchScalarGridSpec(
            num_scalar_prefetch=prefetch,
            grid=grid,
            in_specs=in_specs,
            out_specs=out_specs,
            scratch_shapes=scratch,
        ),
        out_shape=out_shape,
        input_output_aliases=aliases or {},
        compiler_params=params(len(grid)),
        cost_estimate=pl.CostEstimate(flops=1, bytes_accessed=1, transcendentals=0),
    )


def fence(values, *others):
    values = list(values)
    return list(lax.optimization_barrier((*values, *others))[: len(values)])


def shape_of(shape, dtype=BF16):
    return jax.ShapeDtypeStruct(shape, dtype)


def body(
    fsdp_size,
    layer_input,
    gain_attn,
    query_weight,
    key_weight,
    value_weight,
    output_weight,
    gain_ffn,
    router,
    exp_gate,
    exp_up,
    exp_down,
    shared_gate_weight,
    shared_up_weight,
    shared_down_weight,
    routes,
    prefix,
    cotangent,
):
    seqs, rows, width = layer_input.shape
    experts = exp_gate.shape[0]
    hidden = exp_gate.shape[2]
    head_cols = query_weight.shape[1]
    half = width // 2
    paired = fsdp_size == 2
    ctx = lax.axis_index("ctx")
    tp = lax.axis_index("tp")
    ctx_size = lax.axis_size("ctx")
    tp_size = lax.axis_size("tp")
    side = lax.axis_index("fsdp") if paired else jnp.int32(0)
    weight_ctx = ctx if paired else jnp.int32(0)
    blocks = fsdp_size * ctx_size
    direct = paired and ctx_size == 4 and tp_size == 4
    core = ctx % 2 if direct else jnp.int32(0)
    scal = jnp.stack([side, ctx, tp, weight_ctx, core]).astype(jnp.int32)

    def over_x(value):
        return lax.ppermute(value, "fsdp", [(0, 1), (1, 0)])

    def over_tp(value, bit):
        return lax.ppermute(value, "tp", [(i, i ^ bit) for i in range(tp_size)])

    def over_ctx(value, bit):
        return lax.ppermute(value, "ctx", [(i, i ^ bit) for i in range(ctx_size)])

    columns = jnp.concatenate(
        [
            query_weight,
            router,
            gain_attn[:, None],
            gain_ffn[:, None],
            jnp.zeros((query_weight.shape[0], 54), BF16),
            key_weight,
            value_weight,
        ],
        axis=1,
    )
    if paired:
        columns_own, columns_other = columns, over_x(columns)
    else:
        columns = lax.all_gather(columns, "fsdp", axis=0, tiled=True)
        columns_own, columns_other = columns[:half], columns[half:]

    shared_own = (shared_gate_weight, shared_up_weight, shared_down_weight)
    experts_own = (exp_gate, exp_up, exp_down)
    if paired:

        def quarter(value, parts):
            size = value.shape[0] // parts
            return lax.dynamic_slice_in_dim(value, size * ctx, size, 0).reshape(-1, value.shape[-1])

        gate, up, down = [quarter(stack, 4) for stack in experts_own]
        shared_gate, shared_up, shared_down = [quarter(stack, 4) for stack in shared_own]
        wide = jnp.concatenate([gate, up[:half], shared_gate, shared_up], axis=0)
        rest = up[half:]
        down = jnp.concatenate([down, shared_down], axis=0)
        own = experts_own + shared_own
    else:
        gate_all = lax.all_gather(exp_gate, "fsdp", axis=1, tiled=True)
        up_all = lax.all_gather(exp_up, "fsdp", axis=1, tiled=True)
        down_all = lax.all_gather(exp_down, "fsdp", axis=2, tiled=True)
        sg_all = lax.all_gather(shared_gate_weight, "fsdp", axis=0, tiled=True)
        su_all = lax.all_gather(shared_up_weight, "fsdp", axis=0, tiled=True)
        sd_all = lax.all_gather(shared_down_weight, "fsdp", axis=1, tiled=True)
        own = (gate_all[:, :half], up_all[:, :half], down_all[:, :, :half], sg_all[:half], su_all[:half], sd_all[:, :half])

        def split(value):
            return value.reshape((4, value.shape[0] // 4) + value.shape[1:])

        gate_all, up_all, sg_all, su_all = [
            split(value) for value in (gate_all[:, half:], up_all[:, half:], sg_all[half:], su_all[half:])
        ]
        down_all, sd_all = split(down_all[:, :, half:]), split(sd_all[:, half:])
        wide_p = [
            jnp.concatenate([gate_all[p, 0], gate_all[p, 1], up_all[p, 0], sg_all[p], su_all[p]], axis=0) for p in range(4)
        ]
        rest_p = [up_all[p, 1] for p in range(4)]
        down_p = [jnp.concatenate([down_all[p, 0], down_all[p, 1], sd_all[p]], axis=0) for p in range(4)]

    if paired:
        out_pieces = [output_weight, over_x(fence([output_weight], columns)[0])]
    else:
        out_pieces = lax.all_gather(output_weight, "fsdp", axis=1, tiled=True)
        out_pieces = [out_pieces[:, :half], out_pieces[:, half:]]

    positions = (ctx * rows + jnp.arange(rows, dtype=jnp.int32)).astype(F32)
    inverse = jnp.exp(jnp.arange(HD // 2, dtype=F32) * (-math.log(10000.0) / (HD // 2)))
    angles = positions[:, None] * inverse[None, :]
    cosine, sine = jnp.cos(angles), jnp.sin(angles)
    heads = head_cols // HD

    def table(value, rest):
        turned = jnp.tile(value, (1, 2 * heads))
        plain = jnp.full((rows, head_cols), rest, F32)
        return jnp.concatenate([turned, plain[:, :64], turned, plain], axis=1)

    cos_table, sin_table = table(cosine, 1.0), table(sine, 0.0)
    routes_t = jnp.pad(jnp.transpose(routes, (0, 2, 1)), ((0, 0), (0, 6), (0, 0)))

    columns_other, cos_table, sin_table = fence([columns_other, cos_table, sin_table], routes_t)
    if paired:
        out_own, out_other = out_pieces
        columns_other, out_other, cos_table, wide, rest, down = fence(
            [columns_other, out_other, cos_table, wide, rest, down]
        )
        out_pieces = [out_own, out_other]
        wide_0 = over_x(wide)
    out_pieces = lax.all_gather(jnp.stack(out_pieces), "tp", axis=0)
    packed = cos_table.shape[1]

    n1, q, kv, qkv, w_qkv, small = call(
        qkv_kernel,
        (seqs,),
        [
            by_step((rows, width)),
            whole((half, packed)),
            whole((half, packed)),
            whole((rows, packed)),
            whole((rows, packed)),
        ],
        [
            by_step((rows, width)),
            by_step((rows, head_cols)),
            by_step((rows, 2 * head_cols)),
            by_step((rows, packed)),
            whole((width, packed)),
            whole((16, width)),
        ],
        [
            shape_of((seqs, rows, width)),
            shape_of((seqs, rows, head_cols)),
            shape_of((seqs, rows, 2 * head_cols)),
            shape_of((seqs, rows, packed)),
            shape_of((width, packed)),
            shape_of((16, width), F32),
        ],
        [pltpu.VMEM((width, packed), BF16)],
    )(scal, layer_input, columns_own, columns_other, cos_table, sin_table)

    kv_0 = kv
    kv_2 = over_ctx(kv_0, 2)
    kv_1 = over_ctx(kv_0, 1)
    q_now, kv_2 = fence([q, kv_2], kv_1)
    w_part = lax.dynamic_slice_in_dim(w_qkv, (width // 4) * ctx, width // 4, 0)
    w_part = jnp.pad(w_part, ((0, 16), (0, 0)))
    if paired:
        kv_2, wide_0, rest, down, w_part = fence([kv_2, wide_0, rest, down, w_part])
        wide_2 = over_ctx(wide_0, 2)
        down_0, rest_0 = over_x(down), over_x(rest)
    kv_3 = over_ctx(kv_2, 1)
    q_now, kv_3, out_pieces = fence([q_now, kv_3, out_pieces])

    o = call(
        attn_fwd_kernel,
        (seqs,),
        [by_step((rows, head_cols))] + [by_step((rows, 2 * head_cols))] * 4,
        by_step((rows // 2, 2 * head_cols)),
        shape_of((seqs, rows // 2, 2 * head_cols)),
        prefetch=2,
    )(scal, prefix, q_now, kv_0, kv_1, kv_2, kv_3)

    o_all = lax.all_gather(o, "tp", axis=0)
    if paired:
        wide_0, rest_0, down_0, wide_2 = fence([wide_0, rest_0, down_0, wide_2], o)
        down_2, rest_2, wide_1, wide_3 = over_ctx(down_0, 2), over_ctx(rest_0, 2), over_ctx(wide_0, 1), over_ctx(wide_2, 1)
        o_all, wide_1, wide_3 = fence([o_all, wide_1, wide_3])
        down_1, rest_1 = over_ctx(down_0, 1), over_ctx(rest_0, 1)
    w_0 = lax.all_gather(fence([w_part], o_all)[0], "tp", axis=0)
    n2, h2, gates, slots = call(
        post_kernel,
        (seqs,),
        [
            pl.BlockSpec((tp_size, 1, rows // 2, 2 * head_cols), lambda i, *_: (0, i, 0, 0)),
            whole((tp_size, 2, head_cols, half)),
            by_step((rows, width)),
            whole((16, width)),
            by_step((8, rows)),
        ],
        [by_step((rows, width)), whole((rows, width)), by_step((8, rows)), by_step((8, rows))],
        [
            shape_of((seqs, rows, width)),
            shape_of((rows, width), F32),
            shape_of((seqs, 8, rows), F32),
            shape_of((seqs, 8, rows), jnp.int32),
        ],
        [pltpu.VMEM((width, width), BF16)],
    )(scal, o_all, out_pieces, layer_input, small, routes_t)

    if paired:
        down_2, rest_2, n2 = fence([down_2, rest_2, n2])
        down_3, rest_3 = over_ctx(down_2, 1), over_ctx(rest_2, 1)
        wide_p = (wide_0, wide_1, wide_2, wide_3)
        rest_p = (rest_0, rest_1, rest_2, rest_3)
        down_p = (down_0, down_1, down_2, down_3)

    full = pl.BlockSpec((seqs, rows, width), lambda *_: (0, 0, 0), pipeline_mode=pl.Buffered(1))
    part_rows = 3 * (width // 8)
    upper = [pl.BlockSpec((half // 4, hidden), lambda *_, at=at: (at, 0)) for at in (12, 13)]
    lower = pl.BlockSpec((hidden // 4, half), lambda *_: (8, 0))
    weights = [pltpu.VMEM((width, hidden), BF16)] * 2 + [pltpu.VMEM((hidden, width), BF16)]
    hidden_shape = shape_of((seqs, rows, hidden))
    ys, dn_shared, *shared_hidden = call(
        shared_kernel,
        (seqs,),
        [by_step((rows, width))] * 2
        + [whole((half, hidden)), whole((half, hidden)), whole((hidden, half))]
        + [upper[0]] * 4
        + [upper[1]] * 4
        + [lower] * 4,
        [by_step((rows, width))] * 2 + [by_step((rows, hidden))] * 3,
        [shape_of((seqs, rows, width))] * 2 + [hidden_shape] * 3,
        weights,
    )(scal, n2, cotangent, *own[3:], *wide_p, *wide_p, *down_p)

    qkv_late, w_0, ys = fence([qkv, w_0, ys])
    qkv_seq = lax.all_to_all(qkv_late, "tp", 0, 0, tiled=True)
    w_2, w_1 = over_ctx(w_0, 2), over_ctx(w_0, 1)

    def expert_of(i, scal):
        i = jnp.minimum(i, experts - 1)
        return 2 * ((i // 2) ^ scal[3]) + i % 2

    def of_expert(shape):
        return pl.BlockSpec((1,) + shape, lambda i, scal: (expert_of(i, scal), 0, 0))

    def piece_specs(shape):
        return [
            pl.BlockSpec(shape, lambda i, scal, p=p: (jnp.clip(i - 2 * p, 0, 1), 0)) for p in range(4)
        ]

    late = pl.BlockSpec((1, rows, width), lambda i, scal: (jnp.maximum(i - experts, 0), 0, 0))

    dn_rows = rows + 16
    slot_rows = seqs * SLOTS
    block = (4, 1, part_rows, hidden)

    expert_grads = pl.BlockSpec(block, lambda i, scal: (0, expert_of(i, scal), 0, 0))
    y, dn, *expert_group = call(
        moe_kernel,
        (experts + seqs,),
        [full, full, whole((seqs, 8, rows)), whole((seqs, 8, rows)), late, late]
        + [of_expert((half, hidden)), of_expert((half, hidden)), of_expert((hidden, half))]
        + piece_specs((half, hidden))
        + [pl.BlockSpec((half, hidden), lambda *_: (2, 0))] * 4
        + [pl.BlockSpec((half, hidden), lambda *_: (0, 0))] * 4
        + piece_specs((hidden, half)),
        [late, pl.BlockSpec((1, dn_rows, width), lambda i, *_: (jnp.maximum(i - experts, 0), 0, 0))]
        + [expert_grads] * 2,
        [shape_of((seqs, rows, width)), shape_of((seqs, dn_rows, width))]
        + [shape_of((4, experts, part_rows, hidden))] * 2,
        weights
        + [pltpu.VMEM((seqs, experts * SLOTS, rows), BF16)]
        + [pltpu.VMEM((seqs, experts * SLOTS, width), BF16)] * 2
        + [pltpu.VMEM((slot_rows, width), BF16)] * 3
        + [pltpu.VMEM((slot_rows, 128), F32), pltpu.VMEM((seqs, 8, rows), F32)],
    )(scal, n2, cotangent, slots, gates, ys, dn_shared, *own[:3], *wide_p, *wide_p, *rest_p, *down_p)

    dn, qkv_seq, w_2, w_1, n2_late, *expert_group = fence([dn, qkv_seq, w_2, w_1, n2, *expert_group])
    w_pieces = (w_0, w_1, w_2, over_ctx(w_2, 1))
    dn_own = lax.psum_scatter(dn, "tp", scatter_dimension=0, tiled=True)
    kv_seq = qkv_seq[:, :, 256:]
    kv_seq_2, kv_seq_1 = over_ctx(kv_seq, 2), over_ctx(kv_seq, 1)

    shared_group = call(
        shared_grads_kernel,
        (1,),
        [full] * 2 + [whole((seqs, rows, hidden))] * 3,
        [whole(block)] * 2,
        [shape_of(block)] * 2,
    )(scal, n2_late, cotangent, *shared_hidden)

    part = width // blocks
    along_x, along_y = side, ctx // 2

    def pick(value, x, y, first, count):
        value = value.reshape((2, 2) + value.shape[1:])
        sizes = (2 if x is None else 1, 2 if y is None else 1, count) + value.shape[3:]
        begin = (0 if x is None else x, 0 if y is None else y, first, 0, 0)
        value = lax.dynamic_slice(value, begin, sizes)
        value = value.reshape(tuple(n for n, at in zip(sizes[:2], (x, y)) if at is None) + sizes[2:])
        return value.astype(F32)

    def indexed(value, index):
        return lax.dynamic_index_in_dim(value, index, 0, False).astype(F32)

    class Sum:
        def __init__(self, keep, got, y_first, first=0, count=None):
            self.keep, self.got, self.y_first = keep, got, y_first
            self.range = (first, count or keep.shape[1])

        def fence(self, *others):
            (self.got,) = fence([self.got], *others)

        def both(self, x, y):
            return pick(self.keep, x, y, *self.range) + pick(self.got, x, y, *self.range)

        def first(self):
            if self.y_first:
                self.sent = self.both(None, 1 - along_y).astype(BF16)
            else:
                self.sent = self.both(1 - along_x, None).astype(BF16)
            self.far = over_ctx(self.sent, 2) if self.y_first else over_x(self.sent)
            return self.sent

        def second(self):
            if self.y_first:
                self.away = (self.both(1 - along_x, along_y) + indexed(self.far, 1 - along_x)).astype(BF16)
                self.last = over_x(self.away)
            else:
                self.away = (self.both(along_x, 1 - along_y) + indexed(self.far, 1 - along_y)).astype(BF16)
                self.last = over_ctx(self.away, 2)
            return self.away

        def result(self):
            mine = indexed(self.far, along_x if self.y_first else along_y)
            return self.both(along_x, along_y) + mine + self.last.astype(F32)

    def scatter_plain(keep, send):
        count, cols = keep.shape[1], keep.shape[3]
        triples = keep.shape[2] // (width // 8)
        both = jnp.stack([keep, send], axis=1).reshape(8, count, triples, width // 8, cols)
        both = jnp.transpose(both, (0, 3, 1, 2, 4)).reshape(blocks, part, count * triples, cols)
        both = jnp.transpose(both, (0, 2, 1, 3)).reshape(blocks, count * triples * part, cols)
        both = lax.psum_scatter(both, ("fsdp", "ctx"), scatter_dimension=0, tiled=True)
        return both.reshape(count, triples * part, cols).astype(F32)

    if direct:
        got, shared_got = over_ctx(expert_group[1], 1), over_ctx(shared_group[1], 1)
        cuts = ((0, 2, True), (2, 2, False), (4, 4, False))
        sums_of = [Sum(expert_group[0], got, y_first, first, count) for first, count, y_first in cuts]
        sums_of.append(Sum(shared_group[0], shared_got, True))
        sent = [sums_of[1].first(), sums_of[0].first()]
        sums_of[2].fence(*sent)
        sent.append(sums_of[2].first())
        sums_of[3].fence(*sent)
        sent.append(sums_of[3].first())
        (kv_seq_2,) = fence([kv_seq_2], *sent)
    kv_seq_3 = over_ctx(kv_seq_2, 1)
    kv_seqs = (kv_seq, kv_seq_1, kv_seq_2, kv_seq_3)
    (dn_own,) = fence([dn_own], kv_seq_1, kv_seq_3)
    (y_late,) = fence([y], dn_own)
    y_own = lax.psum_scatter(y_late, "tp", scatter_dimension=0, tiled=True)

    mine = pl.BlockSpec((1, rows, width), lambda i, scal: (scal[2], 0, 0))
    dh2, do, dh2_low, sums = call(
        mid_kernel,
        (1,),
        [
            whole((1, dn_rows, width)),
            pl.BlockSpec((1, 8, rows), lambda i, scal: (scal[2], 0, 0)),
            whole((rows, width)),
            mine,
            mine,
            whole((16, width)),
            whole((tp_size, 2, head_cols, half)),
        ],
        [
            whole((rows, width)),
            whole((tp_size, rows // 2, 2 * head_cols)),
            whole((rows, width)),
            whole((16, width)),
        ],
        [
            shape_of((rows, width), F32),
            shape_of((tp_size, rows // 2, 2 * head_cols)),
            shape_of((rows, width)),
            shape_of((16, width), F32),
        ],
        [pltpu.VMEM((width, width), BF16)],
    )(scal, dn_own, gates, h2, n2, cotangent, small, out_pieces)

    cos_t, sin_t = jnp.transpose(cosine), jnp.transpose(sine)
    kv_block = by_step((rows, 2 * head_cols))
    kv_shape = shape_of((tp_size, rows, 2 * head_cols))
    dq, e0, e1, e2, e3 = call(
        attn_bwd_kernel,
        (tp_size,),
        [by_step((rows, packed))]
        + [kv_block] * 4
        + [by_step((rows // 2, 2 * head_cols)), whole((HD // 2, rows)), whole((HD // 2, rows))],
        [by_step((rows, head_cols))] + [kv_block] * 4,
        [shape_of((tp_size, rows, head_cols))] + [kv_shape] * 4,
        prefetch=2,
    )(scal, prefix, qkv_seq, *kv_seqs, do, cos_t, sin_t)
    if direct:
        early = [sums_of[index] for index in (1, 0)]
        flat = fence([total.far for total in early] + [e1, e3])
        for total, value in zip(early, flat):
            total.far = value
        e1, e3 = flat[2:]
    from_core_1 = over_ctx(e1, 1)
    from_core_3 = over_ctx(e3, 1)
    far = (e2.astype(F32) + from_core_3.astype(F32)).astype(BF16)
    dq, far, dh2_low = fence([dq, far, dh2_low], from_core_1)
    from_y = over_ctx(far, 2)
    if direct:
        away = [total.second() for total in early]
        (dh2_low,) = fence([dh2_low], *away)

    pair_out = pl.BlockSpec((4, 1, width // 8, 2 * head_cols), lambda i, *_: (0, i, 0, 0))
    pair_shape = shape_of((4, tp_size, width // 8, 2 * head_cols))
    first_grads = call(
        first_grads_kernel,
        (tp_size,),
        [
            mine,
            by_step((rows, head_cols)),
            whole((rows, width)),
            pl.BlockSpec((1, 1, rows // 2, 2 * head_cols), lambda i, scal: (i, scal[2], 0, 0)),
        ],
        [pair_out] * 2,
        [pair_shape] * 2,
    )(scal, n1, dq, dh2_low, o_all)

    if direct:
        sum_qo = Sum(first_grads[0], over_ctx(first_grads[1], 1), True)
        (from_y,) = fence([from_y], sum_qo.first())
    dkv = call(
        swing_kernel,
        (tp_size,),
        [kv_block] * 3 + [whole((rows, packed))] * 2,
        kv_block,
        kv_shape,
        prefetch=0,
    )(e0, from_core_1, from_y, cos_table, sin_table)

    def by_group(shape):
        return pl.BlockSpec((1,) + shape, lambda i, *_: (i, 0, 0))

    gi, sums = call(
        end_kernel,
        (tp_size,),
        [by_group((rows, head_cols)), by_group((rows, 2 * head_cols))]
        + [by_group((width // 4, packed))] * 4
        + [whole((rows, width)), mine, whole((16, width)), whole((16, width))],
        [whole((rows, width)), whole((16, width))],
        [shape_of((rows, width)), shape_of((16, width), F32)],
        [pltpu.VMEM((width, packed), BF16), pltpu.VMEM((rows, width), F32)],
    )(scal, dq, dkv, *w_pieces, dh2, layer_input, small, sums)
    dkv_late, n1_late, sums, gi = fence([dkv, n1, sums, gi])
    if direct:
        dkv_late, sums_of[1].last = fence([dkv_late, sums_of[1].last])
    gi_all = lax.all_gather(gi, "tp", axis=0)
    last_shape = shape_of((4, tp_size + 1, width // 8, 2 * head_cols))
    second_grads = call(
        second_grads_kernel,
        (tp_size + 1,),
        [
            mine,
            pl.BlockSpec((1, rows, 2 * head_cols), lambda i, *_: (jnp.minimum(i, tp_size - 1), 0, 0)),
            whole((16, width)),
        ],
        [pair_out] * 2,
        [last_shape] * 2,
    )(scal, n1_late, dkv_late, sums)

    if direct:
        sum_kv = Sum(second_grads[0], over_ctx(second_grads[1], 1), False)
        (sum_qo.got,) = fence([sum_qo.got], *second_grads)
        sum_kv.fence(sum_qo.first())
        sums_of[2].far, sums_of[3].far, y_own = fence([sums_of[2].far, sums_of[3].far, y_own], sum_kv.first())
        away = [sums_of[2].second(), sums_of[3].second()]
        early = (1, 0)
        flat = fence([sums_of[index].last for index in early] + [y_own], *away)
        for index, value in zip(early, flat):
            sums_of[index].last = value
        y_own = flat[-1]
        results = [sums_of[index].result() for index in (0, 1)]
        (sum_qo.far,) = fence([sum_qo.far], *results)
        away = sum_qo.second()
        sum_kv.far, gi_all = fence([sum_kv.far, gi_all], away)
        away = sum_kv.second()
        sums_of[2].last, sums_of[3].last = fence([sums_of[2].last, sums_of[3].last], away)
        results += [sums_of[2].result(), sums_of[3].result()]
        sum_kv.last, sum_qo.last = fence([sum_kv.last, sum_qo.last], *results)
        grads_qo, grads_kv = sum_qo.result(), sum_kv.result()
    else:
        grads_qo, grads_kv = scatter_plain(*first_grads), scatter_plain(*second_grads)
        results = [scatter_plain(*expert_group), scatter_plain(*shared_group)]
    activations = lax.all_gather((h2 + y_own[0].astype(F32)).astype(BF16), "tp", axis=0)
    grads_all = jnp.concatenate(
        [grads_qo, grads_kv[:tp_size], jnp.broadcast_to(grads_kv[tp_size:, :, :128], (tp_size, part, 128))], axis=-1
    )
    grads_all, gi_all = fence([grads_all.astype(BF16), gi_all])
    grads_all = jnp.sum(lax.all_to_all(grads_all, "tp", 0, 0, tiled=True).astype(F32), 0)
    grads_qo, grads_kv = grads_all[:, :2 * head_cols], grads_all[:, 2 * head_cols:4 * head_cols]
    sums = jnp.transpose(grads_all[:, 4 * head_cols:4 * head_cols + 16])
    grad_input = gi_all.astype(F32)
    results = [value.reshape(value.shape[0], 3, part, hidden) for value in results]
    grads_shared = results[-1][0]
    results = results[:-1]
    grads_exp = [jnp.concatenate([value[:, i] for value in results], axis=0) for i in range(3)]

    return (
        activations.reshape(layer_input.shape),
        grad_input.reshape(layer_input.shape),
        sums[8],
        grads_qo[:, :head_cols],
        grads_kv[:, :head_cols],
        grads_kv[:, head_cols:],
        jnp.transpose(grads_qo[:, head_cols:]),
        sums[9],
        jnp.transpose(sums[0:8]),
        grads_exp[0],
        grads_exp[1],
        jnp.transpose(grads_exp[2], (0, 2, 1)),
        grads_shared[0],
        grads_shared[1],
        jnp.transpose(grads_shared[2]),
    )


def solution(mesh):
    placed = (
        P("fsdp", "ctx", None),
        P("fsdp"),
        P("fsdp", "tp"),
        P("fsdp", "tp"),
        P("fsdp", "tp"),
        P("tp", "fsdp"),
        P("fsdp"),
        P("fsdp", None),
        P(None, "fsdp", "tp"),
        P(None, "fsdp", "tp"),
        P(None, "tp", "fsdp"),
        P("fsdp", "tp"),
        P("fsdp", "tp"),
        P("tp", "fsdp"),
        P("fsdp", "ctx", None),
        P("fsdp"),
        P("fsdp", "ctx", None),
    )
    return jax.shard_map(
        functools.partial(body, mesh.shape["fsdp"]),
        mesh=mesh,
        in_specs=placed,
        out_specs=(
            P("fsdp", "ctx", None),
            P("fsdp", "ctx", None),
            P(("fsdp", "ctx")),
            P(("fsdp", "ctx"), "tp"),
            P(("fsdp", "ctx"), "tp"),
            P(("fsdp", "ctx"), "tp"),
            P("tp", ("fsdp", "ctx")),
            P(("fsdp", "ctx")),
            P(("fsdp", "ctx"), None),
            P(None, ("fsdp", "ctx"), "tp"),
            P(None, ("fsdp", "ctx"), "tp"),
            P(None, "tp", ("fsdp", "ctx")),
            P(("fsdp", "ctx"), "tp"),
            P(("fsdp", "ctx"), "tp"),
            P("tp", ("fsdp", "ctx")),
        ),
        check_vma=False,
    )
```

```python
import functools
import math

import jax
import jax.numpy as jnp
from jax import lax
from jax.experimental import pallas as pl
from jax.experimental.pallas import tpu as pltpu
from jax.sharding import PartitionSpec as P

HD = 64
SLOTS = 80
EPS = 1e-06
F32 = jnp.float32
BF16 = jnp.bfloat16
VMEM_BYTES = 56 * 1024 * 1024


def mm(a, b):
    return lax.dot_general(a, b, (((1,), (0,)), ((), ())), preferred_element_type=F32)


def mm_nt(a, b):
    return lax.dot_general(a, b, (((1,), (1,)), ((), ())), preferred_element_type=F32)


def mm_tn(a, b):
    return lax.dot_general(a, b, (((0,), (0,)), ((), ())), preferred_element_type=F32)


def params(steps=1):
    return pltpu.CompilerParams(
        dimension_semantics=("arbitrary",) * steps, vmem_limit_bytes=VMEM_BYTES
    )


def rotation(width):
    row = lax.broadcasted_iota(jnp.int32, (width, width), 0)
    col = lax.broadcasted_iota(jnp.int32, (width, width), 1)
    first = (col % HD) < HD // 2
    minus = first & (row == col + HD // 2)
    plus = jnp.logical_not(first) & (row == col - HD // 2)
    return jnp.where(minus, -1.0, jnp.where(plus, 1.0, 0.0)).astype(BF16)


def row_scale(value):
    return lax.rsqrt(jnp.mean(value * value, -1, keepdims=True) + EPS)


def qkv_kernel(scal, x_ref, own_ref, oth_ref, cos_ref, sin_ref, n1_ref, q_ref, kv_ref, all_ref, w_ref, small_ref, swap):
    half = own_ref.shape[1]
    packed = w_ref.shape[0]

    @pl.when(pl.program_id(0) == 0)
    def _():
        mine = pl.multiple_of(scal[0] * half, half)
        other = pl.multiple_of((1 - scal[0]) * half, half)
        w_ref[:, pl.ds(mine, half)] = own_ref[:packed, :]
        w_ref[:, pl.ds(other, half)] = oth_ref[:packed, :]
        swap[...] = mm_tn(rotation(packed), w_ref[...]).astype(BF16)
        small_ref[...] = w_ref[192:208, :].astype(F32)

    x = x_ref[0].astype(F32)
    n1 = (x * row_scale(x) * small_ref[8:9, :]).astype(BF16)
    n1_ref[0] = n1
    turned = (mm_nt(n1, w_ref[...]) * cos_ref[...] + mm_nt(n1, swap[...]) * sin_ref[...]).astype(BF16)
    q_ref[0] = turned[:, :192]
    kv_ref[0] = turned[:, 256:640]
    all_ref[0] = turned


def visible(scal, prefix, keys, rows):
    key_pos = lax.broadcasted_iota(jnp.int32, (keys, rows), 0) ^ (scal[1] * rows)
    row_pos = lax.broadcasted_iota(jnp.int32, (keys, rows), 1) + scal[1] * rows
    return (key_pos <= row_pos) | (key_pos < prefix)


def only_head(rows, head):
    lane = lax.broadcasted_iota(jnp.int32, rows.shape, 1)
    return jnp.where((lane >= head * HD) & (lane < (head + 1) * HD), rows, jnp.zeros_like(rows))


def softmax(scores, seen):
    scores = jnp.where(seen, scores, -1e30)
    expo = jnp.exp(scores - jnp.max(scores, 0, keepdims=True))
    return expo, 1.0 / jnp.sum(expo, 0, keepdims=True)


def attn_fwd_kernel(scal, prefix, q_ref, kv0, kv1, kv2, kv3, o_ref):
    q = q_ref[0]
    rows, width = q.shape
    heads = width // HD
    kv = jnp.concatenate([kv0[0], kv1[0], kv2[0], kv3[0]], axis=0)
    k = kv[:, :width]
    value_t = jnp.transpose(kv[:, width:].astype(F32)).astype(BF16)
    seen = visible(scal, prefix[pl.program_id(0)], kv.shape[0], rows)
    outs = []
    for head in range(heads):
        expo, factor = softmax(mm_nt(k, only_head(q, head) * (HD ** -0.5)), seen)
        outs.append(mm(value_t[head * HD:(head + 1) * HD], expo.astype(BF16)) * factor)
    o = jnp.transpose(jnp.concatenate(outs, axis=0))
    o_ref[0] = jnp.concatenate([o[: rows // 2], o[rows // 2:]], axis=1).astype(BF16)


def fill_out_weights(scal, wo, wo_ref):
    pieces, _, width, half = wo_ref.shape
    for piece in range(pieces):
        for index, side in enumerate((scal[0], 1 - scal[0])):
            at = pl.ds(pl.multiple_of(side * half, half), half)
            wo[piece * width:(piece + 1) * width, at] = wo_ref[piece, index]


def post_kernel(scal, o_ref, wo_ref, x_ref, small_ref, routes_ref, n2_ref, h2_ref, gates_ref, slots_ref, wo):
    step = pl.program_id(0)
    width = wo_ref.shape[2]

    @pl.when(step == 0)
    def _():
        fill_out_weights(scal, wo, wo_ref)

    low = jnp.zeros((o_ref.shape[2], wo.shape[1]), F32)
    high = low
    for piece in range(o_ref.shape[0]):
        block = o_ref[piece, 0]
        weights = wo[piece * width:(piece + 1) * width, :]
        low += mm(block[:, :width], weights)
        high += mm(block[:, width:], weights)
    h2 = x_ref[0].astype(F32) + jnp.concatenate([low, high], axis=0)
    n2 = (h2 * row_scale(h2) * small_ref[9:10, :]).astype(BF16)
    n2_ref[0] = n2

    @pl.when(step == scal[2])
    def _():
        h2_ref[...] = h2

    expo = jnp.exp(mm_nt(small_ref[0:8, :].astype(BF16), n2))
    gates_ref[0] = expo / jnp.sum(expo, 0, keepdims=True)
    rows = n2.shape[0]
    expert = lax.broadcasted_iota(jnp.int32, (8, rows), 0)
    named = (routes_ref[0, 0:1, :] == expert) | (routes_ref[0, 1:2, :] == expert)
    before = lax.broadcasted_iota(jnp.int32, (rows, rows), 0) < lax.broadcasted_iota(jnp.int32, (rows, rows), 1)
    place = mm(named.astype(BF16), before.astype(BF16))
    slots_ref[0] = jnp.where(named, place.astype(jnp.int32), -1)


def silu_parts(value):
    sigma = 1.0 / (1.0 + jnp.exp(-value))
    return sigma, value * sigma


def split_blocks(core, value, blocks):
    rows = value.shape[0] // (2 * blocks)
    value = value.astype(BF16).reshape(blocks, 2, rows, value.shape[1])
    first = core == 0
    return jnp.where(first, value[:, 0], value[:, 1]), jnp.where(first, value[:, 1], value[:, 0])


def put_grads(core, keep_ref, send_ref, index, value):
    keep, send = split_blocks(core, value, keep_ref.shape[0])
    at = slice(index * keep.shape[1], (index + 1) * keep.shape[1])
    keep_ref[:, 0, at, :] = keep
    send_ref[:, 0, at, :] = send


def shared_kernel(
    scal, n2_ref, dy_ref, go_ref, uo_ref, do_ref, g0, g1, g2, g3, u0, u1, u2, u3, d0, d1, d2, d3,
    ys_ref, dn_ref, hid_ref, dab_ref, wgu, wd,
):
    step = pl.program_id(0)
    half = go_ref.shape[0]
    hidden = go_ref.shape[1]

    @pl.when(step == 0)
    def _():
        mine = pl.multiple_of(scal[0] * half, half)
        other = (1 - scal[0]) * half
        wgu[pl.ds(mine, half), :hidden] = go_ref[...]
        wgu[pl.ds(mine, half), hidden:] = uo_ref[...]
        wd[:, pl.ds(mine, half)] = do_ref[...]
        for piece, (g, u, d) in enumerate(((g0, u0, d0), (g1, u1, d1), (g2, u2, d2), (g3, u3, d3))):
            quarter = scal[3] ^ piece
            at = pl.multiple_of(other + quarter * (half // 4), half // 4)
            wgu[pl.ds(at, half // 4), :hidden] = g[...]
            wgu[pl.ds(at, half // 4), hidden:] = u[...]
            at = pl.multiple_of(quarter * (hidden // 4), hidden // 4)
            wd[pl.ds(at, hidden // 4), pl.ds(pl.multiple_of(other, half), half)] = d[...]

    n2 = n2_ref[0]
    dy = dy_ref[0]
    both = mm(n2, wgu[...])
    gate, up = both[:, :hidden], both[:, hidden:]
    sigma, silu = silu_parts(gate)
    hid = (silu * up).astype(BF16)
    ys_ref[0] = mm(hid, wd[...]).astype(BF16)
    back = mm_nt(dy, wd[...])
    da = (back * up * (sigma * (1.0 + gate * (1.0 - sigma)))).astype(BF16)
    db = (back * silu).astype(BF16)
    dab = jnp.concatenate([da, db], axis=1)
    dn_ref[0] = mm_nt(dab, wgu[...]).astype(BF16)
    hid_ref[0] = hid
    dab_ref[0] = dab


def put_all_grads(core, keep_ref, send_ref, value, upstream, hid, dab):
    wide = mm_tn(value, dab)
    hidden = hid.shape[1]
    put_grads(core, keep_ref, send_ref, 0, wide[:, :hidden])
    put_grads(core, keep_ref, send_ref, 1, wide[:, hidden:])
    put_grads(core, keep_ref, send_ref, 2, mm_tn(upstream, hid))


def shared_grads_kernel(scal, n2_ref, dy_ref, hid_ref, dab_ref, keep_ref, send_ref):
    values = [ref[...].reshape(-1, ref.shape[-1]) for ref in (n2_ref, dy_ref, hid_ref, dab_ref)]
    put_all_grads(scal[4], keep_ref, send_ref, *values)


def moe_kernel(
    scal, n2_ref, dy_ref, slots_ref, gates_ref, ys_ref, dn_in_ref, go_ref, uo_ref, do_ref,
    g0, g1, g2, g3, u0, u1, u2, u3, v0, v1, v2, v3, d0, d1, d2, d3,
    y_ref, dn_ref, keep_ref, send_ref, wgu, wd, pick_s, ye_s, dx_s, xe_s, dy_s, de_s, gs_s, dprob_s,
):
    step = pl.program_id(0)
    seqs, rows, width = n2_ref.shape
    half = go_ref.shape[1]
    experts = slots_ref.shape[1]

    @pl.when(step < experts)
    def _():
        piece = step // 2
        expert = 2 * (piece ^ scal[3]) + step % 2
        mine = pl.multiple_of(scal[0] * half, half)
        other = pl.multiple_of((1 - scal[0]) * half, half)
        hidden = go_ref.shape[2]
        wgu[pl.ds(mine, half), :hidden] = go_ref[0]
        wgu[pl.ds(mine, half), hidden:] = uo_ref[0]
        wd[:, pl.ds(mine, half)] = do_ref[0]
        arrived = ((g0, u0, v0, d0), (g1, u1, v1, d1), (g2, u2, v2, d2), (g3, u3, v3, d3))
        for index, (g, u, v, d) in enumerate(arrived):
            @pl.when(piece == index)
            def _(g=g, d=d):
                wgu[pl.ds(other, half), :hidden] = g[...]
                wd[:, pl.ds(other, half)] = d[...]

            for odd, ref in enumerate((u, v)):
                @pl.when((piece == index) & (step % 2 == odd))
                def _(ref=ref):
                    wgu[pl.ds(other, half), hidden:] = ref[...]

        slot_at = pl.ds(pl.multiple_of(step * SLOTS, 16), SLOTS)
        slot = lax.broadcasted_iota(jnp.int32, (SLOTS, rows), 0)
        for s in range(seqs):
            at = slice(s * SLOTS, (s + 1) * SLOTS)
            hit = slots_ref[s, pl.ds(expert, 1), :] == slot
            gate_slot = jnp.sum(jnp.where(hit, gates_ref[s, pl.ds(expert, 1), :], 0.0), 1, keepdims=True)
            pick = hit.astype(BF16)
            pick_s[s, slot_at, :] = pick
            xe_s[at, :] = mm(pick, n2_ref[s]).astype(BF16)
            upstream = mm(pick, dy_ref[s])
            dy_s[at, :] = upstream.astype(BF16)
            de_s[at, :] = (gate_slot * upstream).astype(BF16)
            gs_s[at, :] = jnp.broadcast_to(gate_slot, (SLOTS, 128))

        xe = xe_s[...]
        both = mm(xe, wgu[...])
        gate, up = both[:, :hidden], both[:, hidden:]
        sigma, silu = silu_parts(gate)
        hid = (silu * up).astype(BF16)
        ye = mm(hid, wd[...])
        dots = jnp.sum(ye * dy_s[...].astype(F32), 1, keepdims=True)
        ye = (ye * gs_s[:, 0:1]).astype(BF16)
        for s in range(seqs):
            at = slice(s * SLOTS, (s + 1) * SLOTS)
            ye_s[s, slot_at, :] = ye[at]
            hit = slots_ref[s, pl.ds(expert, 1), :] == slot
            dprob_s[s, pl.ds(expert, 1), :] = jnp.sum(jnp.where(hit, dots[at], 0.0), 0, keepdims=True)
        back = mm_nt(de_s[...], wd[...])
        da = (back * up * (sigma * (1.0 + gate * (1.0 - sigma)))).astype(BF16)
        db = (back * silu).astype(BF16)
        dab = jnp.concatenate([da, db], axis=1)
        dx = mm_nt(dab, wgu[...]).astype(BF16)
        for s in range(seqs):
            dx_s[s, slot_at, :] = dx[s * SLOTS:(s + 1) * SLOTS]
        put_all_grads(scal[4], keep_ref, send_ref, xe, de_s[...], hid, dab)

    @pl.when(step >= experts)
    def _():
        s = step - experts
        pick = pick_s[s]
        y_ref[0] = (ys_ref[0].astype(F32) + mm_tn(pick, ye_s[s])).astype(BF16)
        dn_ref[0, 0:rows, :] = (dn_in_ref[0].astype(F32) + mm_tn(pick, dx_s[s])).astype(BF16)
        tail = jnp.concatenate([dprob_s[s], jnp.zeros((dn_ref.shape[1] - rows - experts, rows), F32)], axis=0)
        tail = jnp.concatenate([tail, jnp.zeros((tail.shape[0], width - rows), F32)], axis=1)
        dn_ref[0, rows:, :] = tail.astype(BF16)


def norm_back(grad_out, value, scale, gain):
    weighted = grad_out * gain
    return scale * weighted - value * (scale * scale * scale) * jnp.mean(weighted * value, -1, keepdims=True)


def mid_kernel(scal, dn_ref, gates_ref, h2_ref, n2_ref, dy_ref, small_ref, wo_ref, dh2_ref, do_ref, low_ref, sums_ref, wo):
    rows = h2_ref.shape[0]
    pieces, _, width, _ = wo_ref.shape
    fill_out_weights(scal, wo, wo_ref)
    parts = dn_ref[0].astype(F32)
    gates = gates_ref[0]
    dprob = parts[rows:rows + 8, 0:rows]
    dlogits = (gates * (dprob - jnp.sum(dprob * gates, 0, keepdims=True))).astype(BF16)
    dn2 = parts[0:rows, :] + mm_tn(dlogits, small_ref[0:8, :].astype(BF16))
    h2 = h2_ref[...]
    scale = row_scale(h2)
    sums_ref[0:8, :] = mm(dlogits, n2_ref[0])
    sums_ref[8:16, :] = jnp.zeros((8, h2.shape[1]), F32)
    sums_ref[9:10, :] = jnp.sum(dn2 * h2 * scale, 0, keepdims=True)
    dh2 = dy_ref[0].astype(F32) + norm_back(dn2, h2, scale, small_ref[9:10, :])
    dh2_ref[...] = dh2
    low = dh2.astype(BF16)
    low_ref[...] = low
    for piece in range(pieces):
        do = mm_nt(low, wo[piece * width:(piece + 1) * width, :])
        do_ref[piece] = jnp.concatenate([do[: rows // 2], do[rows // 2:]], axis=1).astype(BF16)


def attn_bwd_kernel(
    scal, prefix, q_ref, kv0, kv1, kv2, kv3, do_ref, cos_ref, sin_ref, dq_ref, e0, e1, e2, e3
):
    rows, width = dq_ref.shape[1:]
    q = q_ref[0][:, :width]
    heads = width // HD
    kv = jnp.concatenate([kv0[0], kv1[0], kv2[0], kv3[0]], axis=0)
    k = kv[:, :width]
    v = kv[:, width:]
    key_t = jnp.transpose(k.astype(F32)).astype(BF16)
    do = jnp.concatenate([do_ref[0][:, :width], do_ref[0][:, width:]], axis=0)
    seen = visible(scal, prefix[scal[2]], kv.shape[0], rows)
    cosine, sine = cos_ref[...], sin_ref[...]
    turned, ds_all, probs_all, q_all, do_all = [], [], [], [], []
    for head in range(heads):
        q_head = only_head(q, head) * (HD ** -0.5)
        do_head = only_head(do, head)
        expo, factor = softmax(mm_nt(k, q_head), seen)
        probs = expo * factor
        dp = mm_nt(v, do_head)
        ds = (probs * (dp - jnp.sum(dp * probs, 0, keepdims=True))).astype(BF16)
        dq = mm(key_t[head * HD:(head + 1) * HD], ds) * (HD ** -0.5)
        first, second = dq[: HD // 2], dq[HD // 2:]
        turned += [first * cosine + second * sine, second * cosine - first * sine]
        ds_all.append(ds)
        probs_all.append(probs.astype(BF16))
        q_all.append(q_head)
        do_all.append(do_head)
    dq_ref[0] = jnp.transpose(jnp.concatenate(turned, axis=0)).astype(BF16)
    dk = mm(jnp.concatenate(ds_all, axis=1), jnp.concatenate(q_all, axis=0))
    dv = mm(jnp.concatenate(probs_all, axis=1), jnp.concatenate(do_all, axis=0))
    dkv = jnp.concatenate([dk, dv], axis=1).astype(BF16)
    for piece, out in enumerate((e0, e1, e2, e3)):
        out[0] = dkv[piece * rows:(piece + 1) * rows]


def swing_kernel(a_ref, b_ref, c_ref, cos_ref, sin_ref, out_ref):
    dkv = a_ref[0].astype(F32) + b_ref[0].astype(F32) + c_ref[0].astype(F32)
    swung = dkv * sin_ref[:, 256:]
    high = swung.astype(BF16)
    low = (swung - high.astype(F32)).astype(BF16)
    turn = rotation(dkv.shape[1])
    out_ref[0] = (dkv * cos_ref[:, 256:] + mm_nt(high, turn) + mm_nt(low, turn)).astype(BF16)


def end_kernel(scal, dq_ref, dkv_ref, w0, w1, w2, w3, dh2_ref, x_ref, small_ref, sums_in, gi_ref, sums_ref, w, total):
    step = pl.program_id(0)
    head_cols = dq_ref.shape[2]
    quarter = w.shape[0] // 4
    for piece, ref in enumerate((w0, w1, w2, w3)):
        at = pl.multiple_of((scal[1] ^ piece) * quarter, quarter)
        w[pl.ds(at, quarter), :] = ref[0]
    part = mm(dq_ref[0], w[:head_cols, :]) + mm(dkv_ref[0], w[256:, :])

    @pl.when(step == 0)
    def _():
        total[...] = part

    @pl.when(step > 0)
    def _():
        total[...] += part

    @pl.when(step == pl.num_programs(0) - 1)
    def _():
        x = x_ref[0].astype(F32)
        dn1 = total[...]
        scale = row_scale(x)
        sums_ref[...] = sums_in[...]
        sums_ref[8:9, :] = jnp.sum(dn1 * x * scale, 0, keepdims=True)
        gi_ref[...] = (dh2_ref[...] + norm_back(dn1, x, scale, small_ref[8:9, :])).astype(BF16)


def first_grads_kernel(scal, n1_ref, dq_ref, low_ref, o_ref, keep_ref, send_ref):
    head_cols = dq_ref.shape[2]
    block = o_ref[0, 0]
    o = jnp.concatenate([block[:, :head_cols], block[:, head_cols:]], axis=0)
    grads = jnp.concatenate([mm_tn(n1_ref[0], dq_ref[0]), mm_tn(low_ref[...], o)], axis=1)
    keep_ref[:, 0], send_ref[:, 0] = split_blocks(scal[4], grads, keep_ref.shape[0])


def second_grads_kernel(scal, n1_ref, dkv_ref, sums_ref, keep_ref, send_ref):
    step = pl.program_id(0)
    last = pl.num_programs(0) - 1

    @pl.when(step < last)
    def _():
        keep_ref[:, 0], send_ref[:, 0] = split_blocks(scal[4], mm_tn(n1_ref[0], dkv_ref[0]), keep_ref.shape[0])

    @pl.when(step == last)
    def _():
        sums = sums_ref[...]
        sums = jnp.concatenate([sums, jnp.zeros((keep_ref.shape[3] - sums.shape[0], sums.shape[1]), F32)], axis=0)
        keep_ref[:, 0], send_ref[:, 0] = split_blocks(scal[4], jnp.transpose(sums), keep_ref.shape[0])


def whole(shape):
    return pl.BlockSpec(shape, lambda *_: (0,) * len(shape))


def by_step(shape):
    return pl.BlockSpec((1,) + shape, lambda i, *_: (i,) + (0,) * len(shape))


def call(kernel, grid, in_specs, out_specs, out_shape, scratch=(), prefetch=1, aliases=None):
    return pl.pallas_call(
        kernel,
        grid_spec=pltpu.PrefetchScalarGridSpec(
            num_scalar_prefetch=prefetch,
            grid=grid,
            in_specs=in_specs,
            out_specs=out_specs,
            scratch_shapes=scratch,
        ),
        out_shape=out_shape,
        input_output_aliases=aliases or {},
        compiler_params=params(len(grid)),
        cost_estimate=pl.CostEstimate(flops=1, bytes_accessed=1, transcendentals=0),
    )


def fence(values, *others):
    values = list(values)
    return list(lax.optimization_barrier((*values, *others))[: len(values)])


def shape_of(shape, dtype=BF16):
    return jax.ShapeDtypeStruct(shape, dtype)


def body(
    fsdp_size,
    layer_input,
    gain_attn,
    query_weight,
    key_weight,
    value_weight,
    output_weight,
    gain_ffn,
    router,
    exp_gate,
    exp_up,
    exp_down,
    shared_gate_weight,
    shared_up_weight,
    shared_down_weight,
    routes,
    prefix,
    cotangent,
):
    seqs, rows, width = layer_input.shape
    experts = exp_gate.shape[0]
    hidden = exp_gate.shape[2]
    head_cols = query_weight.shape[1]
    half = width // 2
    paired = fsdp_size == 2
    ctx = lax.axis_index("ctx")
    tp = lax.axis_index("tp")
    ctx_size = lax.axis_size("ctx")
    tp_size = lax.axis_size("tp")
    side = lax.axis_index("fsdp") if paired else jnp.int32(0)
    weight_ctx = ctx if paired else jnp.int32(0)
    blocks = fsdp_size * ctx_size
    direct = paired and ctx_size == 4 and tp_size == 4
    core = ctx % 2 if direct else jnp.int32(0)
    scal = jnp.stack([side, ctx, tp, weight_ctx, core]).astype(jnp.int32)

    def over_x(value):
        return lax.ppermute(value, "fsdp", [(0, 1), (1, 0)])

    def over_tp(value, bit):
        return lax.ppermute(value, "tp", [(i, i ^ bit) for i in range(tp_size)])

    def over_ctx(value, bit):
        return lax.ppermute(value, "ctx", [(i, i ^ bit) for i in range(ctx_size)])

    columns = jnp.concatenate(
        [
            query_weight.T,
            router.T,
            gain_attn[None],
            gain_ffn[None],
            jnp.zeros((54, query_weight.shape[0]), BF16),
            key_weight.T,
            value_weight.T,
            output_weight,
        ],
        axis=0,
    )
    if paired:
        columns_own, columns_other = columns, over_x(columns)
    else:
        columns = lax.all_gather(columns, "fsdp", axis=1, tiled=True)
        columns_own, columns_other = columns[:, :half], columns[:, half:]

    shared_own = (shared_gate_weight, shared_up_weight, shared_down_weight)
    experts_own = (exp_gate, exp_up, exp_down)
    if paired:

        def quarter(value, parts):
            size = value.shape[0] // parts
            return lax.dynamic_slice_in_dim(value, size * ctx, size, 0).reshape(-1, value.shape[-1])

        gate, up, down = [quarter(stack, 4) for stack in experts_own]
        shared_gate, shared_up, shared_down = [quarter(stack, 4) for stack in shared_own]
        wide = jnp.concatenate([gate, up[:half], shared_gate, shared_up], axis=0)
        rest = up[half:]
        down = jnp.concatenate([down, shared_down], axis=0)
        own = experts_own + shared_own
    else:
        gate_all = lax.all_gather(exp_gate, "fsdp", axis=1, tiled=True)
        up_all = lax.all_gather(exp_up, "fsdp", axis=1, tiled=True)
        down_all = lax.all_gather(exp_down, "fsdp", axis=2, tiled=True)
        sg_all = lax.all_gather(shared_gate_weight, "fsdp", axis=0, tiled=True)
        su_all = lax.all_gather(shared_up_weight, "fsdp", axis=0, tiled=True)
        sd_all = lax.all_gather(shared_down_weight, "fsdp", axis=1, tiled=True)
        own = (gate_all[:, :half], up_all[:, :half], down_all[:, :, :half], sg_all[:half], su_all[:half], sd_all[:, :half])

        def split(value):
            return value.reshape((4, value.shape[0] // 4) + value.shape[1:])

        gate_all, up_all, sg_all, su_all = [
            split(value) for value in (gate_all[:, half:], up_all[:, half:], sg_all[half:], su_all[half:])
        ]
        down_all, sd_all = split(down_all[:, :, half:]), split(sd_all[:, half:])
        wide_p = [
            jnp.concatenate([gate_all[p, 0], gate_all[p, 1], up_all[p, 0], sg_all[p], su_all[p]], axis=0) for p in range(4)
        ]
        rest_p = [up_all[p, 1] for p in range(4)]
        down_p = [jnp.concatenate([down_all[p, 0], down_all[p, 1], sd_all[p]], axis=0) for p in range(4)]

    positions = (ctx * rows + jnp.arange(rows, dtype=jnp.int32)).astype(F32)
    inverse = jnp.exp(jnp.arange(HD // 2, dtype=F32) * (-math.log(10000.0) / (HD // 2)))
    angles = positions[:, None] * inverse[None, :]
    cosine, sine = jnp.cos(angles), jnp.sin(angles)
    heads = head_cols // HD

    def table(value, rest):
        turned = jnp.tile(value, (1, 2 * heads))
        plain = jnp.full((rows, head_cols), rest, F32)
        return jnp.concatenate([turned, plain[:, :64], turned, plain], axis=1)

    cos_table, sin_table = table(cosine, 1.0), table(sine, 0.0)
    routes_t = jnp.pad(jnp.transpose(routes, (0, 2, 1)), ((0, 0), (0, 6), (0, 0)))

    cos_t, sin_t = jnp.transpose(cosine), jnp.transpose(sine)
    columns_other, cos_table, sin_table, cos_t, sin_t = fence([columns_other, cos_table, sin_table, cos_t, sin_t], routes_t)
    if paired:
        columns_other, cos_table, wide, rest, down = fence([columns_other, cos_table, wide, rest, down])
        wide_0 = over_x(wide)
    out_pieces = jnp.stack([columns_own[-head_cols:], columns_other[-head_cols:]])
    out_pieces = lax.all_gather(out_pieces, "tp", axis=0)
    packed = cos_table.shape[1]

    n1, q, kv, qkv, w_qkv, small = call(
        qkv_kernel,
        (seqs,),
        [
            by_step((rows, width)),
            whole((packed + head_cols, half)),
            whole((packed + head_cols, half)),
            whole((rows, packed)),
            whole((rows, packed)),
        ],
        [
            by_step((rows, width)),
            by_step((rows, head_cols)),
            by_step((rows, 2 * head_cols)),
            by_step((rows, packed)),
            whole((packed, width)),
            whole((16, width)),
        ],
        [
            shape_of((seqs, rows, width)),
            shape_of((seqs, rows, head_cols)),
            shape_of((seqs, rows, 2 * head_cols)),
            shape_of((seqs, rows, packed)),
            shape_of((packed, width)),
            shape_of((16, width), F32),
        ],
        [pltpu.VMEM((packed, width), BF16)],
    )(scal, layer_input, columns_own, columns_other, cos_table, sin_table)

    kv_0 = kv
    kv_2 = over_ctx(kv_0, 2)
    kv_1 = over_ctx(kv_0, 1)
    q_now, kv_2 = fence([q, kv_2], kv_1)
    w_part = lax.dynamic_slice_in_dim(w_qkv, (packed // 4) * ctx, packed // 4, 0)
    w_part = jnp.pad(w_part, ((0, 16), (0, 0)))
    if paired:
        kv_2, wide_0, rest, down, w_part = fence([kv_2, wide_0, rest, down, w_part])
        wide_2 = over_ctx(wide_0, 2)
        rest_0 = over_x(rest)
        (down,) = fence([down], rest)
        down_0 = over_x(down)
    kv_3 = over_ctx(kv_2, 1)
    q_now, kv_3, out_pieces = fence([q_now, kv_3, out_pieces])

    o = call(
        attn_fwd_kernel,
        (seqs,),
        [by_step((rows, head_cols))] + [by_step((rows, 2 * head_cols))] * 4,
        by_step((rows // 2, 2 * head_cols)),
        shape_of((seqs, rows // 2, 2 * head_cols)),
        prefetch=2,
    )(scal, prefix, q_now, kv_0, kv_1, kv_2, kv_3)

    o_all = lax.all_gather(o, "tp", axis=0)
    if paired:
        wide_0, rest_0 = fence([wide_0, rest_0], o)
        rest_2, rest_1, wide_1 = over_ctx(rest_0, 2), over_ctx(rest_0, 1), over_ctx(wide_0, 1)
        down_0, wide_2, rest_1, wide_1 = fence([down_0, wide_2, rest_1, wide_1])
        down_2, down_1, wide_3 = over_ctx(down_0, 2), over_ctx(down_0, 1), over_ctx(wide_2, 1)
        (rest_2,) = fence([rest_2], down_0, wide_2)
        down_1, wide_3 = fence([down_1, wide_3], rest_2)
        rest_3 = over_ctx(rest_2, 1)
        o_all, down_1, wide_3 = fence([o_all, down_1, wide_3])
    w_0 = lax.all_gather(fence([w_part], o_all)[0], "tp", axis=0)
    n2, h2, gates, slots = call(
        post_kernel,
        (seqs,),
        [
            pl.BlockSpec((tp_size, 1, rows // 2, 2 * head_cols), lambda i, *_: (0, i, 0, 0)),
            whole((tp_size, 2, head_cols, half)),
            by_step((rows, width)),
            whole((16, width)),
            by_step((8, rows)),
        ],
        [by_step((rows, width)), whole((rows, width)), by_step((8, rows)), by_step((8, rows))],
        [
            shape_of((seqs, rows, width)),
            shape_of((rows, width), F32),
            shape_of((seqs, 8, rows), F32),
            shape_of((seqs, 8, rows), jnp.int32),
        ],
        [pltpu.VMEM((width, width), BF16)],
    )(scal, o_all, out_pieces, layer_input, small, routes_t)

    if paired:
        down_2, rest_3 = fence([down_2, rest_3], n2)
        down_3 = over_ctx(down_2, 1)
        wide_p = (wide_0, wide_1, wide_2, wide_3)
        rest_p = (rest_0, rest_1, rest_2, rest_3)
        down_p = (down_0, down_1, down_2, down_3)

    full = pl.BlockSpec((seqs, rows, width), lambda *_: (0, 0, 0), pipeline_mode=pl.Buffered(1))
    part_rows = 3 * (width // 8)
    upper = [pl.BlockSpec((half // 4, hidden), lambda *_, at=at: (at, 0)) for at in (12, 13)]
    lower = pl.BlockSpec((hidden // 4, half), lambda *_: (8, 0))
    weights = [pltpu.VMEM((width, 2 * hidden), BF16), pltpu.VMEM((hidden, width), BF16)]
    ys, dn_shared, *shared_hidden = call(
        shared_kernel,
        (seqs,),
        [by_step((rows, width))] * 2
        + [whole((half, hidden)), whole((half, hidden)), whole((hidden, half))]
        + [upper[0]] * 4
        + [upper[1]] * 4
        + [lower] * 4,
        [by_step((rows, width))] * 2 + [by_step((rows, hidden)), by_step((rows, 2 * hidden))],
        [shape_of((seqs, rows, width))] * 2 + [shape_of((seqs, rows, hidden)), shape_of((seqs, rows, 2 * hidden))],
        weights,
    )(scal, n2, cotangent, *own[3:], *wide_p, *wide_p, *down_p)

    qkv_late, w_0, ys = fence([qkv, w_0, ys])
    qkv_seq = lax.all_to_all(qkv_late, "tp", 0, 0, tiled=True)
    w_2, w_1 = over_ctx(w_0, 2), over_ctx(w_0, 1)

    def expert_of(i, scal):
        i = jnp.minimum(i, experts - 1)
        return 2 * ((i // 2) ^ scal[3]) + i % 2

    def of_expert(shape):
        return pl.BlockSpec((1,) + shape, lambda i, scal: (expert_of(i, scal), 0, 0))

    def piece_specs(shape):
        return [
            pl.BlockSpec(shape, lambda i, scal, p=p: (jnp.clip(i - 2 * p, 0, 1), 0)) for p in range(4)
        ]

    late = pl.BlockSpec((1, rows, width), lambda i, scal: (jnp.maximum(i - experts, 0), 0, 0))

    dn_rows = rows + 16
    slot_rows = seqs * SLOTS
    block = (4, 1, part_rows, hidden)

    expert_grads = pl.BlockSpec(block, lambda i, scal: (0, expert_of(i, scal), 0, 0))
    y, dn, *expert_group = call(
        moe_kernel,
        (experts + seqs,),
        [full, full, whole((seqs, 8, rows)), whole((seqs, 8, rows)), late, late]
        + [of_expert((half, hidden)), of_expert((half, hidden)), of_expert((hidden, half))]
        + piece_specs((half, hidden))
        + [pl.BlockSpec((half, hidden), lambda *_: (2, 0))] * 4
        + [pl.BlockSpec((half, hidden), lambda *_: (0, 0))] * 4
        + piece_specs((hidden, half)),
        [late, pl.BlockSpec((1, dn_rows, width), lambda i, *_: (jnp.maximum(i - experts, 0), 0, 0))]
        + [expert_grads] * 2,
        [shape_of((seqs, rows, width)), shape_of((seqs, dn_rows, width))]
        + [shape_of((4, experts, part_rows, hidden))] * 2,
        weights
        + [pltpu.VMEM((seqs, experts * SLOTS, rows), BF16)]
        + [pltpu.VMEM((seqs, experts * SLOTS, width), BF16)] * 2
        + [pltpu.VMEM((slot_rows, width), BF16)] * 3
        + [pltpu.VMEM((slot_rows, 128), F32), pltpu.VMEM((seqs, 8, rows), F32)],
    )(scal, n2, cotangent, slots, gates, ys, dn_shared, *own[:3], *wide_p, *wide_p, *rest_p, *down_p)

    dn, qkv_seq, w_2, w_1, n2_late, *expert_group = fence([dn, qkv_seq, w_2, w_1, n2, *expert_group])
    w_pieces = (w_0, w_1, w_2, over_ctx(w_2, 1))
    dn_own = lax.psum_scatter(dn, "tp", scatter_dimension=0, tiled=True)
    kv_seq = qkv_seq[:, :, 256:]
    kv_seq_2, kv_seq_1 = over_ctx(kv_seq, 2), over_ctx(kv_seq, 1)

    shared_group = call(
        shared_grads_kernel,
        (1,),
        [full] * 2 + [whole((seqs, rows, hidden)), whole((seqs, rows, 2 * hidden))],
        [whole(block)] * 2,
        [shape_of(block)] * 2,
    )(scal, n2_late, cotangent, *shared_hidden)

    part = width // blocks
    along_x, along_y = side, ctx // 2

    def pick(value, x, y, first, count):
        value = value.reshape((2, 2) + value.shape[1:])
        sizes = (2 if x is None else 1, 2 if y is None else 1, count) + value.shape[3:]
        begin = (0 if x is None else x, 0 if y is None else y, first, 0, 0)
        value = lax.dynamic_slice(value, begin, sizes)
        value = value.reshape(tuple(n for n, at in zip(sizes[:2], (x, y)) if at is None) + sizes[2:])
        return value.astype(F32)

    def indexed(value, index):
        return lax.dynamic_index_in_dim(value, index, 0, False).astype(F32)

    class Sum:
        def __init__(self, keep, got, y_first, first=0, count=None):
            self.keep, self.got, self.y_first = keep, got, y_first
            self.range = (first, count or keep.shape[1])

        def fence(self, *others):
            (self.got,) = fence([self.got], *others)

        def both(self, x, y):
            return pick(self.keep, x, y, *self.range) + pick(self.got, x, y, *self.range)

        def first(self):
            if self.y_first:
                self.sent = self.both(None, 1 - along_y).astype(BF16)
            else:
                self.sent = self.both(1 - along_x, None).astype(BF16)
            self.far = over_ctx(self.sent, 2) if self.y_first else over_x(self.sent)
            return self.sent

        def second(self):
            if self.y_first:
                self.away = (self.both(1 - along_x, along_y) + indexed(self.far, 1 - along_x)).astype(BF16)
                self.last = over_x(self.away)
            else:
                self.away = (self.both(along_x, 1 - along_y) + indexed(self.far, 1 - along_y)).astype(BF16)
                self.last = over_ctx(self.away, 2)
            return self.away

        def result(self):
            mine = indexed(self.far, along_x if self.y_first else along_y)
            return self.both(along_x, along_y) + mine + self.last.astype(F32)

    def scatter_plain(keep, send):
        count, cols = keep.shape[1], keep.shape[3]
        triples = keep.shape[2] // (width // 8)
        both = jnp.stack([keep, send], axis=1).reshape(8, count, triples, width // 8, cols)
        both = jnp.transpose(both, (0, 3, 1, 2, 4)).reshape(blocks, part, count * triples, cols)
        both = jnp.transpose(both, (0, 2, 1, 3)).reshape(blocks, count * triples * part, cols)
        both = lax.psum_scatter(both, ("fsdp", "ctx"), scatter_dimension=0, tiled=True)
        return both.reshape(count, triples * part, cols).astype(F32)

    if direct:
        got, shared_got = over_ctx(expert_group[1], 1), over_ctx(shared_group[1], 1)
        cuts = ((0, 2, True), (2, 2, False), (4, 4, False))
        sums_of = [Sum(expert_group[0], got, y_first, first, count) for first, count, y_first in cuts]
        sums_of.append(Sum(shared_group[0], shared_got, True))
        sent = [sums_of[1].first(), sums_of[0].first()]
        sums_of[2].fence(*sent)
        sent.append(sums_of[2].first())
        (kv_seq_2,) = fence([kv_seq_2], *sent)
    kv_seq_3 = over_ctx(kv_seq_2, 1)
    if direct:
        sums_of[3].fence(*sent, kv_seq_2)
        kv_seq_1, kv_seq_3 = fence([kv_seq_1, kv_seq_3], sums_of[3].first())
    kv_seqs = (kv_seq, kv_seq_1, kv_seq_2, kv_seq_3)
    (dn_own,) = fence([dn_own], kv_seq_1, kv_seq_3)
    (y_late,) = fence([y], dn_own)
    y_own = lax.psum_scatter(y_late, "tp", scatter_dimension=0, tiled=True)

    mine = pl.BlockSpec((1, rows, width), lambda i, scal: (scal[2], 0, 0))
    dh2, do, dh2_low, sums = call(
        mid_kernel,
        (1,),
        [
            whole((1, dn_rows, width)),
            pl.BlockSpec((1, 8, rows), lambda i, scal: (scal[2], 0, 0)),
            whole((rows, width)),
            mine,
            mine,
            whole((16, width)),
            whole((tp_size, 2, head_cols, half)),
        ],
        [
            whole((rows, width)),
            whole((tp_size, rows // 2, 2 * head_cols)),
            whole((rows, width)),
            whole((16, width)),
        ],
        [
            shape_of((rows, width), F32),
            shape_of((tp_size, rows // 2, 2 * head_cols)),
            shape_of((rows, width)),
            shape_of((16, width), F32),
        ],
        [pltpu.VMEM((width, width), BF16)],
    )(scal, dn_own, gates, h2, n2, cotangent, small, out_pieces)

    kv_block = by_step((rows, 2 * head_cols))
    kv_shape = shape_of((tp_size, rows, 2 * head_cols))
    dq, e0, e1, e2, e3 = call(
        attn_bwd_kernel,
        (tp_size,),
        [by_step((rows, packed))]
        + [kv_block] * 4
        + [by_step((rows // 2, 2 * head_cols)), whole((HD // 2, rows)), whole((HD // 2, rows))],
        [by_step((rows, head_cols))] + [kv_block] * 4,
        [shape_of((tp_size, rows, head_cols))] + [kv_shape] * 4,
        prefetch=2,
    )(scal, prefix, qkv_seq, *kv_seqs, do, cos_t, sin_t)
    if direct:
        early = [sums_of[index] for index in (1, 0)]
        flat = fence([total.far for total in early] + [e1, e3])
        for total, value in zip(early, flat):
            total.far = value
        e1, e3 = flat[2:]
    from_core_1 = over_ctx(e1, 1)
    from_core_3 = over_ctx(e3, 1)
    far = (e2.astype(F32) + from_core_3.astype(F32)).astype(BF16)
    dq, far, dh2_low = fence([dq, far, dh2_low], from_core_1)
    from_y = over_ctx(far, 2)
    if direct:
        away = [total.second() for total in early]
        (dh2_low,) = fence([dh2_low], *away)

    pair_out = pl.BlockSpec((4, 1, width // 8, 2 * head_cols), lambda i, *_: (0, i, 0, 0))
    pair_shape = shape_of((4, tp_size, width // 8, 2 * head_cols))
    first_grads = call(
        first_grads_kernel,
        (tp_size,),
        [
            mine,
            by_step((rows, head_cols)),
            whole((rows, width)),
            pl.BlockSpec((1, 1, rows // 2, 2 * head_cols), lambda i, scal: (i, scal[2], 0, 0)),
        ],
        [pair_out] * 2,
        [pair_shape] * 2,
    )(scal, n1, dq, dh2_low, o_all)

    if direct:
        sum_qo = Sum(first_grads[0], over_ctx(first_grads[1], 1), True)
        (from_y,) = fence([from_y], sum_qo.first())
    from_y, y_own = fence([from_y, y_own])
    activations = lax.all_gather((h2 + y_own[0].astype(F32)).astype(BF16), "tp", axis=0)
    dkv = call(
        swing_kernel,
        (tp_size,),
        [kv_block] * 3 + [whole((rows, packed))] * 2,
        kv_block,
        kv_shape,
        prefetch=0,
    )(e0, from_core_1, from_y, cos_table, sin_table)

    def by_group(shape):
        return pl.BlockSpec((1,) + shape, lambda i, *_: (i, 0, 0))

    gi, sums = call(
        end_kernel,
        (tp_size,),
        [by_group((rows, head_cols)), by_group((rows, 2 * head_cols))]
        + [by_group((packed // 4, width))] * 4
        + [whole((rows, width)), mine, whole((16, width)), whole((16, width))],
        [whole((rows, width)), whole((16, width))],
        [shape_of((rows, width)), shape_of((16, width), F32)],
        [pltpu.VMEM((packed, width), BF16), pltpu.VMEM((rows, width), F32)],
    )(scal, dq, dkv, *w_pieces, dh2, layer_input, small, sums)
    dkv_late, n1_late, sums, gi = fence([dkv, n1, sums, gi])
    if direct:
        dkv_late, sums_of[1].last = fence([dkv_late, sums_of[1].last])
    gi_all = lax.all_gather(gi, "tp", axis=0)
    last_shape = shape_of((4, tp_size + 1, width // 8, 2 * head_cols))
    second_grads = call(
        second_grads_kernel,
        (tp_size + 1,),
        [
            mine,
            pl.BlockSpec((1, rows, 2 * head_cols), lambda i, *_: (jnp.minimum(i, tp_size - 1), 0, 0)),
            whole((16, width)),
        ],
        [pair_out] * 2,
        [last_shape] * 2,
    )(scal, n1_late, dkv_late, sums)

    if direct:
        sum_kv = Sum(second_grads[0], over_ctx(second_grads[1], 1), False)
        (sums_of[3].far,) = fence([sums_of[3].far], *second_grads)
        sum_kv.fence(sums_of[3].far)
        (sums_of[2].far,) = fence([sums_of[2].far], sum_kv.first())
        (sum_qo.far,) = fence([sum_qo.far], sums_of[2].second(), sums_of[3].second())
        away = sum_qo.second()
        early = (1, 0)
        flat = fence([sums_of[index].last for index in early], away)
        for index, value in zip(early, flat):
            sums_of[index].last = value
        results = [sums_of[index].result() for index in (0, 1)]
        (sum_kv.far,) = fence([sum_kv.far], *results)
        away = sum_kv.second()
        (sums_of[3].last,) = fence([sums_of[3].last], away)
        shared_result = sums_of[3].result()
        (sums_of[2].last,) = fence([sums_of[2].last], away)
        results += [sums_of[2].result(), shared_result]
        sum_kv.last, sum_qo.last = fence([sum_kv.last, sum_qo.last], *results)
        grads_qo, grads_kv = sum_qo.result(), sum_kv.result()
    else:
        grads_qo, grads_kv = scatter_plain(*first_grads), scatter_plain(*second_grads)
        results = [scatter_plain(*expert_group), scatter_plain(*shared_group)]
    grads_all = jnp.concatenate(
        [grads_qo, grads_kv[:tp_size], jnp.broadcast_to(grads_kv[tp_size:, :, :128], (tp_size, part, 128))], axis=-1
    )
    grads_all, gi_all = fence([grads_all.astype(BF16), gi_all])
    grads_all = jnp.sum(lax.all_to_all(grads_all, "tp", 0, 0, tiled=True).astype(F32), 0)
    grads_qo, grads_kv = grads_all[:, :2 * head_cols], grads_all[:, 2 * head_cols:4 * head_cols]
    sums = jnp.transpose(grads_all[:, 4 * head_cols:4 * head_cols + 16])
    grad_input = gi_all.astype(F32)
    results = [value.reshape(value.shape[0], 3, part, hidden) for value in results]
    grads_shared = results[-1][0]
    results = results[:-1]
    grads_exp = [jnp.concatenate([value[:, i] for value in results], axis=0) for i in range(3)]

    return (
        activations.reshape(layer_input.shape),
        grad_input.reshape(layer_input.shape),
        sums[8],
        grads_qo[:, :head_cols],
        grads_kv[:, :head_cols],
        grads_kv[:, head_cols:],
        jnp.transpose(grads_qo[:, head_cols:]),
        sums[9],
        jnp.transpose(sums[0:8]),
        grads_exp[0],
        grads_exp[1],
        jnp.transpose(grads_exp[2], (0, 2, 1)),
        grads_shared[0],
        grads_shared[1],
        jnp.transpose(grads_shared[2]),
    )


def solution(mesh):
    placed = (
        P("fsdp", "ctx", None),
        P("fsdp"),
        P("fsdp", "tp"),
        P("fsdp", "tp"),
        P("fsdp", "tp"),
        P("tp", "fsdp"),
        P("fsdp"),
        P("fsdp", None),
        P(None, "fsdp", "tp"),
        P(None, "fsdp", "tp"),
        P(None, "tp", "fsdp"),
        P("fsdp", "tp"),
        P("fsdp", "tp"),
        P("tp", "fsdp"),
        P("fsdp", "ctx", None),
        P("fsdp"),
        P("fsdp", "ctx", None),
    )
    return jax.shard_map(
        functools.partial(body, mesh.shape["fsdp"]),
        mesh=mesh,
        in_specs=placed,
        out_specs=(
            P("fsdp", "ctx", None),
            P("fsdp", "ctx", None),
            P(("fsdp", "ctx")),
            P(("fsdp", "ctx"), "tp"),
            P(("fsdp", "ctx"), "tp"),
            P(("fsdp", "ctx"), "tp"),
            P("tp", ("fsdp", "ctx")),
            P(("fsdp", "ctx")),
            P(("fsdp", "ctx"), None),
            P(None, ("fsdp", "ctx"), "tp"),
            P(None, ("fsdp", "ctx"), "tp"),
            P(None, "tp", ("fsdp", "ctx")),
            P(("fsdp", "ctx"), "tp"),
            P(("fsdp", "ctx"), "tp"),
            P("tp", ("fsdp", "ctx")),
        ),
        check_vma=False,
    )
```

```python
import functools
import math

import jax
import jax.numpy as jnp
from jax import lax
from jax.experimental import pallas as pl
from jax.experimental.pallas import tpu as pltpu
from jax.sharding import PartitionSpec as P

HD = 64
SLOTS = 80
EPS = 1e-06
F32 = jnp.float32
BF16 = jnp.bfloat16
VMEM_BYTES = 56 * 1024 * 1024


def mm(a, b):
    return lax.dot_general(a, b, (((1,), (0,)), ((), ())), preferred_element_type=F32)


def mm_nt(a, b):
    return lax.dot_general(a, b, (((1,), (1,)), ((), ())), preferred_element_type=F32)


def mm_tn(a, b):
    return lax.dot_general(a, b, (((0,), (0,)), ((), ())), preferred_element_type=F32)


def params(steps=1):
    return pltpu.CompilerParams(
        dimension_semantics=("arbitrary",) * steps, vmem_limit_bytes=VMEM_BYTES
    )


def rotation(width):
    row = lax.broadcasted_iota(jnp.int32, (width, width), 0)
    col = lax.broadcasted_iota(jnp.int32, (width, width), 1)
    first = (col % HD) < HD // 2
    minus = first & (row == col + HD // 2)
    plus = jnp.logical_not(first) & (row == col - HD // 2)
    return jnp.where(minus, -1.0, jnp.where(plus, 1.0, 0.0)).astype(BF16)


def row_scale(value):
    return lax.rsqrt(jnp.mean(value * value, -1, keepdims=True) + EPS)


def qkv_kernel(scal, x_ref, own_ref, oth_ref, cos_ref, sin_ref, n1_ref, q_ref, kv_ref, all_ref, w_ref, small_ref, swap):
    half = own_ref.shape[1]
    packed = w_ref.shape[0]

    @pl.when(pl.program_id(0) == 0)
    def _():
        mine = pl.multiple_of(scal[0] * half, half)
        other = pl.multiple_of((1 - scal[0]) * half, half)
        w_ref[:, pl.ds(mine, half)] = own_ref[:packed, :]
        w_ref[:, pl.ds(other, half)] = oth_ref[:packed, :]
        swap[...] = mm_tn(rotation(packed), w_ref[...]).astype(BF16)
        small_ref[...] = w_ref[192:208, :].astype(F32)

    x = x_ref[0].astype(F32)
    n1 = (x * row_scale(x) * small_ref[8:9, :]).astype(BF16)
    n1_ref[0] = n1
    turned = (mm_nt(n1, w_ref[...]) * cos_ref[...] + mm_nt(n1, swap[...]) * sin_ref[...]).astype(BF16)
    q_ref[0] = turned[:, :192]
    kv_ref[0] = turned[:, 256:640]
    all_ref[0] = turned


def visible(scal, prefix, keys, rows):
    key_pos = lax.broadcasted_iota(jnp.int32, (keys, rows), 0) ^ (scal[1] * rows)
    row_pos = lax.broadcasted_iota(jnp.int32, (keys, rows), 1) + scal[1] * rows
    return (key_pos <= row_pos) | (key_pos < prefix)


def only_head(rows, head):
    lane = lax.broadcasted_iota(jnp.int32, rows.shape, 1)
    return jnp.where((lane >= head * HD) & (lane < (head + 1) * HD), rows, jnp.zeros_like(rows))


def softmax(scores, seen):
    scores = jnp.where(seen, scores, -1e30)
    expo = jnp.exp(scores - jnp.max(scores, 0, keepdims=True))
    return expo, 1.0 / jnp.sum(expo, 0, keepdims=True)


def attn_fwd_kernel(scal, prefix, q_ref, kv0, kv1, kv2, kv3, o_ref):
    q = q_ref[0]
    rows, width = q.shape
    heads = width // HD
    kv = jnp.concatenate([kv0[0], kv1[0], kv2[0], kv3[0]], axis=0)
    k = kv[:, :width]
    value_t = jnp.transpose(kv[:, width:].astype(F32)).astype(BF16)
    seen = visible(scal, prefix[pl.program_id(0)], kv.shape[0], rows)
    outs = []
    for head in range(heads):
        expo, factor = softmax(mm_nt(k, only_head(q, head) * (HD ** -0.5)), seen)
        outs.append(mm(value_t[head * HD:(head + 1) * HD], expo.astype(BF16)) * factor)
    o = jnp.transpose(jnp.concatenate(outs, axis=0))
    o_ref[0] = jnp.concatenate([o[: rows // 2], o[rows // 2:]], axis=1).astype(BF16)


def fill_out_weights(scal, wo, wo_ref):
    pieces, _, width, half = wo_ref.shape
    for piece in range(pieces):
        for index, side in enumerate((scal[0], 1 - scal[0])):
            at = pl.ds(pl.multiple_of(side * half, half), half)
            wo[piece * width:(piece + 1) * width, at] = wo_ref[piece, index]


def post_kernel(scal, o_ref, wo_ref, x_ref, small_ref, routes_ref, n2_ref, h2_ref, gates_ref, slots_ref, wo):
    step = pl.program_id(0)
    width = wo_ref.shape[2]

    @pl.when(step == 0)
    def _():
        fill_out_weights(scal, wo, wo_ref)

    low = jnp.zeros((o_ref.shape[2], wo.shape[1]), F32)
    high = low
    for piece in range(o_ref.shape[0]):
        block = o_ref[piece, 0]
        weights = wo[piece * width:(piece + 1) * width, :]
        low += mm(block[:, :width], weights)
        high += mm(block[:, width:], weights)
    h2 = x_ref[0].astype(F32) + jnp.concatenate([low, high], axis=0)
    n2 = (h2 * row_scale(h2) * small_ref[9:10, :]).astype(BF16)
    n2_ref[0] = n2

    @pl.when(step == scal[2])
    def _():
        h2_ref[...] = h2

    expo = jnp.exp(mm_nt(small_ref[0:8, :].astype(BF16), n2))
    gates_ref[0] = expo / jnp.sum(expo, 0, keepdims=True)
    rows = n2.shape[0]
    expert = lax.broadcasted_iota(jnp.int32, (8, rows), 0)
    named = (routes_ref[0, 0:1, :] == expert) | (routes_ref[0, 1:2, :] == expert)
    before = lax.broadcasted_iota(jnp.int32, (rows, rows), 0) < lax.broadcasted_iota(jnp.int32, (rows, rows), 1)
    place = mm(named.astype(BF16), before.astype(BF16))
    slots_ref[0] = jnp.where(named, place.astype(jnp.int32), -1)


def silu_parts(value):
    sigma = 0.5 * jnp.tanh(0.5 * value) + 0.5
    return sigma, value * sigma


def split_blocks(core, value, blocks):
    rows = value.shape[0] // (2 * blocks)
    value = value.astype(BF16).reshape(blocks, 2, rows, value.shape[1])
    first = core == 0
    return jnp.where(first, value[:, 0], value[:, 1]), jnp.where(first, value[:, 1], value[:, 0])


def put_grads(core, keep_ref, send_ref, index, value):
    keep, send = split_blocks(core, value, keep_ref.shape[0])
    at = slice(index * keep.shape[1], (index + 1) * keep.shape[1])
    keep_ref[:, 0, at, :] = keep
    send_ref[:, 0, at, :] = send


def shared_kernel(
    scal, n2_ref, dy_ref, go_ref, uo_ref, do_ref, g0, g1, g2, g3, u0, u1, u2, u3, d0, d1, d2, d3,
    ys_ref, dn_ref, hid_ref, dab_ref, wgu, wd,
):
    step = pl.program_id(0)
    half = go_ref.shape[0]
    hidden = go_ref.shape[1]

    @pl.when(step == 0)
    def _():
        mine = pl.multiple_of(scal[0] * half, half)
        other = (1 - scal[0]) * half
        wgu[pl.ds(mine, half), :hidden] = go_ref[...]
        wgu[pl.ds(mine, half), hidden:] = uo_ref[...]
        wd[:, pl.ds(mine, half)] = do_ref[...]
        for piece, (g, u, d) in enumerate(((g0, u0, d0), (g1, u1, d1), (g2, u2, d2), (g3, u3, d3))):
            quarter = scal[3] ^ piece
            at = pl.multiple_of(other + quarter * (half // 4), half // 4)
            wgu[pl.ds(at, half // 4), :hidden] = g[...]
            wgu[pl.ds(at, half // 4), hidden:] = u[...]
            at = pl.multiple_of(quarter * (hidden // 4), hidden // 4)
            wd[pl.ds(at, hidden // 4), pl.ds(pl.multiple_of(other, half), half)] = d[...]

    n2 = n2_ref[0]
    dy = dy_ref[0]
    both = mm(n2, wgu[...])
    gate, up = both[:, :hidden], both[:, hidden:]
    sigma, silu = silu_parts(gate)
    hid = (silu * up).astype(BF16)
    ys_ref[0] = mm(hid, wd[...]).astype(BF16)
    back = mm_nt(dy, wd[...])
    da = (back * up * (sigma * (1.0 + gate * (1.0 - sigma)))).astype(BF16)
    db = (back * silu).astype(BF16)
    dab = jnp.concatenate([da, db], axis=1)
    dn_ref[0] = mm_nt(dab, wgu[...]).astype(BF16)
    hid_ref[0] = hid
    dab_ref[0] = dab


def put_all_grads(core, keep_ref, send_ref, value, upstream, hid, dab):
    wide = mm_tn(value, dab)
    hidden = hid.shape[1]
    put_grads(core, keep_ref, send_ref, 0, wide[:, :hidden])
    put_grads(core, keep_ref, send_ref, 1, wide[:, hidden:])
    put_grads(core, keep_ref, send_ref, 2, mm_tn(upstream, hid))


def shared_grads_kernel(scal, n2_ref, dy_ref, hid_ref, dab_ref, keep_ref, send_ref):
    values = [ref[...].reshape(-1, ref.shape[-1]) for ref in (n2_ref, dy_ref, hid_ref, dab_ref)]
    put_all_grads(scal[4], keep_ref, send_ref, *values)


def moe_kernel(
    scal, n2_ref, dy_ref, slots_ref, gates_ref, ys_ref, dn_in_ref, gate_own, up_own, down_own,
    w0, w1, w2, w3, r0, r1, r2, r3, d0, d1, d2, d3,
    y_ref, dn_ref, keep_ref, send_ref, wgu_s, wd_s, sems, pick_s, ye_s, dx_s, xe_s, dy_s, de_s, gs_s, dprob_s,
):
    step = pl.program_id(0)
    seqs, rows, width = n2_ref.shape
    hidden, half = down_own.shape[1:]
    experts = slots_ref.shape[1]
    slot_now = step % 2
    mine = pl.multiple_of(scal[0] * half, half)
    other = pl.multiple_of((1 - scal[0]) * half, half)

    def expert_at(index):
        return 2 * ((index // 2) ^ scal[3]) + index % 2

    def place(slot, index):
        at = pl.ds(mine if index < 3 else other, half)
        if index % 3 == 2:
            return wd_s.at[slot, :, at]
        return wgu_s.at[slot, at, pl.ds(index % 3 * hidden, hidden)]

    def fetch(index):
        slot, piece, odd = index % 2, index // 2, index % 2

        def start(number, source):
            pltpu.make_async_copy(source, place(slot, number), sems.at[slot, number]).start()

        for number, ref in enumerate((gate_own, up_own, down_own)):
            start(number, ref.at[expert_at(index)])
        for number, (wide, rest, down) in enumerate(((w0, r0, d0), (w1, r1, d1), (w2, r2, d2), (w3, r3, d3))):
            @pl.when(piece == number)
            def _(wide=wide, rest=rest, down=down):
                start(3, wide.at[pl.ds(pl.multiple_of(odd * half, half), half), :])
                start(5, down.at[pl.ds(pl.multiple_of(odd * hidden, hidden), hidden), :])

                @pl.when(odd == 0)
                def _():
                    start(4, wide.at[pl.ds(2 * half, half), :])

                @pl.when(odd == 1)
                def _():
                    start(4, rest)

    @pl.when(step == 0)
    def _():
        fetch(step)

    @pl.when(step + 1 < experts)
    def _():
        fetch(step + 1)

    @pl.when(step < experts)
    def _():
        expert = expert_at(step)
        for number in range(6):
            source = down_own.at[0] if number % 3 == 2 else gate_own.at[0]
            pltpu.make_async_copy(source, place(slot_now, number), sems.at[slot_now, number]).wait()
        wgu, wd = wgu_s.at[slot_now], wd_s.at[slot_now]

        slot_at = pl.ds(pl.multiple_of(step * SLOTS, 16), SLOTS)
        slot = lax.broadcasted_iota(jnp.int32, (SLOTS, rows), 0)
        for s in range(seqs):
            at = slice(s * SLOTS, (s + 1) * SLOTS)
            hit = slots_ref[s, pl.ds(expert, 1), :] == slot
            gate_slot = jnp.sum(jnp.where(hit, gates_ref[s, pl.ds(expert, 1), :], 0.0), 1, keepdims=True)
            pick = hit.astype(BF16)
            pick_s[s, slot_at, :] = pick
            xe_s[at, :] = mm(pick, n2_ref[s]).astype(BF16)
            upstream = mm(pick, dy_ref[s])
            dy_s[at, :] = upstream.astype(BF16)
            de_s[at, :] = (gate_slot * upstream).astype(BF16)
            gs_s[at, :] = jnp.broadcast_to(gate_slot, (SLOTS, 128))

        xe = xe_s[...]
        both = mm(xe, wgu[...])
        gate, up = both[:, :hidden], both[:, hidden:]
        sigma, silu = silu_parts(gate)
        hid = (silu * up).astype(BF16)
        ye = mm(hid, wd[...])
        dots = jnp.sum(ye * dy_s[...].astype(F32), 1, keepdims=True)
        ye = (ye * gs_s[:, 0:1]).astype(BF16)
        for s in range(seqs):
            at = slice(s * SLOTS, (s + 1) * SLOTS)
            ye_s[s, slot_at, :] = ye[at]
            hit = slots_ref[s, pl.ds(expert, 1), :] == slot
            dprob_s[s, pl.ds(expert, 1), :] = jnp.sum(jnp.where(hit, dots[at], 0.0), 0, keepdims=True)
        back = mm_nt(de_s[...], wd[...])
        da = (back * up * (sigma * (1.0 + gate * (1.0 - sigma)))).astype(BF16)
        db = (back * silu).astype(BF16)
        dab = jnp.concatenate([da, db], axis=1)
        dx = mm_nt(dab, wgu[...]).astype(BF16)
        for s in range(seqs):
            dx_s[s, slot_at, :] = dx[s * SLOTS:(s + 1) * SLOTS]
        put_all_grads(scal[4], keep_ref, send_ref, xe, de_s[...], hid, dab)

    @pl.when(step >= experts)
    def _():
        s = step - experts
        pick = pick_s[s]
        y_ref[0] = (ys_ref[0].astype(F32) + mm_tn(pick, ye_s[s])).astype(BF16)
        dn_ref[0, 0:rows, :] = (dn_in_ref[0].astype(F32) + mm_tn(pick, dx_s[s])).astype(BF16)
        tail = jnp.concatenate([dprob_s[s], jnp.zeros((dn_ref.shape[1] - rows - experts, rows), F32)], axis=0)
        tail = jnp.concatenate([tail, jnp.zeros((tail.shape[0], width - rows), F32)], axis=1)
        dn_ref[0, rows:, :] = tail.astype(BF16)


def norm_back(grad_out, value, scale, gain):
    weighted = grad_out * gain
    return scale * weighted - value * (scale * scale * scale) * jnp.mean(weighted * value, -1, keepdims=True)


def mid_kernel(scal, dn_ref, gates_ref, h2_ref, n2_ref, dy_ref, small_ref, wo_ref, dh2_ref, do_ref, low_ref, sums_ref, wo):
    rows = h2_ref.shape[0]
    pieces, _, width, _ = wo_ref.shape
    fill_out_weights(scal, wo, wo_ref)
    parts = dn_ref[0].astype(F32)
    gates = gates_ref[0]
    dprob = parts[rows:rows + 8, 0:rows]
    dlogits = (gates * (dprob - jnp.sum(dprob * gates, 0, keepdims=True))).astype(BF16)
    dn2 = parts[0:rows, :] + mm_tn(dlogits, small_ref[0:8, :].astype(BF16))
    h2 = h2_ref[...]
    scale = row_scale(h2)
    sums_ref[0:8, :] = mm(dlogits, n2_ref[0])
    sums_ref[8:16, :] = jnp.zeros((8, h2.shape[1]), F32)
    sums_ref[9:10, :] = jnp.sum(dn2 * h2 * scale, 0, keepdims=True)
    dh2 = dy_ref[0].astype(F32) + norm_back(dn2, h2, scale, small_ref[9:10, :])
    dh2_ref[...] = dh2
    low = dh2.astype(BF16)
    low_ref[...] = low
    for piece in range(pieces):
        do = mm_nt(low, wo[piece * width:(piece + 1) * width, :])
        do_ref[piece] = jnp.concatenate([do[: rows // 2], do[rows // 2:]], axis=1).astype(BF16)


def attn_bwd_kernel(
    scal, prefix, q_ref, kv0, kv1, kv2, kv3, do_ref, cos_ref, sin_ref, dq_ref, e0, e1, e2, e3
):
    rows, width = dq_ref.shape[1:]
    q = q_ref[0][:, :width]
    heads = width // HD
    kv = jnp.concatenate([kv0[0], kv1[0], kv2[0], kv3[0]], axis=0)
    k = kv[:, :width]
    v = kv[:, width:]
    key_t = jnp.transpose(k.astype(F32)).astype(BF16)
    do = jnp.concatenate([do_ref[0][:, :width], do_ref[0][:, width:]], axis=0)
    seen = visible(scal, prefix[scal[2]], kv.shape[0], rows)
    cosine, sine = cos_ref[...], sin_ref[...]
    turned, ds_all, probs_all, q_all, do_all = [], [], [], [], []
    for head in range(heads):
        q_head = only_head(q, head) * (HD ** -0.5)
        do_head = only_head(do, head)
        expo, factor = softmax(mm_nt(k, q_head), seen)
        probs = expo * factor
        dp = mm_nt(v, do_head)
        ds = (probs * (dp - jnp.sum(dp * probs, 0, keepdims=True))).astype(BF16)
        dq = mm(key_t[head * HD:(head + 1) * HD], ds) * (HD ** -0.5)
        first, second = dq[: HD // 2], dq[HD // 2:]
        turned += [first * cosine + second * sine, second * cosine - first * sine]
        ds_all.append(ds)
        probs_all.append(probs.astype(BF16))
        q_all.append(q_head)
        do_all.append(do_head)
    dq_ref[0] = jnp.transpose(jnp.concatenate(turned, axis=0)).astype(BF16)
    dk = mm(jnp.concatenate(ds_all, axis=1), jnp.concatenate(q_all, axis=0))
    dv = mm(jnp.concatenate(probs_all, axis=1), jnp.concatenate(do_all, axis=0))
    dkv = jnp.concatenate([dk, dv], axis=1).astype(BF16)
    for piece, out in enumerate((e0, e1, e2, e3)):
        out[0] = dkv[piece * rows:(piece + 1) * rows]


def swing_kernel(a_ref, b_ref, c_ref, cos_ref, sin_ref, out_ref):
    dkv = a_ref[0].astype(F32) + b_ref[0].astype(F32) + c_ref[0].astype(F32)
    swung = dkv * sin_ref[:, 256:]
    high = swung.astype(BF16)
    low = (swung - high.astype(F32)).astype(BF16)
    turn = rotation(dkv.shape[1])
    out_ref[0] = (dkv * cos_ref[:, 256:] + mm_nt(high, turn) + mm_nt(low, turn)).astype(BF16)


def end_kernel(scal, dq_ref, dkv_ref, w0, w1, w2, w3, dh2_ref, x_ref, small_ref, sums_in, gi_ref, sums_ref, w, total):
    step = pl.program_id(0)
    head_cols = dq_ref.shape[2]
    quarter = w.shape[0] // 4
    for piece, ref in enumerate((w0, w1, w2, w3)):
        at = pl.multiple_of((scal[1] ^ piece) * quarter, quarter)
        w[pl.ds(at, quarter), :] = ref[0]
    part = mm(dq_ref[0], w[:head_cols, :]) + mm(dkv_ref[0], w[256:, :])

    @pl.when(step == 0)
    def _():
        total[...] = part

    @pl.when(step > 0)
    def _():
        total[...] += part

    @pl.when(step == pl.num_programs(0) - 1)
    def _():
        x = x_ref[0].astype(F32)
        dn1 = total[...]
        scale = row_scale(x)
        sums_ref[...] = sums_in[...]
        sums_ref[8:9, :] = jnp.sum(dn1 * x * scale, 0, keepdims=True)
        gi_ref[...] = (dh2_ref[...] + norm_back(dn1, x, scale, small_ref[8:9, :])).astype(BF16)


def first_grads_kernel(scal, n1_ref, dq_ref, low_ref, o_ref, keep_ref, send_ref):
    head_cols = dq_ref.shape[2]
    block = o_ref[0, 0]
    o = jnp.concatenate([block[:, :head_cols], block[:, head_cols:]], axis=0)
    grads = jnp.concatenate([mm_tn(n1_ref[0], dq_ref[0]), mm_tn(low_ref[...], o)], axis=1)
    keep_ref[:, 0], send_ref[:, 0] = split_blocks(scal[4], grads, keep_ref.shape[0])


def second_grads_kernel(scal, n1_ref, dkv_ref, sums_ref, keep_ref, send_ref):
    step = pl.program_id(0)
    last = pl.num_programs(0) - 1

    @pl.when(step < last)
    def _():
        keep_ref[:, 0], send_ref[:, 0] = split_blocks(scal[4], mm_tn(n1_ref[0], dkv_ref[0]), keep_ref.shape[0])

    @pl.when(step == last)
    def _():
        sums = sums_ref[...]
        sums = jnp.concatenate([sums, jnp.zeros((keep_ref.shape[3] - sums.shape[0], sums.shape[1]), F32)], axis=0)
        keep_ref[:, 0], send_ref[:, 0] = split_blocks(scal[4], jnp.transpose(sums), keep_ref.shape[0])


def whole(shape):
    return pl.BlockSpec(shape, lambda *_: (0,) * len(shape))


def by_step(shape):
    return pl.BlockSpec((1,) + shape, lambda i, *_: (i,) + (0,) * len(shape))


def call(kernel, grid, in_specs, out_specs, out_shape, scratch=(), prefetch=1, aliases=None):
    return pl.pallas_call(
        kernel,
        grid_spec=pltpu.PrefetchScalarGridSpec(
            num_scalar_prefetch=prefetch,
            grid=grid,
            in_specs=in_specs,
            out_specs=out_specs,
            scratch_shapes=scratch,
        ),
        out_shape=out_shape,
        input_output_aliases=aliases or {},
        compiler_params=params(len(grid)),
        cost_estimate=pl.CostEstimate(flops=1, bytes_accessed=1, transcendentals=0),
    )


def fence(values, *others):
    values = list(values)
    return list(lax.optimization_barrier((*values, *others))[: len(values)])


def shape_of(shape, dtype=BF16):
    return jax.ShapeDtypeStruct(shape, dtype)


def body(
    fsdp_size,
    layer_input,
    gain_attn,
    query_weight,
    key_weight,
    value_weight,
    output_weight,
    gain_ffn,
    router,
    exp_gate,
    exp_up,
    exp_down,
    shared_gate_weight,
    shared_up_weight,
    shared_down_weight,
    routes,
    prefix,
    cotangent,
):
    seqs, rows, width = layer_input.shape
    experts = exp_gate.shape[0]
    hidden = exp_gate.shape[2]
    head_cols = query_weight.shape[1]
    half = width // 2
    paired = fsdp_size == 2
    ctx = lax.axis_index("ctx")
    tp = lax.axis_index("tp")
    ctx_size = lax.axis_size("ctx")
    tp_size = lax.axis_size("tp")
    side = lax.axis_index("fsdp") if paired else jnp.int32(0)
    weight_ctx = ctx if paired else jnp.int32(0)
    blocks = fsdp_size * ctx_size
    direct = paired and ctx_size == 4 and tp_size == 4
    core = ctx % 2 if direct else jnp.int32(0)
    scal = jnp.stack([side, ctx, tp, weight_ctx, core]).astype(jnp.int32)

    def over_x(value):
        return lax.ppermute(value, "fsdp", [(0, 1), (1, 0)])

    def over_tp(value, bit):
        return lax.ppermute(value, "tp", [(i, i ^ bit) for i in range(tp_size)])

    def over_ctx(value, bit):
        return lax.ppermute(value, "ctx", [(i, i ^ bit) for i in range(ctx_size)])

    columns = jnp.concatenate(
        [
            query_weight.T,
            router.T,
            gain_attn[None],
            gain_ffn[None],
            jnp.zeros((54, query_weight.shape[0]), BF16),
            key_weight.T,
            value_weight.T,
            output_weight,
        ],
        axis=0,
    )
    if paired:
        columns_own, columns_other = columns, over_x(columns)
    else:
        columns = lax.all_gather(columns, "fsdp", axis=1, tiled=True)
        columns_own, columns_other = columns[:, :half], columns[:, half:]

    shared_own = (shared_gate_weight, shared_up_weight, shared_down_weight)
    experts_own = (exp_gate, exp_up, exp_down)
    if paired:

        def quarter(value, parts):
            size = value.shape[0] // parts
            return lax.dynamic_slice_in_dim(value, size * ctx, size, 0).reshape(-1, value.shape[-1])

        gate, up, down = [quarter(stack, 4) for stack in experts_own]
        shared_gate, shared_up, shared_down = [quarter(stack, 4) for stack in shared_own]
        wide = jnp.concatenate([gate, up[:half], shared_gate, shared_up], axis=0)
        rest = up[half:]
        down = jnp.concatenate([down, shared_down], axis=0)
        own = experts_own + shared_own
    else:
        gate_all = lax.all_gather(exp_gate, "fsdp", axis=1, tiled=True)
        up_all = lax.all_gather(exp_up, "fsdp", axis=1, tiled=True)
        down_all = lax.all_gather(exp_down, "fsdp", axis=2, tiled=True)
        sg_all = lax.all_gather(shared_gate_weight, "fsdp", axis=0, tiled=True)
        su_all = lax.all_gather(shared_up_weight, "fsdp", axis=0, tiled=True)
        sd_all = lax.all_gather(shared_down_weight, "fsdp", axis=1, tiled=True)
        own = (gate_all[:, :half], up_all[:, :half], down_all[:, :, :half], sg_all[:half], su_all[:half], sd_all[:, :half])

        def split(value):
            return value.reshape((4, value.shape[0] // 4) + value.shape[1:])

        gate_all, up_all, sg_all, su_all = [
            split(value) for value in (gate_all[:, half:], up_all[:, half:], sg_all[half:], su_all[half:])
        ]
        down_all, sd_all = split(down_all[:, :, half:]), split(sd_all[:, half:])
        wide_p = [
            jnp.concatenate([gate_all[p, 0], gate_all[p, 1], up_all[p, 0], sg_all[p], su_all[p]], axis=0) for p in range(4)
        ]
        rest_p = [up_all[p, 1] for p in range(4)]
        down_p = [jnp.concatenate([down_all[p, 0], down_all[p, 1], sd_all[p]], axis=0) for p in range(4)]

    positions = (ctx * rows + jnp.arange(rows, dtype=jnp.int32)).astype(F32)
    inverse = jnp.exp(jnp.arange(HD // 2, dtype=F32) * (-math.log(10000.0) / (HD // 2)))
    angles = positions[:, None] * inverse[None, :]
    cosine, sine = jnp.cos(angles), jnp.sin(angles)
    heads = head_cols // HD

    def table(value, rest):
        turned = jnp.tile(value, (1, 2 * heads))
        plain = jnp.full((rows, head_cols), rest, F32)
        return jnp.concatenate([turned, plain[:, :64], turned, plain], axis=1)

    cos_table, sin_table = table(cosine, 1.0), table(sine, 0.0)
    routes_t = jnp.pad(jnp.transpose(routes, (0, 2, 1)), ((0, 0), (0, 6), (0, 0)))

    cos_t, sin_t = jnp.transpose(cosine), jnp.transpose(sine)
    columns_other, cos_table, sin_table, cos_t, sin_t = fence([columns_other, cos_table, sin_table, cos_t, sin_t], routes_t)
    if paired:
        columns_other, cos_table, wide, rest, down = fence([columns_other, cos_table, wide, rest, down])
        wide_0 = over_x(wide)
    out_pieces = jnp.stack([columns_own[-head_cols:], columns_other[-head_cols:]])
    out_pieces = lax.all_gather(out_pieces, "tp", axis=0)
    packed = cos_table.shape[1]

    n1, q, kv, qkv, w_qkv, small = call(
        qkv_kernel,
        (seqs,),
        [
            by_step((rows, width)),
            whole((packed + head_cols, half)),
            whole((packed + head_cols, half)),
            whole((rows, packed)),
            whole((rows, packed)),
        ],
        [
            by_step((rows, width)),
            by_step((rows, head_cols)),
            by_step((rows, 2 * head_cols)),
            by_step((rows, packed)),
            whole((packed, width)),
            whole((16, width)),
        ],
        [
            shape_of((seqs, rows, width)),
            shape_of((seqs, rows, head_cols)),
            shape_of((seqs, rows, 2 * head_cols)),
            shape_of((seqs, rows, packed)),
            shape_of((packed, width)),
            shape_of((16, width), F32),
        ],
        [pltpu.VMEM((packed, width), BF16)],
    )(scal, layer_input, columns_own, columns_other, cos_table, sin_table)

    kv_0 = kv
    kv_2 = over_ctx(kv_0, 2)
    kv_1 = over_ctx(kv_0, 1)
    q_now, kv_2 = fence([q, kv_2], kv_1)
    w_part = lax.dynamic_slice_in_dim(w_qkv, (packed // 4) * ctx, packed // 4, 0)
    w_part = jnp.pad(w_part, ((0, 16), (0, 0)))
    if paired:
        kv_2, wide_0, rest, down, w_part = fence([kv_2, wide_0, rest, down, w_part])
        wide_2 = over_ctx(wide_0, 2)
        rest_0 = over_x(rest)
        (down,) = fence([down], rest)
        down_0 = over_x(down)
    kv_3 = over_ctx(kv_2, 1)
    q_now, kv_3, out_pieces = fence([q_now, kv_3, out_pieces])

    o = call(
        attn_fwd_kernel,
        (seqs,),
        [by_step((rows, head_cols))] + [by_step((rows, 2 * head_cols))] * 4,
        by_step((rows // 2, 2 * head_cols)),
        shape_of((seqs, rows // 2, 2 * head_cols)),
        prefetch=2,
    )(scal, prefix, q_now, kv_0, kv_1, kv_2, kv_3)

    o_all = lax.all_gather(o, "tp", axis=0)
    if paired:
        wide_0, rest_0 = fence([wide_0, rest_0], o)
        rest_2, rest_1, wide_1 = over_ctx(rest_0, 2), over_ctx(rest_0, 1), over_ctx(wide_0, 1)
        down_0, wide_2, rest_1, wide_1 = fence([down_0, wide_2, rest_1, wide_1])
        down_2, down_1, wide_3 = over_ctx(down_0, 2), over_ctx(down_0, 1), over_ctx(wide_2, 1)
        (rest_2,) = fence([rest_2], down_0, wide_2)
        down_1, wide_3 = fence([down_1, wide_3], rest_2)
        rest_3 = over_ctx(rest_2, 1)
        o_all, down_1, wide_3 = fence([o_all, down_1, wide_3])
    w_0 = lax.all_gather(fence([w_part], o_all)[0], "tp", axis=0)
    n2, h2, gates, slots = call(
        post_kernel,
        (seqs,),
        [
            pl.BlockSpec((tp_size, 1, rows // 2, 2 * head_cols), lambda i, *_: (0, i, 0, 0)),
            whole((tp_size, 2, head_cols, half)),
            by_step((rows, width)),
            whole((16, width)),
            by_step((8, rows)),
        ],
        [by_step((rows, width)), whole((rows, width)), by_step((8, rows)), by_step((8, rows))],
        [
            shape_of((seqs, rows, width)),
            shape_of((rows, width), F32),
            shape_of((seqs, 8, rows), F32),
            shape_of((seqs, 8, rows), jnp.int32),
        ],
        [pltpu.VMEM((width, width), BF16)],
    )(scal, o_all, out_pieces, layer_input, small, routes_t)

    if paired:
        down_2, rest_3 = fence([down_2, rest_3], n2)
        down_3 = over_ctx(down_2, 1)
        wide_p = (wide_0, wide_1, wide_2, wide_3)
        rest_p = (rest_0, rest_1, rest_2, rest_3)
        down_p = (down_0, down_1, down_2, down_3)

    full = pl.BlockSpec((seqs, rows, width), lambda *_: (0, 0, 0), pipeline_mode=pl.Buffered(1))
    part_rows = 3 * (width // 8)
    upper = [pl.BlockSpec((half // 4, hidden), lambda *_, at=at: (at, 0)) for at in (12, 13)]
    lower = pl.BlockSpec((hidden // 4, half), lambda *_: (8, 0))
    weights = [pltpu.VMEM((width, 2 * hidden), BF16), pltpu.VMEM((hidden, width), BF16)]
    ys, dn_shared, *shared_hidden = call(
        shared_kernel,
        (seqs,),
        [by_step((rows, width))] * 2
        + [whole((half, hidden)), whole((half, hidden)), whole((hidden, half))]
        + [upper[0]] * 4
        + [upper[1]] * 4
        + [lower] * 4,
        [by_step((rows, width))] * 2 + [by_step((rows, hidden)), by_step((rows, 2 * hidden))],
        [shape_of((seqs, rows, width))] * 2 + [shape_of((seqs, rows, hidden)), shape_of((seqs, rows, 2 * hidden))],
        weights,
    )(scal, n2, cotangent, *own[3:], *wide_p, *wide_p, *down_p)

    qkv_late, w_0, ys = fence([qkv, w_0, ys])
    qkv_seq = lax.all_to_all(qkv_late, "tp", 0, 0, tiled=True)
    w_2, w_1 = over_ctx(w_0, 2), over_ctx(w_0, 1)

    def expert_of(i, scal):
        i = jnp.minimum(i, experts - 1)
        return 2 * ((i // 2) ^ scal[3]) + i % 2

    late = pl.BlockSpec((1, rows, width), lambda i, scal: (jnp.maximum(i - experts, 0), 0, 0))

    dn_rows = rows + 16
    slot_rows = seqs * SLOTS
    block = (4, 1, part_rows, hidden)

    expert_grads = pl.BlockSpec(block, lambda i, scal: (0, expert_of(i, scal), 0, 0))
    y, dn, *expert_group = call(
        moe_kernel,
        (experts + seqs,),
        [full, full, whole((seqs, 8, rows)), whole((seqs, 8, rows)), late, late]
        + [pl.BlockSpec(memory_space=pl.ANY)] * 15,
        [late, pl.BlockSpec((1, dn_rows, width), lambda i, *_: (jnp.maximum(i - experts, 0), 0, 0))]
        + [expert_grads] * 2,
        [shape_of((seqs, rows, width)), shape_of((seqs, dn_rows, width))]
        + [shape_of((4, experts, part_rows, hidden))] * 2,
        [pltpu.VMEM((2, width, 2 * hidden), BF16), pltpu.VMEM((2, hidden, width), BF16)]
        + [pltpu.SemaphoreType.DMA((2, 6))]
        + [pltpu.VMEM((seqs, experts * SLOTS, rows), BF16)]
        + [pltpu.VMEM((seqs, experts * SLOTS, width), BF16)] * 2
        + [pltpu.VMEM((slot_rows, width), BF16)] * 3
        + [pltpu.VMEM((slot_rows, 128), F32), pltpu.VMEM((seqs, 8, rows), F32)],
    )(scal, n2, cotangent, slots, gates, ys, dn_shared, *own[:3], *wide_p, *rest_p, *down_p)

    dn, qkv_seq, w_2, w_1, n2_late, *expert_group = fence([dn, qkv_seq, w_2, w_1, n2, *expert_group])
    w_pieces = (w_0, w_1, w_2, over_ctx(w_2, 1))
    dn_own = lax.psum_scatter(dn, "tp", scatter_dimension=0, tiled=True)
    kv_seq = qkv_seq[:, :, 256:]
    kv_seq_2, kv_seq_1 = over_ctx(kv_seq, 2), over_ctx(kv_seq, 1)

    shared_group = call(
        shared_grads_kernel,
        (1,),
        [full] * 2 + [whole((seqs, rows, hidden)), whole((seqs, rows, 2 * hidden))],
        [whole(block)] * 2,
        [shape_of(block)] * 2,
    )(scal, n2_late, cotangent, *shared_hidden)

    part = width // blocks
    along_x, along_y = side, ctx // 2

    def pick(value, x, y, first, count):
        value = value.reshape((2, 2) + value.shape[1:])
        sizes = (2 if x is None else 1, 2 if y is None else 1, count) + value.shape[3:]
        begin = (0 if x is None else x, 0 if y is None else y, first, 0, 0)
        value = lax.dynamic_slice(value, begin, sizes)
        value = value.reshape(tuple(n for n, at in zip(sizes[:2], (x, y)) if at is None) + sizes[2:])
        return value.astype(F32)

    def indexed(value, index):
        return lax.dynamic_index_in_dim(value, index, 0, False).astype(F32)

    class Sum:
        def __init__(self, keep, got, y_first, first=0, count=None):
            self.keep, self.got, self.y_first = keep, got, y_first
            self.range = (first, count or keep.shape[1])

        def fence(self, *others):
            (self.got,) = fence([self.got], *others)

        def both(self, x, y):
            return pick(self.keep, x, y, *self.range) + pick(self.got, x, y, *self.range)

        def first(self):
            if self.y_first:
                self.sent = self.both(None, 1 - along_y).astype(BF16)
            else:
                self.sent = self.both(1 - along_x, None).astype(BF16)
            self.far = over_ctx(self.sent, 2) if self.y_first else over_x(self.sent)
            return self.sent

        def second(self):
            if self.y_first:
                self.away = (self.both(1 - along_x, along_y) + indexed(self.far, 1 - along_x)).astype(BF16)
                self.last = over_x(self.away)
            else:
                self.away = (self.both(along_x, 1 - along_y) + indexed(self.far, 1 - along_y)).astype(BF16)
                self.last = over_ctx(self.away, 2)
            return self.away

        def result(self):
            mine = indexed(self.far, along_x if self.y_first else along_y)
            return self.both(along_x, along_y) + mine + self.last.astype(F32)

    def scatter_plain(keep, send):
        count, cols = keep.shape[1], keep.shape[3]
        triples = keep.shape[2] // (width // 8)
        both = jnp.stack([keep, send], axis=1).reshape(8, count, triples, width // 8, cols)
        both = jnp.transpose(both, (0, 3, 1, 2, 4)).reshape(blocks, part, count * triples, cols)
        both = jnp.transpose(both, (0, 2, 1, 3)).reshape(blocks, count * triples * part, cols)
        both = lax.psum_scatter(both, ("fsdp", "ctx"), scatter_dimension=0, tiled=True)
        return both.reshape(count, triples * part, cols).astype(F32)

    if direct:
        got, shared_got = over_ctx(expert_group[1], 1), over_ctx(shared_group[1], 1)
        cuts = ((0, 2, True), (2, 2, False), (4, 4, False))
        sums_of = [Sum(expert_group[0], got, y_first, first, count) for first, count, y_first in cuts]
        sums_of.append(Sum(shared_group[0], shared_got, True))
        sent = [sums_of[1].first(), sums_of[0].first()]
        sums_of[2].fence(*sent)
        sent.append(sums_of[2].first())
        (kv_seq_2,) = fence([kv_seq_2], *sent)
    kv_seq_3 = over_ctx(kv_seq_2, 1)
    if direct:
        sums_of[3].fence(*sent, kv_seq_2)
        kv_seq_1, kv_seq_3 = fence([kv_seq_1, kv_seq_3], sums_of[3].first())
    kv_seqs = (kv_seq, kv_seq_1, kv_seq_2, kv_seq_3)
    (dn_own,) = fence([dn_own], kv_seq_1, kv_seq_3)
    (y_late,) = fence([y], dn_own)
    y_own = lax.psum_scatter(y_late, "tp", scatter_dimension=0, tiled=True)

    mine = pl.BlockSpec((1, rows, width), lambda i, scal: (scal[2], 0, 0))
    dh2, do, dh2_low, sums = call(
        mid_kernel,
        (1,),
        [
            whole((1, dn_rows, width)),
            pl.BlockSpec((1, 8, rows), lambda i, scal: (scal[2], 0, 0)),
            whole((rows, width)),
            mine,
            mine,
            whole((16, width)),
            whole((tp_size, 2, head_cols, half)),
        ],
        [
            whole((rows, width)),
            whole((tp_size, rows // 2, 2 * head_cols)),
            whole((rows, width)),
            whole((16, width)),
        ],
        [
            shape_of((rows, width), F32),
            shape_of((tp_size, rows // 2, 2 * head_cols)),
            shape_of((rows, width)),
            shape_of((16, width), F32),
        ],
        [pltpu.VMEM((width, width), BF16)],
    )(scal, dn_own, gates, h2, n2, cotangent, small, out_pieces)

    kv_block = by_step((rows, 2 * head_cols))
    kv_shape = shape_of((tp_size, rows, 2 * head_cols))
    dq, e0, e1, e2, e3 = call(
        attn_bwd_kernel,
        (tp_size,),
        [by_step((rows, packed))]
        + [kv_block] * 4
        + [by_step((rows // 2, 2 * head_cols)), whole((HD // 2, rows)), whole((HD // 2, rows))],
        [by_step((rows, head_cols))] + [kv_block] * 4,
        [shape_of((tp_size, rows, head_cols))] + [kv_shape] * 4,
        prefetch=2,
    )(scal, prefix, qkv_seq, *kv_seqs, do, cos_t, sin_t)
    if direct:
        early = [sums_of[index] for index in (1, 0)]
        flat = fence([total.far for total in early] + [e1, e3])
        for total, value in zip(early, flat):
            total.far = value
        e1, e3 = flat[2:]
    from_core_1 = over_ctx(e1, 1)
    from_core_3 = over_ctx(e3, 1)
    far = (e2.astype(F32) + from_core_3.astype(F32)).astype(BF16)
    dq, far, dh2_low = fence([dq, far, dh2_low], from_core_1)
    from_y = over_ctx(far, 2)
    if direct:
        away = [total.second() for total in early]
        (dh2_low,) = fence([dh2_low], *away)

    pair_out = pl.BlockSpec((4, 1, width // 8, 2 * head_cols), lambda i, *_: (0, i, 0, 0))
    pair_shape = shape_of((4, tp_size, width // 8, 2 * head_cols))
    first_grads = call(
        first_grads_kernel,
        (tp_size,),
        [
            mine,
            by_step((rows, head_cols)),
            whole((rows, width)),
            pl.BlockSpec((1, 1, rows // 2, 2 * head_cols), lambda i, scal: (i, scal[2], 0, 0)),
        ],
        [pair_out] * 2,
        [pair_shape] * 2,
    )(scal, n1, dq, dh2_low, o_all)

    if direct:
        sum_qo = Sum(first_grads[0], over_ctx(first_grads[1], 1), True)
        (from_y,) = fence([from_y], sum_qo.first())
    from_y, y_own = fence([from_y, y_own])
    activations = lax.all_gather((h2 + y_own[0].astype(F32)).astype(BF16), "tp", axis=0)
    dkv = call(
        swing_kernel,
        (tp_size,),
        [kv_block] * 3 + [whole((rows, packed))] * 2,
        kv_block,
        kv_shape,
        prefetch=0,
    )(e0, from_core_1, from_y, cos_table, sin_table)

    def by_group(shape):
        return pl.BlockSpec((1,) + shape, lambda i, *_: (i, 0, 0))

    gi, sums = call(
        end_kernel,
        (tp_size,),
        [by_group((rows, head_cols)), by_group((rows, 2 * head_cols))]
        + [by_group((packed // 4, width))] * 4
        + [whole((rows, width)), mine, whole((16, width)), whole((16, width))],
        [whole((rows, width)), whole((16, width))],
        [shape_of((rows, width)), shape_of((16, width), F32)],
        [pltpu.VMEM((packed, width), BF16), pltpu.VMEM((rows, width), F32)],
    )(scal, dq, dkv, *w_pieces, dh2, layer_input, small, sums)
    dkv_late, n1_late, sums, gi = fence([dkv, n1, sums, gi])
    if direct:
        dkv_late, sums_of[1].last = fence([dkv_late, sums_of[1].last])
    gi_all = lax.all_gather(gi, "tp", axis=0)
    last_shape = shape_of((4, tp_size + 1, width // 8, 2 * head_cols))
    second_grads = call(
        second_grads_kernel,
        (tp_size + 1,),
        [
            mine,
            pl.BlockSpec((1, rows, 2 * head_cols), lambda i, *_: (jnp.minimum(i, tp_size - 1), 0, 0)),
            whole((16, width)),
        ],
        [pair_out] * 2,
        [last_shape] * 2,
    )(scal, n1_late, dkv_late, sums)

    if direct:
        sum_kv = Sum(second_grads[0], over_ctx(second_grads[1], 1), False)
        (sums_of[3].far,) = fence([sums_of[3].far], *second_grads)
        sum_kv.fence(sums_of[3].far)
        (sums_of[2].far,) = fence([sums_of[2].far], sum_kv.first())
        (sum_qo.far,) = fence([sum_qo.far], sums_of[2].second(), sums_of[3].second())
        away = sum_qo.second()
        early = (1, 0)
        flat = fence([sums_of[index].last for index in early], away)
        for index, value in zip(early, flat):
            sums_of[index].last = value
        results = [sums_of[index].result() for index in (0, 1)]
        (sum_kv.far,) = fence([sum_kv.far], *results)
        away = sum_kv.second()
        (sums_of[3].last,) = fence([sums_of[3].last], away)
        shared_result = sums_of[3].result()
        (sums_of[2].last,) = fence([sums_of[2].last], away)
        results += [sums_of[2].result(), shared_result]
        sum_kv.last, sum_qo.last = fence([sum_kv.last, sum_qo.last], *results)
        grads_qo, grads_kv = sum_qo.result(), sum_kv.result()
    else:
        grads_qo, grads_kv = scatter_plain(*first_grads), scatter_plain(*second_grads)
        results = [scatter_plain(*expert_group), scatter_plain(*shared_group)]
    grads_all = jnp.concatenate(
        [grads_qo, grads_kv[:tp_size], jnp.broadcast_to(grads_kv[tp_size:, :, :128], (tp_size, part, 128))], axis=-1
    )
    grads_all, gi_all = fence([grads_all.astype(BF16), gi_all])
    grads_all = jnp.sum(lax.all_to_all(grads_all, "tp", 0, 0, tiled=True).astype(F32), 0)
    grads_qo, grads_kv = grads_all[:, :2 * head_cols], grads_all[:, 2 * head_cols:4 * head_cols]
    sums = jnp.transpose(grads_all[:, 4 * head_cols:4 * head_cols + 16])
    grad_input = gi_all.astype(F32)
    results = [value.reshape(value.shape[0], 3, part, hidden) for value in results]
    grads_shared = results[-1][0]
    results = results[:-1]
    grads_exp = [jnp.concatenate([value[:, i] for value in results], axis=0) for i in range(3)]

    return (
        activations.reshape(layer_input.shape),
        grad_input.reshape(layer_input.shape),
        sums[8],
        grads_qo[:, :head_cols],
        grads_kv[:, :head_cols],
        grads_kv[:, head_cols:],
        jnp.transpose(grads_qo[:, head_cols:]),
        sums[9],
        jnp.transpose(sums[0:8]),
        grads_exp[0],
        grads_exp[1],
        jnp.transpose(grads_exp[2], (0, 2, 1)),
        grads_shared[0],
        grads_shared[1],
        jnp.transpose(grads_shared[2]),
    )


def solution(mesh):
    placed = (
        P("fsdp", "ctx", None),
        P("fsdp"),
        P("fsdp", "tp"),
        P("fsdp", "tp"),
        P("fsdp", "tp"),
        P("tp", "fsdp"),
        P("fsdp"),
        P("fsdp", None),
        P(None, "fsdp", "tp"),
        P(None, "fsdp", "tp"),
        P(None, "tp", "fsdp"),
        P("fsdp", "tp"),
        P("fsdp", "tp"),
        P("tp", "fsdp"),
        P("fsdp", "ctx", None),
        P("fsdp"),
        P("fsdp", "ctx", None),
    )
    return jax.shard_map(
        functools.partial(body, mesh.shape["fsdp"]),
        mesh=mesh,
        in_specs=placed,
        out_specs=(
            P("fsdp", "ctx", None),
            P("fsdp", "ctx", None),
            P(("fsdp", "ctx")),
            P(("fsdp", "ctx"), "tp"),
            P(("fsdp", "ctx"), "tp"),
            P(("fsdp", "ctx"), "tp"),
            P("tp", ("fsdp", "ctx")),
            P(("fsdp", "ctx")),
            P(("fsdp", "ctx"), None),
            P(None, ("fsdp", "ctx"), "tp"),
            P(None, ("fsdp", "ctx"), "tp"),
            P(None, "tp", ("fsdp", "ctx")),
            P(("fsdp", "ctx"), "tp"),
            P(("fsdp", "ctx"), "tp"),
            P("tp", ("fsdp", "ctx")),
        ),
        check_vma=False,
    )
```

```python
import functools
import math

import jax
import jax.numpy as jnp
from jax import lax
from jax.experimental import pallas as pl
from jax.experimental.pallas import tpu as pltpu
from jax.sharding import PartitionSpec as P

HD = 64
SLOTS = 80
EPS = 1e-06
F32 = jnp.float32
BF16 = jnp.bfloat16
VMEM_BYTES = 56 * 1024 * 1024


def mm(a, b):
    return lax.dot_general(a, b, (((1,), (0,)), ((), ())), preferred_element_type=F32)


def mm_nt(a, b):
    return lax.dot_general(a, b, (((1,), (1,)), ((), ())), preferred_element_type=F32)


def mm_tn(a, b):
    return lax.dot_general(a, b, (((0,), (0,)), ((), ())), preferred_element_type=F32)


def params(steps=1):
    return pltpu.CompilerParams(
        dimension_semantics=("arbitrary",) * steps, vmem_limit_bytes=VMEM_BYTES
    )


def rotation(width):
    row = lax.broadcasted_iota(jnp.int32, (width, width), 0)
    col = lax.broadcasted_iota(jnp.int32, (width, width), 1)
    first = (col % HD) < HD // 2
    minus = first & (row == col + HD // 2)
    plus = jnp.logical_not(first) & (row == col - HD // 2)
    return jnp.where(minus, -1.0, jnp.where(plus, 1.0, 0.0)).astype(BF16)


def row_scale(value):
    return lax.rsqrt(jnp.mean(value * value, -1, keepdims=True) + EPS)


def qkv_kernel(scal, x_ref, own_ref, oth_ref, cos_ref, sin_ref, n1_ref, q_ref, kv_ref, all_ref, w_ref, small_ref, swap):
    half = own_ref.shape[1]
    packed = w_ref.shape[0]

    @pl.when(pl.program_id(0) == 0)
    def _():
        mine = pl.multiple_of(scal[0] * half, half)
        other = pl.multiple_of((1 - scal[0]) * half, half)
        w_ref[:, pl.ds(mine, half)] = own_ref[:packed, :]
        w_ref[:, pl.ds(other, half)] = oth_ref[:packed, :]
        swap[...] = jnp.zeros_like(swap)
        for head in list(range(0, 192, HD)) + list(range(256, 448, HD)):
            middle, end = head + HD // 2, head + HD
            swap[head:middle, :] = -w_ref[middle:end, :]
            swap[middle:end, :] = w_ref[head:middle, :]
        small_ref[...] = w_ref[192:208, :].astype(F32)

    x = x_ref[0].astype(F32)
    n1 = (x * row_scale(x) * small_ref[8:9, :]).astype(BF16)
    n1_ref[0] = n1
    turned = (mm_nt(n1, w_ref[...]) * cos_ref[...] + mm_nt(n1, swap[...]) * sin_ref[...]).astype(BF16)
    q_ref[0] = turned[:, :192]
    kv_ref[0] = turned[:, 256:640]
    all_ref[0] = turned


def visible(scal, prefix, keys, rows):
    key_pos = lax.broadcasted_iota(jnp.int32, (keys, rows), 0) ^ (scal[1] * rows)
    row_pos = lax.broadcasted_iota(jnp.int32, (keys, rows), 1) + scal[1] * rows
    return (key_pos <= row_pos) | (key_pos < prefix)


def only_head(rows, head):
    lane = lax.broadcasted_iota(jnp.int32, rows.shape, 1)
    return jnp.where((lane >= head * HD) & (lane < (head + 1) * HD), rows, jnp.zeros_like(rows))


def softmax(scores, seen):
    scores = jnp.where(seen, scores, -1e30)
    expo = jnp.exp(scores - jnp.max(scores, 0, keepdims=True))
    return expo, 1.0 / jnp.sum(expo, 0, keepdims=True)


def attn_fwd_kernel(scal, prefix, q_ref, kv0, kv1, kv2, kv3, o_ref):
    q = q_ref[0]
    rows, width = q.shape
    heads = width // HD
    kv = jnp.concatenate([kv0[0], kv1[0], kv2[0], kv3[0]], axis=0)
    k = kv[:, :width]
    value_t = jnp.transpose(kv[:, width:].astype(F32)).astype(BF16)
    seen = visible(scal, prefix[pl.program_id(0)], kv.shape[0], rows)
    outs = []
    for head in range(heads):
        expo, factor = softmax(mm_nt(k, only_head(q, head) * (HD ** -0.5)), seen)
        outs.append(mm(value_t[head * HD:(head + 1) * HD], expo.astype(BF16)) * factor)
    o = jnp.transpose(jnp.concatenate(outs, axis=0))
    o_ref[0] = jnp.concatenate([o[: rows // 2], o[rows // 2:]], axis=1).astype(BF16)


def fill_out_weights(scal, wo, wo_ref):
    pieces, _, width, half = wo_ref.shape
    for piece in range(pieces):
        for index, side in enumerate((scal[0], 1 - scal[0])):
            at = pl.ds(pl.multiple_of(side * half, half), half)
            wo[piece * width:(piece + 1) * width, at] = wo_ref[piece, index]


def post_kernel(scal, o_ref, wo_ref, x_ref, small_ref, routes_ref, n2_ref, h2_ref, gates_ref, slots_ref, wo):
    step = pl.program_id(0)
    width = wo_ref.shape[2]

    @pl.when(step == 0)
    def _():
        fill_out_weights(scal, wo, wo_ref)

    low = jnp.zeros((o_ref.shape[2], wo.shape[1]), F32)
    high = low
    for piece in range(o_ref.shape[0]):
        block = o_ref[piece, 0]
        weights = wo[piece * width:(piece + 1) * width, :]
        low += mm(block[:, :width], weights)
        high += mm(block[:, width:], weights)
    h2 = x_ref[0].astype(F32) + jnp.concatenate([low, high], axis=0)
    n2 = (h2 * row_scale(h2) * small_ref[9:10, :]).astype(BF16)
    n2_ref[0] = n2

    @pl.when(step == scal[2])
    def _():
        h2_ref[...] = h2

    expo = jnp.exp(mm_nt(small_ref[0:8, :].astype(BF16), n2))
    gates_ref[0] = expo / jnp.sum(expo, 0, keepdims=True)
    rows = n2.shape[0]
    expert = lax.broadcasted_iota(jnp.int32, (8, rows), 0)
    named = (routes_ref[0, 0:1, :] == expert) | (routes_ref[0, 1:2, :] == expert)
    before = lax.broadcasted_iota(jnp.int32, (rows, rows), 0) < lax.broadcasted_iota(jnp.int32, (rows, rows), 1)
    place = mm(named.astype(BF16), before.astype(BF16))
    slots_ref[0] = jnp.where(named, place.astype(jnp.int32), -1)


def silu_parts(value):
    sigma = 0.5 * jnp.tanh(0.5 * value) + 0.5
    return sigma, value * sigma


def split_blocks(core, value, blocks):
    rows = value.shape[0] // (2 * blocks)
    value = value.astype(BF16).reshape(blocks, 2, rows, value.shape[1])
    first = core == 0
    return jnp.where(first, value[:, 0], value[:, 1]), jnp.where(first, value[:, 1], value[:, 0])


def put_grads(core, keep_ref, send_ref, index, value):
    keep, send = split_blocks(core, value, keep_ref.shape[0])
    at = slice(index * keep.shape[1], (index + 1) * keep.shape[1])
    keep_ref[:, 0, at, :] = keep
    send_ref[:, 0, at, :] = send


def shared_kernel(
    scal, n2_ref, dy_ref, go_ref, uo_ref, do_ref, g0, g1, g2, g3, u0, u1, u2, u3, d0, d1, d2, d3,
    ys_ref, dn_ref, hid_ref, dab_ref, wgu, wd,
):
    step = pl.program_id(0)
    half = go_ref.shape[0]
    hidden = go_ref.shape[1]

    @pl.when(step == 0)
    def _():
        mine = pl.multiple_of(scal[0] * half, half)
        other = (1 - scal[0]) * half
        wgu[pl.ds(mine, half), :hidden] = go_ref[...]
        wgu[pl.ds(mine, half), hidden:] = uo_ref[...]
        wd[:, pl.ds(mine, half)] = do_ref[...]
        for piece, (g, u, d) in enumerate(((g0, u0, d0), (g1, u1, d1), (g2, u2, d2), (g3, u3, d3))):
            quarter = scal[3] ^ piece
            at = pl.multiple_of(other + quarter * (half // 4), half // 4)
            wgu[pl.ds(at, half // 4), :hidden] = g[...]
            wgu[pl.ds(at, half // 4), hidden:] = u[...]
            at = pl.multiple_of(quarter * (hidden // 4), hidden // 4)
            wd[pl.ds(at, hidden // 4), pl.ds(pl.multiple_of(other, half), half)] = d[...]

    shape = n2_ref.shape[:2]
    n2 = n2_ref[...].reshape(-1, n2_ref.shape[2])
    dy = dy_ref[...].reshape(-1, dy_ref.shape[2])

    def put(ref, value):
        ref[...] = value.astype(BF16).reshape(shape + (value.shape[1],))

    both = mm(n2, wgu[...])
    gate, up = both[:, :hidden], both[:, hidden:]
    sigma, silu = silu_parts(gate)
    hid = (silu * up).astype(BF16)
    put(ys_ref, mm(hid, wd[...]))
    back = mm_nt(dy, wd[...])
    da = (back * up * (sigma * (1.0 + gate * (1.0 - sigma)))).astype(BF16)
    db = (back * silu).astype(BF16)
    dab = jnp.concatenate([da, db], axis=1)
    put(dn_ref, mm_nt(dab, wgu[...]))
    put(hid_ref, hid)
    put(dab_ref, dab)


def put_all_grads(core, keep_ref, send_ref, value, upstream, hid, dab):
    wide = mm_tn(value, dab)
    hidden = hid.shape[1]
    put_grads(core, keep_ref, send_ref, 0, wide[:, :hidden])
    put_grads(core, keep_ref, send_ref, 1, wide[:, hidden:])
    put_grads(core, keep_ref, send_ref, 2, mm_tn(upstream, hid))


def shared_grads_kernel(scal, n2_ref, dy_ref, hid_ref, dab_ref, keep_ref, send_ref):
    values = [ref[...].reshape(-1, ref.shape[-1]) for ref in (n2_ref, dy_ref, hid_ref, dab_ref)]
    put_all_grads(scal[4], keep_ref, send_ref, *values)


def moe_kernel(
    scal, n2_ref, dy_ref, slots_ref, gates_ref, ys_ref, dn_in_ref, gate_own, up_own, down_own,
    w0, w1, w2, w3, r0, r1, r2, r3, d0, d1, d2, d3,
    y_ref, dn_ref, keep_ref, send_ref, wgu_s, wd_s, sems, pick_s, ye_s, dx_s, xe_s, dy_s, de_s, gs_s, dprob_s,
):
    step = pl.program_id(0)
    seqs, rows, width = n2_ref.shape
    hidden, half = down_own.shape[1:]
    experts = slots_ref.shape[1]
    slot_now = step % 2
    mine = pl.multiple_of(scal[0] * half, half)
    other = pl.multiple_of((1 - scal[0]) * half, half)

    def expert_at(index):
        return 2 * ((index // 2) ^ scal[3]) + index % 2

    def place(slot, index):
        at = pl.ds(mine if index < 3 else other, half)
        if index % 3 == 2:
            return wd_s.at[slot, :, at]
        return wgu_s.at[slot, at, pl.ds(index % 3 * hidden, hidden)]

    def fetch(index):
        slot, piece, odd = index % 2, index // 2, index % 2

        def start(number, source):
            pltpu.make_async_copy(source, place(slot, number), sems.at[slot, number]).start()

        for number, ref in enumerate((gate_own, up_own, down_own)):
            start(number, ref.at[expert_at(index)])
        for number, (wide, rest, down) in enumerate(((w0, r0, d0), (w1, r1, d1), (w2, r2, d2), (w3, r3, d3))):
            @pl.when(piece == number)
            def _(wide=wide, rest=rest, down=down):
                start(3, wide.at[pl.ds(pl.multiple_of(odd * half, half), half), :])
                start(5, down.at[pl.ds(pl.multiple_of(odd * hidden, hidden), hidden), :])

                @pl.when(odd == 0)
                def _():
                    start(4, wide.at[pl.ds(2 * half, half), :])

                @pl.when(odd == 1)
                def _():
                    start(4, rest)

    @pl.when(step == 0)
    def _():
        fetch(step)

    @pl.when(step + 1 < experts)
    def _():
        fetch(step + 1)

    @pl.when(step < experts)
    def _():
        expert = expert_at(step)
        for number in range(6):
            source = down_own.at[0] if number % 3 == 2 else gate_own.at[0]
            pltpu.make_async_copy(source, place(slot_now, number), sems.at[slot_now, number]).wait()
        wgu, wd = wgu_s.at[slot_now], wd_s.at[slot_now]

        slot_at = pl.ds(pl.multiple_of(step * SLOTS, 16), SLOTS)
        slot = lax.broadcasted_iota(jnp.int32, (SLOTS, rows), 0)
        odd = step % 2

        @pl.when(odd == 0)
        def _():
            for s in range(seqs):
                at = slice(s * SLOTS, (s + 1) * SLOTS)
                hits = [slots_ref[s, pl.ds(expert + k, 1), :] == slot for k in range(2)]
                pick = jnp.concatenate([hit.astype(BF16) for hit in hits], axis=0)
                pick_s[s, pl.ds(pl.multiple_of(step * SLOTS, 16), 2 * SLOTS), :] = pick
                rows_in = mm(pick, n2_ref[s]).astype(BF16)
                upstream = mm(pick, dy_ref[s])
                for k, hit in enumerate(hits):
                    part = slice(k * SLOTS, (k + 1) * SLOTS)
                    gate_slot = jnp.sum(jnp.where(hit, gates_ref[s, pl.ds(expert + k, 1), :], 0.0), 1, keepdims=True)
                    xe_s[k, at, :] = rows_in[part]
                    dy_s[k, at, :] = upstream[part].astype(BF16)
                    de_s[k, at, :] = (gate_slot * upstream[part]).astype(BF16)
                    gs_s[k, at, :] = jnp.broadcast_to(gate_slot, (SLOTS, 128))

        xe = xe_s[odd]
        both = mm(xe, wgu[...])
        gate, up = both[:, :hidden], both[:, hidden:]
        sigma, silu = silu_parts(gate)
        hid = (silu * up).astype(BF16)
        ye = mm(hid, wd[...])
        dots = jnp.sum(ye * dy_s[odd].astype(F32), 1, keepdims=True)
        ye = (ye * gs_s[odd][:, 0:1]).astype(BF16)
        for s in range(seqs):
            at = slice(s * SLOTS, (s + 1) * SLOTS)
            ye_s[s, slot_at, :] = ye[at]
            hit = slots_ref[s, pl.ds(expert, 1), :] == slot
            dprob_s[s, pl.ds(expert, 1), :] = jnp.sum(jnp.where(hit, dots[at], 0.0), 0, keepdims=True)
        back = mm_nt(de_s[odd], wd[...])
        da = (back * up * (sigma * (1.0 + gate * (1.0 - sigma)))).astype(BF16)
        db = (back * silu).astype(BF16)
        dab = jnp.concatenate([da, db], axis=1)
        dx = mm_nt(dab, wgu[...]).astype(BF16)
        for s in range(seqs):
            dx_s[s, slot_at, :] = dx[s * SLOTS:(s + 1) * SLOTS]
        put_all_grads(scal[4], keep_ref, send_ref, xe, de_s[odd], hid, dab)

    @pl.when(step >= experts)
    def _():
        s = step - experts
        pick = pick_s[s]
        y_ref[0] = (ys_ref[0].astype(F32) + mm_tn(pick, ye_s[s])).astype(BF16)
        dn_ref[0, 0:rows, :] = (dn_in_ref[0].astype(F32) + mm_tn(pick, dx_s[s])).astype(BF16)
        tail = jnp.concatenate([dprob_s[s], jnp.zeros((dn_ref.shape[1] - rows - experts, rows), F32)], axis=0)
        tail = jnp.concatenate([tail, jnp.zeros((tail.shape[0], width - rows), F32)], axis=1)
        dn_ref[0, rows:, :] = tail.astype(BF16)


def norm_back(grad_out, value, scale, gain):
    weighted = grad_out * gain
    return scale * weighted - value * (scale * scale * scale) * jnp.mean(weighted * value, -1, keepdims=True)


def mid_kernel(scal, dn_ref, gates_ref, h2_ref, n2_ref, dy_ref, small_ref, wo_ref, dh2_ref, do_ref, low_ref, sums_ref, wo):
    rows = h2_ref.shape[0]
    pieces, _, width, _ = wo_ref.shape
    fill_out_weights(scal, wo, wo_ref)
    parts = dn_ref[0].astype(F32)
    gates = gates_ref[0]
    dprob = parts[rows:rows + 8, 0:rows]
    dlogits = (gates * (dprob - jnp.sum(dprob * gates, 0, keepdims=True))).astype(BF16)
    dn2 = parts[0:rows, :] + mm_tn(dlogits, small_ref[0:8, :].astype(BF16))
    h2 = h2_ref[...]
    scale = row_scale(h2)
    sums_ref[0:8, :] = mm(dlogits, n2_ref[0])
    sums_ref[8:16, :] = jnp.zeros((8, h2.shape[1]), F32)
    sums_ref[9:10, :] = jnp.sum(dn2 * h2 * scale, 0, keepdims=True)
    dh2 = dy_ref[0].astype(F32) + norm_back(dn2, h2, scale, small_ref[9:10, :])
    dh2_ref[...] = dh2
    low = dh2.astype(BF16)
    low_ref[...] = low
    for piece in range(pieces):
        do = mm_nt(low, wo[piece * width:(piece + 1) * width, :])
        do_ref[piece] = jnp.concatenate([do[: rows // 2], do[rows // 2:]], axis=1).astype(BF16)


def attn_bwd_kernel(
    scal, prefix, q_ref, kv0, kv1, kv2, kv3, do_ref, cos_ref, sin_ref, dq_ref, e0, e1, e2, e3
):
    rows, width = dq_ref.shape[1:]
    q = q_ref[0][:, :width]
    heads = width // HD
    kv = jnp.concatenate([kv0[0], kv1[0], kv2[0], kv3[0]], axis=0)
    k = kv[:, :width]
    v = kv[:, width:]
    key_t = jnp.transpose(k.astype(F32)).astype(BF16)
    do = jnp.concatenate([do_ref[0][:, :width], do_ref[0][:, width:]], axis=0)
    seen = visible(scal, prefix[scal[2]], kv.shape[0], rows)
    cosine, sine = cos_ref[...], sin_ref[...]
    turned, ds_all, probs_all, q_all, do_all = [], [], [], [], []
    for head in range(heads):
        q_head = only_head(q, head) * (HD ** -0.5)
        do_head = only_head(do, head)
        expo, factor = softmax(mm_nt(k, q_head), seen)
        probs = expo * factor
        dp = mm_nt(v, do_head)
        ds = (probs * (dp - jnp.sum(dp * probs, 0, keepdims=True))).astype(BF16)
        dq = mm(key_t[head * HD:(head + 1) * HD], ds) * (HD ** -0.5)
        first, second = dq[: HD // 2], dq[HD // 2:]
        turned += [first * cosine + second * sine, second * cosine - first * sine]
        ds_all.append(ds)
        probs_all.append(probs.astype(BF16))
        q_all.append(q_head)
        do_all.append(do_head)
    dq_ref[0] = jnp.transpose(jnp.concatenate(turned, axis=0)).astype(BF16)
    dk = mm(jnp.concatenate(ds_all, axis=1), jnp.concatenate(q_all, axis=0))
    dv = mm(jnp.concatenate(probs_all, axis=1), jnp.concatenate(do_all, axis=0))
    dkv = jnp.concatenate([dk, dv], axis=1).astype(BF16)
    for piece, out in enumerate((e0, e1, e2, e3)):
        out[0] = dkv[piece * rows:(piece + 1) * rows]


def swing_kernel(a_ref, b_ref, c_ref, cos_ref, sin_ref, out_ref):
    dkv = a_ref[0].astype(F32) + b_ref[0].astype(F32) + c_ref[0].astype(F32)
    swung = dkv * sin_ref[:, 256:]
    high = swung.astype(BF16)
    low = (swung - high.astype(F32)).astype(BF16)
    turn = rotation(dkv.shape[1])
    out_ref[0] = (dkv * cos_ref[:, 256:] + mm_nt(high, turn) + mm_nt(low, turn)).astype(BF16)


def end_kernel(scal, dq_ref, dkv_ref, w0, w1, w2, w3, dh2_ref, x_ref, small_ref, sums_in, gi_ref, sums_ref, w, total):
    step = pl.program_id(0)
    head_cols = dq_ref.shape[2]
    quarter = w.shape[0] // 4
    for piece, ref in enumerate((w0, w1, w2, w3)):
        at = pl.multiple_of((scal[1] ^ piece) * quarter, quarter)
        w[pl.ds(at, quarter), :] = ref[0]
    part = mm(dq_ref[0], w[:head_cols, :]) + mm(dkv_ref[0], w[256:, :])

    @pl.when(step == 0)
    def _():
        total[...] = part

    @pl.when(step > 0)
    def _():
        total[...] += part

    @pl.when(step == pl.num_programs(0) - 1)
    def _():
        x = x_ref[0].astype(F32)
        dn1 = total[...]
        scale = row_scale(x)
        sums_ref[...] = sums_in[...]
        sums_ref[8:9, :] = jnp.sum(dn1 * x * scale, 0, keepdims=True)
        gi_ref[...] = (dh2_ref[...] + norm_back(dn1, x, scale, small_ref[8:9, :])).astype(BF16)


def first_grads_kernel(scal, n1_ref, dq_ref, low_ref, o_ref, keep_ref, send_ref):
    head_cols = dq_ref.shape[2]
    block = o_ref[0, 0]
    o = jnp.concatenate([block[:, :head_cols], block[:, head_cols:]], axis=0)
    grads = jnp.concatenate([mm_tn(n1_ref[0], dq_ref[0]), mm_tn(low_ref[...], o)], axis=1)
    keep_ref[:, 0], send_ref[:, 0] = split_blocks(scal[4], grads, keep_ref.shape[0])


def second_grads_kernel(scal, n1_ref, dkv_ref, sums_ref, keep_ref, send_ref):
    step = pl.program_id(0)
    last = pl.num_programs(0) - 1

    @pl.when(step < last)
    def _():
        keep_ref[:, 0], send_ref[:, 0] = split_blocks(scal[4], mm_tn(n1_ref[0], dkv_ref[0]), keep_ref.shape[0])

    @pl.when(step == last)
    def _():
        sums = sums_ref[...]
        sums = jnp.concatenate([sums, jnp.zeros((keep_ref.shape[3] - sums.shape[0], sums.shape[1]), F32)], axis=0)
        keep_ref[:, 0], send_ref[:, 0] = split_blocks(scal[4], jnp.transpose(sums), keep_ref.shape[0])


def whole(shape):
    return pl.BlockSpec(shape, lambda *_: (0,) * len(shape))


def by_step(shape):
    return pl.BlockSpec((1,) + shape, lambda i, *_: (i,) + (0,) * len(shape))


def call(kernel, grid, in_specs, out_specs, out_shape, scratch=(), prefetch=1, aliases=None):
    return pl.pallas_call(
        kernel,
        grid_spec=pltpu.PrefetchScalarGridSpec(
            num_scalar_prefetch=prefetch,
            grid=grid,
            in_specs=in_specs,
            out_specs=out_specs,
            scratch_shapes=scratch,
        ),
        out_shape=out_shape,
        input_output_aliases=aliases or {},
        compiler_params=params(len(grid)),
        cost_estimate=pl.CostEstimate(flops=1, bytes_accessed=1, transcendentals=0),
    )


def fence(values, *others):
    values = list(values)
    return list(lax.optimization_barrier((*values, *others))[: len(values)])


def shape_of(shape, dtype=BF16):
    return jax.ShapeDtypeStruct(shape, dtype)


def body(
    fsdp_size,
    layer_input,
    gain_attn,
    query_weight,
    key_weight,
    value_weight,
    output_weight,
    gain_ffn,
    router,
    exp_gate,
    exp_up,
    exp_down,
    shared_gate_weight,
    shared_up_weight,
    shared_down_weight,
    routes,
    prefix,
    cotangent,
):
    seqs, rows, width = layer_input.shape
    experts = exp_gate.shape[0]
    hidden = exp_gate.shape[2]
    head_cols = query_weight.shape[1]
    half = width // 2
    paired = fsdp_size == 2
    ctx = lax.axis_index("ctx")
    tp = lax.axis_index("tp")
    ctx_size = lax.axis_size("ctx")
    tp_size = lax.axis_size("tp")
    side = lax.axis_index("fsdp") if paired else jnp.int32(0)
    weight_ctx = ctx if paired else jnp.int32(0)
    blocks = fsdp_size * ctx_size
    direct = paired and ctx_size == 4 and tp_size == 4
    core = ctx % 2 if direct else jnp.int32(0)
    scal = jnp.stack([side, ctx, tp, weight_ctx, core]).astype(jnp.int32)

    def over_x(value):
        return lax.ppermute(value, "fsdp", [(0, 1), (1, 0)])

    def over_tp(value, bit):
        return lax.ppermute(value, "tp", [(i, i ^ bit) for i in range(tp_size)])

    def over_ctx(value, bit):
        return lax.ppermute(value, "ctx", [(i, i ^ bit) for i in range(ctx_size)])

    columns = jnp.concatenate(
        [
            query_weight.T,
            router.T,
            gain_attn[None],
            gain_ffn[None],
            jnp.zeros((54, query_weight.shape[0]), BF16),
            key_weight.T,
            value_weight.T,
            output_weight,
        ],
        axis=0,
    )
    if paired:
        columns_own, columns_other = columns, over_x(columns)
    else:
        columns = lax.all_gather(columns, "fsdp", axis=1, tiled=True)
        columns_own, columns_other = columns[:, :half], columns[:, half:]

    shared_own = (shared_gate_weight, shared_up_weight, shared_down_weight)
    experts_own = (exp_gate, exp_up, exp_down)
    if paired:

        def quarter(value, parts):
            size = value.shape[0] // parts
            return lax.dynamic_slice_in_dim(value, size * ctx, size, 0).reshape(-1, value.shape[-1])

        gate, up, down = [quarter(stack, 4) for stack in experts_own]
        shared_gate, shared_up, shared_down = [quarter(stack, 4) for stack in shared_own]
        wide = jnp.concatenate([gate, up[:half], shared_gate, shared_up], axis=0)
        rest = up[half:]
        down = jnp.concatenate([down, shared_down], axis=0)
        own = experts_own + shared_own
    else:
        gate_all = lax.all_gather(exp_gate, "fsdp", axis=1, tiled=True)
        up_all = lax.all_gather(exp_up, "fsdp", axis=1, tiled=True)
        down_all = lax.all_gather(exp_down, "fsdp", axis=2, tiled=True)
        sg_all = lax.all_gather(shared_gate_weight, "fsdp", axis=0, tiled=True)
        su_all = lax.all_gather(shared_up_weight, "fsdp", axis=0, tiled=True)
        sd_all = lax.all_gather(shared_down_weight, "fsdp", axis=1, tiled=True)
        own = (gate_all[:, :half], up_all[:, :half], down_all[:, :, :half], sg_all[:half], su_all[:half], sd_all[:, :half])

        def split(value):
            return value.reshape((4, value.shape[0] // 4) + value.shape[1:])

        gate_all, up_all, sg_all, su_all = [
            split(value) for value in (gate_all[:, half:], up_all[:, half:], sg_all[half:], su_all[half:])
        ]
        down_all, sd_all = split(down_all[:, :, half:]), split(sd_all[:, half:])
        wide_p = [
            jnp.concatenate([gate_all[p, 0], gate_all[p, 1], up_all[p, 0], sg_all[p], su_all[p]], axis=0) for p in range(4)
        ]
        rest_p = [up_all[p, 1] for p in range(4)]
        down_p = [jnp.concatenate([down_all[p, 0], down_all[p, 1], sd_all[p]], axis=0) for p in range(4)]

    positions = (ctx * rows + jnp.arange(rows, dtype=jnp.int32)).astype(F32)
    inverse = jnp.exp(jnp.arange(HD // 2, dtype=F32) * (-math.log(10000.0) / (HD // 2)))
    angles = positions[:, None] * inverse[None, :]
    cosine, sine = jnp.cos(angles), jnp.sin(angles)
    heads = head_cols // HD

    def table(value, rest):
        turned = jnp.tile(value, (1, 2 * heads))
        plain = jnp.full((rows, head_cols), rest, F32)
        return jnp.concatenate([turned, plain[:, :64], turned, plain], axis=1)

    cos_table, sin_table = table(cosine, 1.0), table(sine, 0.0)
    routes_t = jnp.pad(jnp.transpose(routes, (0, 2, 1)), ((0, 0), (0, 6), (0, 0)))

    cos_t, sin_t = jnp.transpose(cosine), jnp.transpose(sine)
    columns_other, cos_table, sin_table, cos_t, sin_t = fence([columns_other, cos_table, sin_table, cos_t, sin_t], routes_t)
    if paired:
        columns_other, cos_table, wide, rest, down = fence([columns_other, cos_table, wide, rest, down])
        wide_0 = over_x(wide)
    out_pieces = jnp.stack([columns_own[-head_cols:], columns_other[-head_cols:]])
    out_pieces = lax.all_gather(out_pieces, "tp", axis=0)
    packed = cos_table.shape[1]

    n1, q, kv, qkv, w_qkv, small = call(
        qkv_kernel,
        (seqs,),
        [
            by_step((rows, width)),
            whole((packed + head_cols, half)),
            whole((packed + head_cols, half)),
            whole((rows, packed)),
            whole((rows, packed)),
        ],
        [
            by_step((rows, width)),
            by_step((rows, head_cols)),
            by_step((rows, 2 * head_cols)),
            by_step((rows, packed)),
            whole((packed, width)),
            whole((16, width)),
        ],
        [
            shape_of((seqs, rows, width)),
            shape_of((seqs, rows, head_cols)),
            shape_of((seqs, rows, 2 * head_cols)),
            shape_of((seqs, rows, packed)),
            shape_of((packed, width)),
            shape_of((16, width), F32),
        ],
        [pltpu.VMEM((packed, width), BF16)],
    )(scal, layer_input, columns_own, columns_other, cos_table, sin_table)

    kv_0 = kv
    kv_2 = over_ctx(kv_0, 2)
    kv_1 = over_ctx(kv_0, 1)
    q_now, kv_2 = fence([q, kv_2], kv_1)
    w_part = lax.dynamic_slice_in_dim(w_qkv, (packed // 4) * ctx, packed // 4, 0)
    w_part = jnp.pad(w_part, ((0, 16), (0, 0)))
    if paired:
        kv_2, wide_0, rest, down, w_part = fence([kv_2, wide_0, rest, down, w_part])
        wide_2 = over_ctx(wide_0, 2)
        rest_0 = over_x(rest)
        (down,) = fence([down], rest)
        down_0 = over_x(down)
    kv_3 = over_ctx(kv_2, 1)
    q_now, kv_3, out_pieces = fence([q_now, kv_3, out_pieces])

    o = call(
        attn_fwd_kernel,
        (seqs,),
        [by_step((rows, head_cols))] + [by_step((rows, 2 * head_cols))] * 4,
        by_step((rows // 2, 2 * head_cols)),
        shape_of((seqs, rows // 2, 2 * head_cols)),
        prefetch=2,
    )(scal, prefix, q_now, kv_0, kv_1, kv_2, kv_3)

    o_all = lax.all_gather(o, "tp", axis=0)
    if paired:
        wide_0, rest_0 = fence([wide_0, rest_0], o)
        rest_2, rest_1, wide_1 = over_ctx(rest_0, 2), over_ctx(rest_0, 1), over_ctx(wide_0, 1)
        down_0, wide_2, rest_1, wide_1 = fence([down_0, wide_2, rest_1, wide_1])
        down_2, down_1, wide_3 = over_ctx(down_0, 2), over_ctx(down_0, 1), over_ctx(wide_2, 1)
        (rest_2,) = fence([rest_2], down_0, wide_2)
        down_1, wide_3 = fence([down_1, wide_3], rest_2)
        rest_3 = over_ctx(rest_2, 1)
        o_all, down_1, wide_3 = fence([o_all, down_1, wide_3])
    w_0 = lax.all_gather(fence([w_part], o_all)[0], "tp", axis=0)
    n2, h2, gates, slots = call(
        post_kernel,
        (seqs,),
        [
            pl.BlockSpec((tp_size, 1, rows // 2, 2 * head_cols), lambda i, *_: (0, i, 0, 0)),
            whole((tp_size, 2, head_cols, half)),
            by_step((rows, width)),
            whole((16, width)),
            by_step((8, rows)),
        ],
        [by_step((rows, width)), whole((rows, width)), by_step((8, rows)), by_step((8, rows))],
        [
            shape_of((seqs, rows, width)),
            shape_of((rows, width), F32),
            shape_of((seqs, 8, rows), F32),
            shape_of((seqs, 8, rows), jnp.int32),
        ],
        [pltpu.VMEM((width, width), BF16)],
    )(scal, o_all, out_pieces, layer_input, small, routes_t)

    if paired:
        down_2, rest_3 = fence([down_2, rest_3], n2)
        down_3 = over_ctx(down_2, 1)
        wide_p = (wide_0, wide_1, wide_2, wide_3)
        rest_p = (rest_0, rest_1, rest_2, rest_3)
        down_p = (down_0, down_1, down_2, down_3)

    full = pl.BlockSpec((seqs, rows, width), lambda *_: (0, 0, 0), pipeline_mode=pl.Buffered(1))
    part_rows = 3 * (width // 8)
    upper = [pl.BlockSpec((half // 4, hidden), lambda *_, at=at: (at, 0)) for at in (12, 13)]
    lower = pl.BlockSpec((hidden // 4, half), lambda *_: (8, 0))
    weights = [pltpu.VMEM((width, 2 * hidden), BF16), pltpu.VMEM((hidden, width), BF16)]

    def by_pair(cols):
        return pl.BlockSpec((2, rows, cols), lambda i, *_: (i, 0, 0))

    ys, dn_shared, *shared_hidden = call(
        shared_kernel,
        (seqs // 2,),
        [by_pair(width)] * 2
        + [whole((half, hidden)), whole((half, hidden)), whole((hidden, half))]
        + [upper[0]] * 4
        + [upper[1]] * 4
        + [lower] * 4,
        [by_pair(width)] * 2 + [by_pair(hidden), by_pair(2 * hidden)],
        [shape_of((seqs, rows, width))] * 2 + [shape_of((seqs, rows, hidden)), shape_of((seqs, rows, 2 * hidden))],
        weights,
    )(scal, n2, cotangent, *own[3:], *wide_p, *wide_p, *down_p)

    qkv_late, w_0, ys = fence([qkv, w_0, ys])
    qkv_seq = lax.all_to_all(qkv_late, "tp", 0, 0, tiled=True)
    w_2, w_1 = over_ctx(w_0, 2), over_ctx(w_0, 1)

    def expert_of(i, scal):
        i = jnp.minimum(i, experts - 1)
        return 2 * ((i // 2) ^ scal[3]) + i % 2

    late = pl.BlockSpec((1, rows, width), lambda i, scal: (jnp.maximum(i - experts, 0), 0, 0))

    dn_rows = rows + 16
    slot_rows = seqs * SLOTS
    block = (4, 1, part_rows, hidden)

    expert_grads = pl.BlockSpec(block, lambda i, scal: (0, expert_of(i, scal), 0, 0))
    y, dn, *expert_group = call(
        moe_kernel,
        (experts + seqs,),
        [full, full, whole((seqs, 8, rows)), whole((seqs, 8, rows)), late, late]
        + [pl.BlockSpec(memory_space=pl.ANY)] * 15,
        [late, pl.BlockSpec((1, dn_rows, width), lambda i, *_: (jnp.maximum(i - experts, 0), 0, 0))]
        + [expert_grads] * 2,
        [shape_of((seqs, rows, width)), shape_of((seqs, dn_rows, width))]
        + [shape_of((4, experts, part_rows, hidden))] * 2,
        [pltpu.VMEM((2, width, 2 * hidden), BF16), pltpu.VMEM((2, hidden, width), BF16)]
        + [pltpu.SemaphoreType.DMA((2, 6))]
        + [pltpu.VMEM((seqs, experts * SLOTS, rows), BF16)]
        + [pltpu.VMEM((seqs, experts * SLOTS, width), BF16)] * 2
        + [pltpu.VMEM((2, slot_rows, width), BF16)] * 3
        + [pltpu.VMEM((2, slot_rows, 128), F32), pltpu.VMEM((seqs, 8, rows), F32)],
    )(scal, n2, cotangent, slots, gates, ys, dn_shared, *own[:3], *wide_p, *rest_p, *down_p)

    dn, qkv_seq, w_2, w_1, n2_late, *expert_group = fence([dn, qkv_seq, w_2, w_1, n2, *expert_group])
    w_pieces = (w_0, w_1, w_2, over_ctx(w_2, 1))
    dn_own = lax.psum_scatter(dn, "tp", scatter_dimension=0, tiled=True)
    kv_seq = qkv_seq[:, :, 256:]
    kv_seq_2, kv_seq_1 = over_ctx(kv_seq, 2), over_ctx(kv_seq, 1)

    shared_group = call(
        shared_grads_kernel,
        (1,),
        [full] * 2 + [whole((seqs, rows, hidden)), whole((seqs, rows, 2 * hidden))],
        [whole(block)] * 2,
        [shape_of(block)] * 2,
    )(scal, n2_late, cotangent, *shared_hidden)

    part = width // blocks
    along_x, along_y = side, ctx // 2

    def pick(value, x, y, first, count):
        value = value.reshape((2, 2) + value.shape[1:])
        sizes = (2 if x is None else 1, 2 if y is None else 1, count) + value.shape[3:]
        begin = (0 if x is None else x, 0 if y is None else y, first, 0, 0)
        value = lax.dynamic_slice(value, begin, sizes)
        value = value.reshape(tuple(n for n, at in zip(sizes[:2], (x, y)) if at is None) + sizes[2:])
        return value.astype(F32)

    def indexed(value, index):
        return lax.dynamic_index_in_dim(value, index, 0, False).astype(F32)

    class Sum:
        def __init__(self, keep, got, y_first, first=0, count=None):
            self.keep, self.got, self.y_first = keep, got, y_first
            self.range = (first, count or keep.shape[1])

        def fence(self, *others):
            (self.got,) = fence([self.got], *others)

        def both(self, x, y):
            return pick(self.keep, x, y, *self.range) + pick(self.got, x, y, *self.range)

        def first(self):
            if self.y_first:
                self.sent = self.both(None, 1 - along_y).astype(BF16)
            else:
                self.sent = self.both(1 - along_x, None).astype(BF16)
            self.far = over_ctx(self.sent, 2) if self.y_first else over_x(self.sent)
            return self.sent

        def second(self):
            if self.y_first:
                self.away = (self.both(1 - along_x, along_y) + indexed(self.far, 1 - along_x)).astype(BF16)
                self.last = over_x(self.away)
            else:
                self.away = (self.both(along_x, 1 - along_y) + indexed(self.far, 1 - along_y)).astype(BF16)
                self.last = over_ctx(self.away, 2)
            return self.away

        def result(self):
            mine = indexed(self.far, along_x if self.y_first else along_y)
            return self.both(along_x, along_y) + mine + self.last.astype(F32)

    def scatter_plain(keep, send):
        count, cols = keep.shape[1], keep.shape[3]
        triples = keep.shape[2] // (width // 8)
        both = jnp.stack([keep, send], axis=1).reshape(8, count, triples, width // 8, cols)
        both = jnp.transpose(both, (0, 3, 1, 2, 4)).reshape(blocks, part, count * triples, cols)
        both = jnp.transpose(both, (0, 2, 1, 3)).reshape(blocks, count * triples * part, cols)
        both = lax.psum_scatter(both, ("fsdp", "ctx"), scatter_dimension=0, tiled=True)
        return both.reshape(count, triples * part, cols).astype(F32)

    if direct:
        got, shared_got = over_ctx(expert_group[1], 1), over_ctx(shared_group[1], 1)
        cuts = ((0, 2, True), (2, 2, False), (4, 4, False))
        sums_of = [Sum(expert_group[0], got, y_first, first, count) for first, count, y_first in cuts]
        sums_of.append(Sum(shared_group[0], shared_got, True))
        sent = [sums_of[1].first(), sums_of[0].first()]
        sums_of[2].fence(*sent)
        sent.append(sums_of[2].first())
        (kv_seq_2,) = fence([kv_seq_2], *sent)
    kv_seq_3 = over_ctx(kv_seq_2, 1)
    if direct:
        sums_of[3].fence(*sent, kv_seq_2)
        kv_seq_1, kv_seq_3 = fence([kv_seq_1, kv_seq_3], sums_of[3].first())
    kv_seqs = (kv_seq, kv_seq_1, kv_seq_2, kv_seq_3)
    (dn_own,) = fence([dn_own], kv_seq_1, kv_seq_3)
    (y_late,) = fence([y], dn_own)
    y_own = lax.psum_scatter(y_late, "tp", scatter_dimension=0, tiled=True)

    mine = pl.BlockSpec((1, rows, width), lambda i, scal: (scal[2], 0, 0))
    dh2, do, dh2_low, sums = call(
        mid_kernel,
        (1,),
        [
            whole((1, dn_rows, width)),
            pl.BlockSpec((1, 8, rows), lambda i, scal: (scal[2], 0, 0)),
            whole((rows, width)),
            mine,
            mine,
            whole((16, width)),
            whole((tp_size, 2, head_cols, half)),
        ],
        [
            whole((rows, width)),
            whole((tp_size, rows // 2, 2 * head_cols)),
            whole((rows, width)),
            whole((16, width)),
        ],
        [
            shape_of((rows, width), F32),
            shape_of((tp_size, rows // 2, 2 * head_cols)),
            shape_of((rows, width)),
            shape_of((16, width), F32),
        ],
        [pltpu.VMEM((width, width), BF16)],
    )(scal, dn_own, gates, h2, n2, cotangent, small, out_pieces)

    kv_block = by_step((rows, 2 * head_cols))
    kv_shape = shape_of((tp_size, rows, 2 * head_cols))
    dq, e0, e1, e2, e3 = call(
        attn_bwd_kernel,
        (tp_size,),
        [by_step((rows, packed))]
        + [kv_block] * 4
        + [by_step((rows // 2, 2 * head_cols)), whole((HD // 2, rows)), whole((HD // 2, rows))],
        [by_step((rows, head_cols))] + [kv_block] * 4,
        [shape_of((tp_size, rows, head_cols))] + [kv_shape] * 4,
        prefetch=2,
    )(scal, prefix, qkv_seq, *kv_seqs, do, cos_t, sin_t)
    if direct:
        early = [sums_of[index] for index in (1, 0)]
        flat = fence([total.far for total in early] + [e1, e3])
        for total, value in zip(early, flat):
            total.far = value
        e1, e3 = flat[2:]
    from_core_1 = over_ctx(e1, 1)
    from_core_3 = over_ctx(e3, 1)
    far = (e2.astype(F32) + from_core_3.astype(F32)).astype(BF16)
    dq, far, dh2_low = fence([dq, far, dh2_low], from_core_1)
    from_y = over_ctx(far, 2)
    if direct:
        away = [total.second() for total in early]
        (dh2_low,) = fence([dh2_low], *away)

    pair_out = pl.BlockSpec((4, 1, width // 8, 2 * head_cols), lambda i, *_: (0, i, 0, 0))
    pair_shape = shape_of((4, tp_size, width // 8, 2 * head_cols))
    first_grads = call(
        first_grads_kernel,
        (tp_size,),
        [
            mine,
            by_step((rows, head_cols)),
            whole((rows, width)),
            pl.BlockSpec((1, 1, rows // 2, 2 * head_cols), lambda i, scal: (i, scal[2], 0, 0)),
        ],
        [pair_out] * 2,
        [pair_shape] * 2,
    )(scal, n1, dq, dh2_low, o_all)

    if direct:
        sum_qo = Sum(first_grads[0], over_ctx(first_grads[1], 1), True)
        (from_y,) = fence([from_y], sum_qo.first())
    from_y, y_own = fence([from_y, y_own])
    activations = lax.all_gather((h2 + y_own[0].astype(F32)).astype(BF16), "tp", axis=0)
    dkv = call(
        swing_kernel,
        (tp_size,),
        [kv_block] * 3 + [whole((rows, packed))] * 2,
        kv_block,
        kv_shape,
        prefetch=0,
    )(e0, from_core_1, from_y, cos_table, sin_table)

    def by_group(shape):
        return pl.BlockSpec((1,) + shape, lambda i, *_: (i, 0, 0))

    gi, sums = call(
        end_kernel,
        (tp_size,),
        [by_group((rows, head_cols)), by_group((rows, 2 * head_cols))]
        + [by_group((packed // 4, width))] * 4
        + [whole((rows, width)), mine, whole((16, width)), whole((16, width))],
        [whole((rows, width)), whole((16, width))],
        [shape_of((rows, width)), shape_of((16, width), F32)],
        [pltpu.VMEM((packed, width), BF16), pltpu.VMEM((rows, width), F32)],
    )(scal, dq, dkv, *w_pieces, dh2, layer_input, small, sums)
    dkv_late, n1_late, sums, gi = fence([dkv, n1, sums, gi])
    if direct:
        dkv_late, sums_of[1].last = fence([dkv_late, sums_of[1].last])
    gi_all = lax.all_gather(gi, "tp", axis=0)
    last_shape = shape_of((4, tp_size + 1, width // 8, 2 * head_cols))
    second_grads = call(
        second_grads_kernel,
        (tp_size + 1,),
        [
            mine,
            pl.BlockSpec((1, rows, 2 * head_cols), lambda i, *_: (jnp.minimum(i, tp_size - 1), 0, 0)),
            whole((16, width)),
        ],
        [pair_out] * 2,
        [last_shape] * 2,
    )(scal, n1_late, dkv_late, sums)

    if direct:
        sum_kv = Sum(second_grads[0], over_ctx(second_grads[1], 1), False)
        (sums_of[3].far,) = fence([sums_of[3].far], *second_grads)
        sum_kv.fence(sums_of[3].far)
        (sums_of[2].far,) = fence([sums_of[2].far], sum_kv.first())
        (sum_qo.far,) = fence([sum_qo.far], sums_of[2].second(), sums_of[3].second())
        away = sum_qo.second()
        early = (1, 0)
        flat = fence([sums_of[index].last for index in early], away)
        for index, value in zip(early, flat):
            sums_of[index].last = value
        results = [sums_of[index].result() for index in (0, 1)]
        (sum_kv.far,) = fence([sum_kv.far], *results)
        away = sum_kv.second()
        (sums_of[3].last,) = fence([sums_of[3].last], away)
        shared_result = sums_of[3].result()
        (sums_of[2].last,) = fence([sums_of[2].last], away)
        results += [sums_of[2].result(), shared_result]
        sum_kv.last, sum_qo.last = fence([sum_kv.last, sum_qo.last], *results)
        grads_qo, grads_kv = sum_qo.result(), sum_kv.result()
    else:
        grads_qo, grads_kv = scatter_plain(*first_grads), scatter_plain(*second_grads)
        results = [scatter_plain(*expert_group), scatter_plain(*shared_group)]
    grads_all = jnp.concatenate(
        [grads_qo, grads_kv[:tp_size], jnp.broadcast_to(grads_kv[tp_size:, :, :128], (tp_size, part, 128))], axis=-1
    )
    grads_all, gi_all = fence([grads_all.astype(BF16), gi_all])
    grads_all = jnp.sum(lax.all_to_all(grads_all, "tp", 0, 0, tiled=True).astype(F32), 0)
    grads_qo, grads_kv = grads_all[:, :2 * head_cols], grads_all[:, 2 * head_cols:4 * head_cols]
    sums = jnp.transpose(grads_all[:, 4 * head_cols:4 * head_cols + 16])
    grad_input = gi_all.astype(F32)
    results = [value.reshape(value.shape[0], 3, part, hidden) for value in results]
    grads_shared = results[-1][0]
    results = results[:-1]
    grads_exp = [jnp.concatenate([value[:, i] for value in results], axis=0) for i in range(3)]

    return (
        activations.reshape(layer_input.shape),
        grad_input.reshape(layer_input.shape),
        sums[8],
        grads_qo[:, :head_cols],
        grads_kv[:, :head_cols],
        grads_kv[:, head_cols:],
        jnp.transpose(grads_qo[:, head_cols:]),
        sums[9],
        jnp.transpose(sums[0:8]),
        grads_exp[0],
        grads_exp[1],
        jnp.transpose(grads_exp[2], (0, 2, 1)),
        grads_shared[0],
        grads_shared[1],
        jnp.transpose(grads_shared[2]),
    )


def solution(mesh):
    placed = (
        P("fsdp", "ctx", None),
        P("fsdp"),
        P("fsdp", "tp"),
        P("fsdp", "tp"),
        P("fsdp", "tp"),
        P("tp", "fsdp"),
        P("fsdp"),
        P("fsdp", None),
        P(None, "fsdp", "tp"),
        P(None, "fsdp", "tp"),
        P(None, "tp", "fsdp"),
        P("fsdp", "tp"),
        P("fsdp", "tp"),
        P("tp", "fsdp"),
        P("fsdp", "ctx", None),
        P("fsdp"),
        P("fsdp", "ctx", None),
    )
    return jax.shard_map(
        functools.partial(body, mesh.shape["fsdp"]),
        mesh=mesh,
        in_specs=placed,
        out_specs=(
            P("fsdp", "ctx", None),
            P("fsdp", "ctx", None),
            P(("fsdp", "ctx")),
            P(("fsdp", "ctx"), "tp"),
            P(("fsdp", "ctx"), "tp"),
            P(("fsdp", "ctx"), "tp"),
            P("tp", ("fsdp", "ctx")),
            P(("fsdp", "ctx")),
            P(("fsdp", "ctx"), None),
            P(None, ("fsdp", "ctx"), "tp"),
            P(None, ("fsdp", "ctx"), "tp"),
            P(None, "tp", ("fsdp", "ctx")),
            P(("fsdp", "ctx"), "tp"),
            P(("fsdp", "ctx"), "tp"),
            P("tp", ("fsdp", "ctx")),
        ),
        check_vma=False,
    )
```

```python
import functools
import math

import jax
import jax.numpy as jnp
from jax import lax
from jax.experimental import pallas as pl
from jax.experimental.pallas import tpu as pltpu
from jax.sharding import PartitionSpec as P

HD = 64
SLOTS = 80
EPS = 1e-06
F32 = jnp.float32
BF16 = jnp.bfloat16
VMEM_BYTES = 56 * 1024 * 1024


def mm(a, b):
    return lax.dot_general(a, b, (((1,), (0,)), ((), ())), preferred_element_type=F32)


def mm_nt(a, b):
    return lax.dot_general(a, b, (((1,), (1,)), ((), ())), preferred_element_type=F32)


def mm_tn(a, b):
    return lax.dot_general(a, b, (((0,), (0,)), ((), ())), preferred_element_type=F32)


def params(steps=1):
    return pltpu.CompilerParams(
        dimension_semantics=("arbitrary",) * steps, vmem_limit_bytes=VMEM_BYTES
    )


def rotation(width):
    row = lax.broadcasted_iota(jnp.int32, (width, width), 0)
    col = lax.broadcasted_iota(jnp.int32, (width, width), 1)
    first = (col % HD) < HD // 2
    minus = first & (row == col + HD // 2)
    plus = jnp.logical_not(first) & (row == col - HD // 2)
    return jnp.where(minus, -1.0, jnp.where(plus, 1.0, 0.0)).astype(BF16)


def row_scale(value):
    return lax.rsqrt(jnp.mean(value * value, -1, keepdims=True) + EPS)


def qkv_kernel(scal, x_ref, own_ref, oth_ref, cos_ref, sin_ref, n1_ref, q_ref, kv_ref, all_ref, w_ref, small_ref, swap):
    half = own_ref.shape[1]
    packed = w_ref.shape[0]

    @pl.when(pl.program_id(0) == 0)
    def _():
        mine = pl.multiple_of(scal[0] * half, half)
        other = pl.multiple_of((1 - scal[0]) * half, half)
        w_ref[:, pl.ds(mine, half)] = own_ref[:packed, :]
        w_ref[:, pl.ds(other, half)] = oth_ref[:packed, :]
        swap[...] = jnp.zeros_like(swap)
        for head in list(range(0, 192, HD)) + list(range(256, 448, HD)):
            middle, end = head + HD // 2, head + HD
            swap[head:middle, :] = -w_ref[middle:end, :]
            swap[middle:end, :] = w_ref[head:middle, :]
        small_ref[...] = w_ref[192:208, :].astype(F32)

    x = x_ref[0].astype(F32)
    n1 = (x * row_scale(x) * small_ref[8:9, :]).astype(BF16)
    n1_ref[0] = n1
    turned = (mm_nt(n1, w_ref[...]) * cos_ref[...] + mm_nt(n1, swap[...]) * sin_ref[...]).astype(BF16)
    q_ref[0] = turned[:, :192]
    kv_ref[0] = turned[:, 256:640]
    all_ref[0] = turned


def visible(scal, prefix, keys, rows):
    key_pos = lax.broadcasted_iota(jnp.int32, (keys, rows), 0) ^ (scal[1] * rows)
    row_pos = lax.broadcasted_iota(jnp.int32, (keys, rows), 1) + scal[1] * rows
    return (key_pos <= row_pos) | (key_pos < prefix)


def only_head(rows, head):
    lane = lax.broadcasted_iota(jnp.int32, rows.shape, 1)
    return jnp.where((lane >= head * HD) & (lane < (head + 1) * HD), rows, jnp.zeros_like(rows))


def softmax(scores, seen):
    scores = jnp.where(seen, scores, -1e30)
    expo = jnp.exp(scores - jnp.max(scores, 0, keepdims=True))
    return expo, 1.0 / jnp.sum(expo, 0, keepdims=True)


def attn_fwd_kernel(scal, prefix, q_ref, kv0, kv1, kv2, kv3, o_ref):
    q = q_ref[0]
    rows, width = q.shape
    heads = width // HD
    kv = jnp.concatenate([kv0[0], kv1[0], kv2[0], kv3[0]], axis=0)
    k = kv[:, :width]
    value_t = jnp.transpose(kv[:, width:])
    seen = visible(scal, prefix[pl.program_id(0)], kv.shape[0], rows)
    outs = []
    for head in range(heads):
        expo, factor = softmax(mm_nt(k, only_head(q, head) * (HD ** -0.5)), seen)
        outs.append(mm(value_t[head * HD:(head + 1) * HD], expo.astype(BF16)) * factor)
    o = jnp.transpose(jnp.concatenate(outs, axis=0))
    o_ref[0] = jnp.concatenate([o[: rows // 2], o[rows // 2:]], axis=1).astype(BF16)


def fill_out_weights(scal, wo, wo_ref):
    pieces, _, width, half = wo_ref.shape
    for piece in range(pieces):
        for index, side in enumerate((scal[0], 1 - scal[0])):
            at = pl.ds(pl.multiple_of(side * half, half), half)
            wo[piece * width:(piece + 1) * width, at] = wo_ref[piece, index]


def post_kernel(scal, o_ref, wo_ref, x_ref, small_ref, routes_ref, n2_ref, h2_ref, gates_ref, slots_ref, wo):
    step = pl.program_id(0)
    width = wo_ref.shape[2]

    @pl.when(step == 0)
    def _():
        fill_out_weights(scal, wo, wo_ref)

    low = jnp.zeros((o_ref.shape[2], wo.shape[1]), F32)
    high = low
    for piece in range(o_ref.shape[0]):
        block = o_ref[piece, 0]
        weights = wo[piece * width:(piece + 1) * width, :]
        low += mm(block[:, :width], weights)
        high += mm(block[:, width:], weights)
    h2 = x_ref[0].astype(F32) + jnp.concatenate([low, high], axis=0)
    n2 = (h2 * row_scale(h2) * small_ref[9:10, :]).astype(BF16)
    n2_ref[0] = n2

    @pl.when(step == scal[2])
    def _():
        h2_ref[...] = h2

    expo = jnp.exp(mm_nt(small_ref[0:8, :].astype(BF16), n2))
    gates_ref[0] = expo / jnp.sum(expo, 0, keepdims=True)
    rows = n2.shape[0]
    expert = lax.broadcasted_iota(jnp.int32, (8, rows), 0)
    named = (routes_ref[0, 0:1, :] == expert) | (routes_ref[0, 1:2, :] == expert)
    before = lax.broadcasted_iota(jnp.int32, (rows, rows), 0) < lax.broadcasted_iota(jnp.int32, (rows, rows), 1)
    place = mm(named.astype(BF16), before.astype(BF16))
    slots_ref[0] = jnp.where(named, place.astype(jnp.int32), -1)


def silu_parts(value):
    sigma = 0.5 * jnp.tanh(0.5 * value) + 0.5
    return sigma, value * sigma


def split_blocks(core, value, blocks):
    rows = value.shape[0] // (2 * blocks)
    value = value.astype(BF16).reshape(blocks, 2, rows, value.shape[1])
    first = core == 0
    return jnp.where(first, value[:, 0], value[:, 1]), jnp.where(first, value[:, 1], value[:, 0])


def put_grads(core, keep_ref, send_ref, index, value):
    keep, send = split_blocks(core, value, keep_ref.shape[0])
    at = slice(index * keep.shape[1], (index + 1) * keep.shape[1])
    keep_ref[:, 0, at, :] = keep
    send_ref[:, 0, at, :] = send


def shared_kernel(
    scal, n2_ref, dy_ref, go_ref, uo_ref, do_ref, g0, g1, g2, g3, u0, u1, u2, u3, d0, d1, d2, d3,
    ys_ref, dn_ref, hid_ref, dab_ref, wgu, wd,
):
    step = pl.program_id(0)
    half = go_ref.shape[0]
    hidden = go_ref.shape[1]

    @pl.when(step == 0)
    def _():
        mine = pl.multiple_of(scal[0] * half, half)
        other = (1 - scal[0]) * half
        wgu[pl.ds(mine, half), :hidden] = go_ref[...]
        wgu[pl.ds(mine, half), hidden:] = uo_ref[...]
        wd[:, pl.ds(mine, half)] = do_ref[...]
        for piece, (g, u, d) in enumerate(((g0, u0, d0), (g1, u1, d1), (g2, u2, d2), (g3, u3, d3))):
            quarter = scal[3] ^ piece
            at = pl.multiple_of(other + quarter * (half // 4), half // 4)
            wgu[pl.ds(at, half // 4), :hidden] = g[...]
            wgu[pl.ds(at, half // 4), hidden:] = u[...]
            at = pl.multiple_of(quarter * (hidden // 4), hidden // 4)
            wd[pl.ds(at, hidden // 4), pl.ds(pl.multiple_of(other, half), half)] = d[...]

    shape = n2_ref.shape[:2]
    n2 = n2_ref[...].reshape(-1, n2_ref.shape[2])
    dy = dy_ref[...].reshape(-1, dy_ref.shape[2])

    def put(ref, value):
        ref[...] = value.astype(BF16).reshape(shape + (value.shape[1],))

    both = mm(n2, wgu[...])
    gate, up = both[:, :hidden], both[:, hidden:]
    sigma, silu = silu_parts(gate)
    hid = (silu * up).astype(BF16)
    put(ys_ref, mm(hid, wd[...]))
    back = mm_nt(dy, wd[...])
    da = (back * up * (sigma * (1.0 + gate * (1.0 - sigma)))).astype(BF16)
    db = (back * silu).astype(BF16)
    dab = jnp.concatenate([da, db], axis=1)
    put(dn_ref, mm_nt(dab, wgu[...]))
    put(hid_ref, hid)
    put(dab_ref, dab)


def put_all_grads(core, keep_ref, send_ref, value, upstream, hid, dab):
    wide = mm_tn(value, dab)
    hidden = hid.shape[1]
    put_grads(core, keep_ref, send_ref, 0, wide[:, :hidden])
    put_grads(core, keep_ref, send_ref, 1, wide[:, hidden:])
    put_grads(core, keep_ref, send_ref, 2, mm_tn(upstream, hid))


def shared_grads_kernel(scal, n2_ref, dy_ref, hid_ref, dab_ref, keep_ref, send_ref):
    values = [ref[...].reshape(-1, ref.shape[-1]) for ref in (n2_ref, dy_ref, hid_ref, dab_ref)]
    put_all_grads(scal[4], keep_ref, send_ref, *values)


def moe_kernel(
    scal, n2_ref, dy_ref, slots_ref, gates_ref, ys_ref, dn_in_ref, gate_own, up_own, down_own,
    w0, w1, w2, w3, r0, r1, r2, r3, d0, d1, d2, d3,
    y_ref, dn_ref, keep_ref, send_ref, wgu_s, wd_s, sems, pick_s, ye_s, dx_s, xe_s, dy_s, de_s, gs_s, dprob_s,
):
    step = pl.program_id(0)
    seqs, rows, width = n2_ref.shape
    hidden, half = down_own.shape[1:]
    experts = slots_ref.shape[1]
    slot_now = step % 2
    mine = pl.multiple_of(scal[0] * half, half)
    other = pl.multiple_of((1 - scal[0]) * half, half)

    def expert_at(index):
        return 2 * ((index // 2) ^ scal[3]) + index % 2

    def place(slot, index):
        at = pl.ds(mine if index < 3 else other, half)
        if index % 3 == 2:
            return wd_s.at[slot, :, at]
        return wgu_s.at[slot, at, pl.ds(index % 3 * hidden, hidden)]

    def fetch(index):
        slot, piece, odd = index % 2, index // 2, index % 2

        def start(number, source):
            pltpu.make_async_copy(source, place(slot, number), sems.at[slot, number]).start()

        for number, ref in enumerate((gate_own, up_own, down_own)):
            start(number, ref.at[expert_at(index)])
        for number, (wide, rest, down) in enumerate(((w0, r0, d0), (w1, r1, d1), (w2, r2, d2), (w3, r3, d3))):
            @pl.when(piece == number)
            def _(wide=wide, rest=rest, down=down):
                start(3, wide.at[pl.ds(pl.multiple_of(odd * half, half), half), :])
                start(5, down.at[pl.ds(pl.multiple_of(odd * hidden, hidden), hidden), :])

                @pl.when(odd == 0)
                def _():
                    start(4, wide.at[pl.ds(2 * half, half), :])

                @pl.when(odd == 1)
                def _():
                    start(4, rest)

    @pl.when(step == 0)
    def _():
        fetch(step)

    @pl.when(step + 1 < experts)
    def _():
        fetch(step + 1)

    @pl.when(step < experts)
    def _():
        expert = expert_at(step)
        for number in range(6):
            source = down_own.at[0] if number % 3 == 2 else gate_own.at[0]
            pltpu.make_async_copy(source, place(slot_now, number), sems.at[slot_now, number]).wait()
        wgu, wd = wgu_s.at[slot_now], wd_s.at[slot_now]

        slot_at = pl.ds(pl.multiple_of(step * SLOTS, 16), SLOTS)
        slot = lax.broadcasted_iota(jnp.int32, (SLOTS, rows), 0)
        odd = step % 2

        @pl.when(odd == 0)
        def _():
            for s in range(seqs):
                at = slice(s * SLOTS, (s + 1) * SLOTS)
                hits = [slots_ref[s, pl.ds(expert + k, 1), :] == slot for k in range(2)]
                pick = jnp.concatenate([hit.astype(BF16) for hit in hits], axis=0)
                pick_s[s, pl.ds(pl.multiple_of(step * SLOTS, 16), 2 * SLOTS), :] = pick
                rows_in = mm(pick, n2_ref[s]).astype(BF16)
                upstream = mm(pick, dy_ref[s])
                for k, hit in enumerate(hits):
                    part = slice(k * SLOTS, (k + 1) * SLOTS)
                    gate_slot = jnp.sum(jnp.where(hit, gates_ref[s, pl.ds(expert + k, 1), :], 0.0), 1, keepdims=True)
                    xe_s[k, at, :] = rows_in[part]
                    dy_s[k, at, :] = upstream[part].astype(BF16)
                    de_s[k, at, :] = (gate_slot * upstream[part]).astype(BF16)
                    gs_s[k, at, :] = jnp.broadcast_to(gate_slot, (SLOTS, 128))

        xe = xe_s[odd]
        both = mm(xe, wgu[...])
        gate, up = both[:, :hidden], both[:, hidden:]
        sigma, silu = silu_parts(gate)
        hid = (silu * up).astype(BF16)
        ye = mm(hid, wd[...])
        dots = jnp.sum(ye * dy_s[odd].astype(F32), 1, keepdims=True)
        ye = (ye * gs_s[odd][:, 0:1]).astype(BF16)
        for s in range(seqs):
            at = slice(s * SLOTS, (s + 1) * SLOTS)
            ye_s[s, slot_at, :] = ye[at]
            hit = slots_ref[s, pl.ds(expert, 1), :] == slot
            dprob_s[s, pl.ds(expert, 1), :] = jnp.sum(jnp.where(hit, dots[at], 0.0), 0, keepdims=True)
        back = mm_nt(de_s[odd], wd[...])
        da = (back * up * (sigma * (1.0 + gate * (1.0 - sigma)))).astype(BF16)
        db = (back * silu).astype(BF16)
        dab = jnp.concatenate([da, db], axis=1)
        dx = mm_nt(dab, wgu[...]).astype(BF16)
        for s in range(seqs):
            dx_s[s, slot_at, :] = dx[s * SLOTS:(s + 1) * SLOTS]
        put_all_grads(scal[4], keep_ref, send_ref, xe, de_s[odd], hid, dab)

    @pl.when(step >= experts)
    def _():
        s = step - experts
        pick = pick_s[s]
        y_ref[0] = (ys_ref[0].astype(F32) + mm_tn(pick, ye_s[s])).astype(BF16)
        dn_ref[0, 0:rows, :] = (dn_in_ref[0].astype(F32) + mm_tn(pick, dx_s[s])).astype(BF16)
        tail = jnp.concatenate([dprob_s[s], jnp.zeros((dn_ref.shape[1] - rows - experts, rows), F32)], axis=0)
        tail = jnp.concatenate([tail, jnp.zeros((tail.shape[0], width - rows), F32)], axis=1)
        dn_ref[0, rows:, :] = tail.astype(BF16)


def norm_back(grad_out, value, scale, gain):
    weighted = grad_out * gain
    return scale * weighted - value * (scale * scale * scale) * jnp.mean(weighted * value, -1, keepdims=True)


def mid_kernel(scal, dn_ref, gates_ref, h2_ref, n2_ref, dy_ref, small_ref, wo_ref, dh2_ref, do_ref, low_ref, sums_ref, wo):
    rows = h2_ref.shape[0]
    pieces, _, width, _ = wo_ref.shape
    fill_out_weights(scal, wo, wo_ref)
    parts = dn_ref[0].astype(F32)
    gates = gates_ref[0]
    dprob = parts[rows:rows + 8, 0:rows]
    dlogits = (gates * (dprob - jnp.sum(dprob * gates, 0, keepdims=True))).astype(BF16)
    dn2 = parts[0:rows, :] + mm_tn(dlogits, small_ref[0:8, :].astype(BF16))
    h2 = h2_ref[...]
    scale = row_scale(h2)
    sums_ref[0:8, :] = mm(dlogits, n2_ref[0])
    sums_ref[8:16, :] = jnp.zeros((8, h2.shape[1]), F32)
    sums_ref[9:10, :] = jnp.sum(dn2 * h2 * scale, 0, keepdims=True)
    dh2 = dy_ref[0].astype(F32) + norm_back(dn2, h2, scale, small_ref[9:10, :])
    dh2_ref[...] = dh2
    low = dh2.astype(BF16)
    low_ref[...] = low
    for piece in range(pieces):
        do = mm_nt(low, wo[piece * width:(piece + 1) * width, :])
        do_ref[piece] = jnp.concatenate([do[: rows // 2], do[rows // 2:]], axis=1).astype(BF16)


def attn_bwd_kernel(
    scal, prefix, q_ref, kv0, kv1, kv2, kv3, do_ref, cos_ref, sin_ref, dq_ref, e0, e1, e2, e3
):
    rows, width = dq_ref.shape[1:]
    q = q_ref[0][:, :width]
    heads = width // HD
    kv = jnp.concatenate([kv0[0], kv1[0], kv2[0], kv3[0]], axis=0)
    k = kv[:, :width]
    v = kv[:, width:]
    key_t = jnp.transpose(k)
    do = jnp.concatenate([do_ref[0][:, :width], do_ref[0][:, width:]], axis=0)
    seen = visible(scal, prefix[scal[2]], kv.shape[0], rows)
    cosine, sine = cos_ref[...], sin_ref[...]
    turned, ds_all, probs_all, q_all, do_all = [], [], [], [], []
    for head in range(heads):
        q_head = only_head(q, head) * (HD ** -0.5)
        do_head = only_head(do, head)
        expo, factor = softmax(mm_nt(k, q_head), seen)
        probs = expo * factor
        dp = mm_nt(v, do_head)
        ds = (probs * (dp - jnp.sum(dp * probs, 0, keepdims=True))).astype(BF16)
        dq = mm(key_t[head * HD:(head + 1) * HD], ds) * (HD ** -0.5)
        first, second = dq[: HD // 2], dq[HD // 2:]
        turned += [first * cosine + second * sine, second * cosine - first * sine]
        ds_all.append(ds)
        probs_all.append(probs.astype(BF16))
        q_all.append(q_head)
        do_all.append(do_head)
    dq_ref[0] = jnp.transpose(jnp.concatenate(turned, axis=0)).astype(BF16)
    dk = mm(jnp.concatenate(ds_all, axis=1), jnp.concatenate(q_all, axis=0))
    dv = mm(jnp.concatenate(probs_all, axis=1), jnp.concatenate(do_all, axis=0))
    dkv = jnp.concatenate([dk, dv], axis=1).astype(BF16)
    for piece, out in enumerate((e0, e1, e2, e3)):
        out[0] = dkv[piece * rows:(piece + 1) * rows]


def swing_kernel(a_ref, b_ref, c_ref, cos_ref, sin_ref, out_ref):
    dkv = a_ref[0].astype(F32) + b_ref[0].astype(F32) + c_ref[0].astype(F32)
    swung = dkv * sin_ref[:, 256:]
    high = swung.astype(BF16)
    low = (swung - high.astype(F32)).astype(BF16)
    turn = rotation(dkv.shape[1])
    out_ref[0] = (dkv * cos_ref[:, 256:] + mm_nt(high, turn) + mm_nt(low, turn)).astype(BF16)


def end_kernel(scal, dq_ref, dkv_ref, w0, w1, w2, w3, dh2_ref, x_ref, small_ref, sums_in, gi_ref, sums_ref, w, total):
    step = pl.program_id(0)
    head_cols = dq_ref.shape[2]
    quarter = w.shape[0] // 4
    for piece, ref in enumerate((w0, w1, w2, w3)):
        at = pl.multiple_of((scal[1] ^ piece) * quarter, quarter)
        w[pl.ds(at, quarter), :] = ref[0]
    part = mm(dq_ref[0], w[:head_cols, :]) + mm(dkv_ref[0], w[256:, :])

    @pl.when(step == 0)
    def _():
        total[...] = part

    @pl.when(step > 0)
    def _():
        total[...] += part

    @pl.when(step == pl.num_programs(0) - 1)
    def _():
        x = x_ref[0].astype(F32)
        dn1 = total[...]
        scale = row_scale(x)
        sums_ref[...] = sums_in[...]
        sums_ref[8:9, :] = jnp.sum(dn1 * x * scale, 0, keepdims=True)
        gi_ref[...] = (dh2_ref[...] + norm_back(dn1, x, scale, small_ref[8:9, :])).astype(BF16)


def first_grads_kernel(scal, n1_ref, dq_ref, low_ref, o_ref, keep_ref, send_ref):
    head_cols = dq_ref.shape[2]
    block = o_ref[0, 0]
    o = jnp.concatenate([block[:, :head_cols], block[:, head_cols:]], axis=0)
    grads = jnp.concatenate([mm_tn(n1_ref[0], dq_ref[0]), mm_tn(low_ref[...], o)], axis=1)
    keep_ref[:, 0], send_ref[:, 0] = split_blocks(scal[4], grads, keep_ref.shape[0])


def second_grads_kernel(scal, n1_ref, dkv_ref, sums_ref, keep_ref, send_ref):
    step = pl.program_id(0)
    last = pl.num_programs(0) - 1

    @pl.when(step < last)
    def _():
        keep_ref[:, 0], send_ref[:, 0] = split_blocks(scal[4], mm_tn(n1_ref[0], dkv_ref[0]), keep_ref.shape[0])

    @pl.when(step == last)
    def _():
        sums = sums_ref[...]
        sums = jnp.concatenate([sums, jnp.zeros((keep_ref.shape[3] - sums.shape[0], sums.shape[1]), F32)], axis=0)
        keep_ref[:, 0], send_ref[:, 0] = split_blocks(scal[4], jnp.transpose(sums), keep_ref.shape[0])


def whole(shape):
    return pl.BlockSpec(shape, lambda *_: (0,) * len(shape))


def by_step(shape):
    return pl.BlockSpec((1,) + shape, lambda i, *_: (i,) + (0,) * len(shape))


def call(kernel, grid, in_specs, out_specs, out_shape, scratch=(), prefetch=1, aliases=None):
    return pl.pallas_call(
        kernel,
        grid_spec=pltpu.PrefetchScalarGridSpec(
            num_scalar_prefetch=prefetch,
            grid=grid,
            in_specs=in_specs,
            out_specs=out_specs,
            scratch_shapes=scratch,
        ),
        out_shape=out_shape,
        input_output_aliases=aliases or {},
        compiler_params=params(len(grid)),
        cost_estimate=pl.CostEstimate(flops=1, bytes_accessed=1, transcendentals=0),
    )


def fence(values, *others):
    values = list(values)
    return list(lax.optimization_barrier((*values, *others))[: len(values)])


def shape_of(shape, dtype=BF16):
    return jax.ShapeDtypeStruct(shape, dtype)


def body(
    fsdp_size,
    layer_input,
    gain_attn,
    query_weight,
    key_weight,
    value_weight,
    output_weight,
    gain_ffn,
    router,
    exp_gate,
    exp_up,
    exp_down,
    shared_gate_weight,
    shared_up_weight,
    shared_down_weight,
    routes,
    prefix,
    cotangent,
):
    seqs, rows, width = layer_input.shape
    experts = exp_gate.shape[0]
    hidden = exp_gate.shape[2]
    head_cols = query_weight.shape[1]
    half = width // 2
    paired = fsdp_size == 2
    ctx = lax.axis_index("ctx")
    tp = lax.axis_index("tp")
    ctx_size = lax.axis_size("ctx")
    tp_size = lax.axis_size("tp")
    side = lax.axis_index("fsdp") if paired else jnp.int32(0)
    weight_ctx = ctx if paired else jnp.int32(0)
    blocks = fsdp_size * ctx_size
    direct = paired and ctx_size == 4 and tp_size == 4
    core = ctx % 2 if direct else jnp.int32(0)
    scal = jnp.stack([side, ctx, tp, weight_ctx, core]).astype(jnp.int32)

    def over_x(value):
        return lax.ppermute(value, "fsdp", [(0, 1), (1, 0)])

    def over_tp(value, bit):
        return lax.ppermute(value, "tp", [(i, i ^ bit) for i in range(tp_size)])

    def over_ctx(value, bit):
        return lax.ppermute(value, "ctx", [(i, i ^ bit) for i in range(ctx_size)])

    columns = jnp.concatenate(
        [
            query_weight.T,
            router.T,
            gain_attn[None],
            gain_ffn[None],
            jnp.zeros((54, query_weight.shape[0]), BF16),
            key_weight.T,
            value_weight.T,
            output_weight,
        ],
        axis=0,
    )
    if paired:
        columns_own, columns_other = columns, over_x(columns)
    else:
        columns = lax.all_gather(columns, "fsdp", axis=1, tiled=True)
        columns_own, columns_other = columns[:, :half], columns[:, half:]

    shared_own = (shared_gate_weight, shared_up_weight, shared_down_weight)
    experts_own = (exp_gate, exp_up, exp_down)
    if paired:

        def quarter(value, parts):
            size = value.shape[0] // parts
            return lax.dynamic_slice_in_dim(value, size * ctx, size, 0).reshape(-1, value.shape[-1])

        gate, up, down = [quarter(stack, 4) for stack in experts_own]
        shared_gate, shared_up, shared_down = [quarter(stack, 4) for stack in shared_own]
        wide = jnp.concatenate([gate, up[:half], shared_gate, shared_up], axis=0)
        rest = up[half:]
        down = jnp.concatenate([down, shared_down], axis=0)
        own = experts_own + shared_own
    else:
        gate_all = lax.all_gather(exp_gate, "fsdp", axis=1, tiled=True)
        up_all = lax.all_gather(exp_up, "fsdp", axis=1, tiled=True)
        down_all = lax.all_gather(exp_down, "fsdp", axis=2, tiled=True)
        sg_all = lax.all_gather(shared_gate_weight, "fsdp", axis=0, tiled=True)
        su_all = lax.all_gather(shared_up_weight, "fsdp", axis=0, tiled=True)
        sd_all = lax.all_gather(shared_down_weight, "fsdp", axis=1, tiled=True)
        own = (gate_all[:, :half], up_all[:, :half], down_all[:, :, :half], sg_all[:half], su_all[:half], sd_all[:, :half])

        def split(value):
            return value.reshape((4, value.shape[0] // 4) + value.shape[1:])

        gate_all, up_all, sg_all, su_all = [
            split(value) for value in (gate_all[:, half:], up_all[:, half:], sg_all[half:], su_all[half:])
        ]
        down_all, sd_all = split(down_all[:, :, half:]), split(sd_all[:, half:])
        wide_p = [
            jnp.concatenate([gate_all[p, 0], gate_all[p, 1], up_all[p, 0], sg_all[p], su_all[p]], axis=0) for p in range(4)
        ]
        rest_p = [up_all[p, 1] for p in range(4)]
        down_p = [jnp.concatenate([down_all[p, 0], down_all[p, 1], sd_all[p]], axis=0) for p in range(4)]

    positions = (ctx * rows + jnp.arange(rows, dtype=jnp.int32)).astype(F32)
    inverse = jnp.exp(jnp.arange(HD // 2, dtype=F32) * (-math.log(10000.0) / (HD // 2)))
    angles = positions[:, None] * inverse[None, :]
    cosine, sine = jnp.cos(angles), jnp.sin(angles)
    heads = head_cols // HD

    def table(value, rest):
        turned = jnp.tile(value, (1, 2 * heads))
        plain = jnp.full((rows, head_cols), rest, F32)
        return jnp.concatenate([turned, plain[:, :64], turned, plain], axis=1)

    cos_table, sin_table = table(cosine, 1.0), table(sine, 0.0)
    routes_t = jnp.pad(jnp.transpose(routes, (0, 2, 1)), ((0, 0), (0, 6), (0, 0)))

    cos_t, sin_t = jnp.transpose(cosine), jnp.transpose(sine)
    columns_other, cos_table, sin_table, cos_t, sin_t = fence([columns_other, cos_table, sin_table, cos_t, sin_t], routes_t)
    if paired:
        columns_other, cos_table, wide, rest, down = fence([columns_other, cos_table, wide, rest, down])
        wide_0 = over_x(wide)
    out_pieces = jnp.stack([columns_own[-head_cols:], columns_other[-head_cols:]])
    out_pieces = lax.all_gather(out_pieces, "tp", axis=0)
    packed = cos_table.shape[1]

    n1, q, kv, qkv, w_qkv, small = call(
        qkv_kernel,
        (seqs,),
        [
            by_step((rows, width)),
            whole((packed + head_cols, half)),
            whole((packed + head_cols, half)),
            whole((rows, packed)),
            whole((rows, packed)),
        ],
        [
            by_step((rows, width)),
            by_step((rows, head_cols)),
            by_step((rows, 2 * head_cols)),
            by_step((rows, packed)),
            whole((packed, width)),
            whole((16, width)),
        ],
        [
            shape_of((seqs, rows, width)),
            shape_of((seqs, rows, head_cols)),
            shape_of((seqs, rows, 2 * head_cols)),
            shape_of((seqs, rows, packed)),
            shape_of((packed, width)),
            shape_of((16, width), F32),
        ],
        [pltpu.VMEM((packed, width), BF16)],
    )(scal, layer_input, columns_own, columns_other, cos_table, sin_table)

    kv_0 = kv
    kv_2 = over_ctx(kv_0, 2)
    kv_1 = over_ctx(kv_0, 1)
    q_now, kv_2 = fence([q, kv_2], kv_1)
    w_part = lax.dynamic_slice_in_dim(w_qkv, (packed // 4) * ctx, packed // 4, 0)
    w_part = jnp.pad(w_part, ((0, 16), (0, 0)))
    if paired:
        kv_2, wide_0, rest, down, w_part = fence([kv_2, wide_0, rest, down, w_part])
        wide_2 = over_ctx(wide_0, 2)
        rest_0 = over_x(rest)
        (down,) = fence([down], rest)
        down_0 = over_x(down)
    kv_3 = over_ctx(kv_2, 1)
    q_now, kv_3, out_pieces = fence([q_now, kv_3, out_pieces])

    o = call(
        attn_fwd_kernel,
        (seqs,),
        [by_step((rows, head_cols))] + [by_step((rows, 2 * head_cols))] * 4,
        by_step((rows // 2, 2 * head_cols)),
        shape_of((seqs, rows // 2, 2 * head_cols)),
        prefetch=2,
    )(scal, prefix, q_now, kv_0, kv_1, kv_2, kv_3)

    o_all = lax.all_gather(o, "tp", axis=0)
    if paired:
        wide_0, rest_0 = fence([wide_0, rest_0], o)
        rest_2, rest_1, wide_1 = over_ctx(rest_0, 2), over_ctx(rest_0, 1), over_ctx(wide_0, 1)
        down_0, wide_2, rest_1, wide_1 = fence([down_0, wide_2, rest_1, wide_1])
        down_2, down_1, wide_3 = over_ctx(down_0, 2), over_ctx(down_0, 1), over_ctx(wide_2, 1)
        (rest_2,) = fence([rest_2], down_0, wide_2)
        down_1, wide_3 = fence([down_1, wide_3], rest_2)
        rest_3 = over_ctx(rest_2, 1)
        o_all, down_1, wide_3 = fence([o_all, down_1, wide_3])
    w_0 = lax.all_gather(fence([w_part], o_all)[0], "tp", axis=0)
    n2, h2, gates, slots = call(
        post_kernel,
        (seqs,),
        [
            pl.BlockSpec((tp_size, 1, rows // 2, 2 * head_cols), lambda i, *_: (0, i, 0, 0)),
            whole((tp_size, 2, head_cols, half)),
            by_step((rows, width)),
            whole((16, width)),
            by_step((8, rows)),
        ],
        [by_step((rows, width)), whole((rows, width)), by_step((8, rows)), by_step((8, rows))],
        [
            shape_of((seqs, rows, width)),
            shape_of((rows, width), F32),
            shape_of((seqs, 8, rows), F32),
            shape_of((seqs, 8, rows), jnp.int32),
        ],
        [pltpu.VMEM((width, width), BF16)],
    )(scal, o_all, out_pieces, layer_input, small, routes_t)

    if paired:
        down_2, rest_3 = fence([down_2, rest_3], n2)
        down_3 = over_ctx(down_2, 1)
        wide_p = (wide_0, wide_1, wide_2, wide_3)
        rest_p = (rest_0, rest_1, rest_2, rest_3)
        down_p = (down_0, down_1, down_2, down_3)

    full = pl.BlockSpec((seqs, rows, width), lambda *_: (0, 0, 0), pipeline_mode=pl.Buffered(1))
    part_rows = 3 * (width // 8)
    upper = [pl.BlockSpec((half // 4, hidden), lambda *_, at=at: (at, 0)) for at in (12, 13)]
    lower = pl.BlockSpec((hidden // 4, half), lambda *_: (8, 0))
    weights = [pltpu.VMEM((width, 2 * hidden), BF16), pltpu.VMEM((hidden, width), BF16)]

    def by_pair(cols):
        return pl.BlockSpec((2, rows, cols), lambda i, *_: (i, 0, 0))

    ys, dn_shared, *shared_hidden = call(
        shared_kernel,
        (seqs // 2,),
        [by_pair(width)] * 2
        + [whole((half, hidden)), whole((half, hidden)), whole((hidden, half))]
        + [upper[0]] * 4
        + [upper[1]] * 4
        + [lower] * 4,
        [by_pair(width)] * 2 + [by_pair(hidden), by_pair(2 * hidden)],
        [shape_of((seqs, rows, width))] * 2 + [shape_of((seqs, rows, hidden)), shape_of((seqs, rows, 2 * hidden))],
        weights,
    )(scal, n2, cotangent, *own[3:], *wide_p, *wide_p, *down_p)

    qkv_late, w_0, ys = fence([qkv, w_0, ys])
    qkv_seq = lax.all_to_all(qkv_late, "tp", 0, 0, tiled=True)
    w_2, w_1 = over_ctx(w_0, 2), over_ctx(w_0, 1)

    def expert_of(i, scal):
        i = jnp.minimum(i, experts - 1)
        return 2 * ((i // 2) ^ scal[3]) + i % 2

    late = pl.BlockSpec((1, rows, width), lambda i, scal: (jnp.maximum(i - experts, 0), 0, 0))

    dn_rows = rows + 16
    slot_rows = seqs * SLOTS
    block = (4, 1, part_rows, hidden)

    expert_grads = pl.BlockSpec(block, lambda i, scal: (0, expert_of(i, scal), 0, 0))
    y, dn, *expert_group = call(
        moe_kernel,
        (experts + seqs,),
        [full, full, whole((seqs, 8, rows)), whole((seqs, 8, rows)), late, late]
        + [pl.BlockSpec(memory_space=pl.ANY)] * 15,
        [late, pl.BlockSpec((1, dn_rows, width), lambda i, *_: (jnp.maximum(i - experts, 0), 0, 0))]
        + [expert_grads] * 2,
        [shape_of((seqs, rows, width)), shape_of((seqs, dn_rows, width))]
        + [shape_of((4, experts, part_rows, hidden))] * 2,
        [pltpu.VMEM((2, width, 2 * hidden), BF16), pltpu.VMEM((2, hidden, width), BF16)]
        + [pltpu.SemaphoreType.DMA((2, 6))]
        + [pltpu.VMEM((seqs, experts * SLOTS, rows), BF16)]
        + [pltpu.VMEM((seqs, experts * SLOTS, width), BF16)] * 2
        + [pltpu.VMEM((2, slot_rows, width), BF16)] * 3
        + [pltpu.VMEM((2, slot_rows, 128), F32), pltpu.VMEM((seqs, 8, rows), F32)],
    )(scal, n2, cotangent, slots, gates, ys, dn_shared, *own[:3], *wide_p, *rest_p, *down_p)

    dn, qkv_seq, w_2, w_1, n2_late, *expert_group = fence([dn, qkv_seq, w_2, w_1, n2, *expert_group])
    w_pieces = (w_0, w_1, w_2, over_ctx(w_2, 1))
    dn_own = lax.psum_scatter(dn, "tp", scatter_dimension=0, tiled=True)
    kv_seq = qkv_seq[:, :, 256:]
    kv_seq_2, kv_seq_1 = over_ctx(kv_seq, 2), over_ctx(kv_seq, 1)

    shared_group = call(
        shared_grads_kernel,
        (1,),
        [full] * 2 + [whole((seqs, rows, hidden)), whole((seqs, rows, 2 * hidden))],
        [whole(block)] * 2,
        [shape_of(block)] * 2,
    )(scal, n2_late, cotangent, *shared_hidden)

    part = width // blocks
    along_x, along_y = side, ctx // 2

    def pick(value, x, y, first, count):
        value = value.reshape((2, 2) + value.shape[1:])
        sizes = (2 if x is None else 1, 2 if y is None else 1, count) + value.shape[3:]
        begin = (0 if x is None else x, 0 if y is None else y, first, 0, 0)
        value = lax.dynamic_slice(value, begin, sizes)
        value = value.reshape(tuple(n for n, at in zip(sizes[:2], (x, y)) if at is None) + sizes[2:])
        return value.astype(F32)

    def indexed(value, index):
        return lax.dynamic_index_in_dim(value, index, 0, False).astype(F32)

    class Sum:
        def __init__(self, keep, got, y_first, first=0, count=None):
            self.keep, self.got, self.y_first = keep, got, y_first
            self.range = (first, count or keep.shape[1])

        def fence(self, *others):
            (self.got,) = fence([self.got], *others)

        def both(self, x, y):
            return pick(self.keep, x, y, *self.range) + pick(self.got, x, y, *self.range)

        def first(self):
            if self.y_first:
                self.sent = self.both(None, 1 - along_y).astype(BF16)
            else:
                self.sent = self.both(1 - along_x, None).astype(BF16)
            self.far = over_ctx(self.sent, 2) if self.y_first else over_x(self.sent)
            return self.sent

        def second(self):
            if self.y_first:
                self.away = (self.both(1 - along_x, along_y) + indexed(self.far, 1 - along_x)).astype(BF16)
                self.last = over_x(self.away)
            else:
                self.away = (self.both(along_x, 1 - along_y) + indexed(self.far, 1 - along_y)).astype(BF16)
                self.last = over_ctx(self.away, 2)
            return self.away

        def result(self):
            mine = indexed(self.far, along_x if self.y_first else along_y)
            return self.both(along_x, along_y) + mine + self.last.astype(F32)

    def scatter_plain(keep, send):
        count, cols = keep.shape[1], keep.shape[3]
        triples = keep.shape[2] // (width // 8)
        both = jnp.stack([keep, send], axis=1).reshape(8, count, triples, width // 8, cols)
        both = jnp.transpose(both, (0, 3, 1, 2, 4)).reshape(blocks, part, count * triples, cols)
        both = jnp.transpose(both, (0, 2, 1, 3)).reshape(blocks, count * triples * part, cols)
        both = lax.psum_scatter(both, ("fsdp", "ctx"), scatter_dimension=0, tiled=True)
        return both.reshape(count, triples * part, cols).astype(F32)

    if direct:
        got, shared_got = over_ctx(expert_group[1], 1), over_ctx(shared_group[1], 1)
        cuts = ((0, 2, True), (2, 2, False), (4, 4, False))
        sums_of = [Sum(expert_group[0], got, y_first, first, count) for first, count, y_first in cuts]
        sums_of.append(Sum(shared_group[0], shared_got, True))
        sent = [sums_of[0].first(), sums_of[1].first()]
        sums_of[2].fence(*sent)
        sent.append(sums_of[2].first())
        (kv_seq_2,) = fence([kv_seq_2], *sent)
    kv_seq_3 = over_ctx(kv_seq_2, 1)
    if direct:
        sums_of[3].fence(*sent, kv_seq_2)
        kv_seq_1, kv_seq_3 = fence([kv_seq_1, kv_seq_3], sums_of[3].first())
    kv_seqs = (kv_seq, kv_seq_1, kv_seq_2, kv_seq_3)
    (dn_own,) = fence([dn_own], kv_seq_1, kv_seq_3)
    (y_late,) = fence([y], dn_own)
    y_own = lax.psum_scatter(y_late, "tp", scatter_dimension=0, tiled=True)

    mine = pl.BlockSpec((1, rows, width), lambda i, scal: (scal[2], 0, 0))
    dh2, do, dh2_low, sums = call(
        mid_kernel,
        (1,),
        [
            whole((1, dn_rows, width)),
            pl.BlockSpec((1, 8, rows), lambda i, scal: (scal[2], 0, 0)),
            whole((rows, width)),
            mine,
            mine,
            whole((16, width)),
            whole((tp_size, 2, head_cols, half)),
        ],
        [
            whole((rows, width)),
            whole((tp_size, rows // 2, 2 * head_cols)),
            whole((rows, width)),
            whole((16, width)),
        ],
        [
            shape_of((rows, width), F32),
            shape_of((tp_size, rows // 2, 2 * head_cols)),
            shape_of((rows, width)),
            shape_of((16, width), F32),
        ],
        [pltpu.VMEM((width, width), BF16)],
    )(scal, dn_own, gates, h2, n2, cotangent, small, out_pieces)

    kv_block = by_step((rows, 2 * head_cols))
    kv_shape = shape_of((tp_size, rows, 2 * head_cols))
    dq, e0, e1, e2, e3 = call(
        attn_bwd_kernel,
        (tp_size,),
        [by_step((rows, packed))]
        + [kv_block] * 4
        + [by_step((rows // 2, 2 * head_cols)), whole((HD // 2, rows)), whole((HD // 2, rows))],
        [by_step((rows, head_cols))] + [kv_block] * 4,
        [shape_of((tp_size, rows, head_cols))] + [kv_shape] * 4,
        prefetch=2,
    )(scal, prefix, qkv_seq, *kv_seqs, do, cos_t, sin_t)
    if direct:
        early = [sums_of[index] for index in (1, 0)]
        flat = fence([total.far for total in early] + [e1, e3])
        for total, value in zip(early, flat):
            total.far = value
        e1, e3 = flat[2:]
    from_core_1 = over_ctx(e1, 1)
    from_core_3 = over_ctx(e3, 1)
    far = (e2.astype(F32) + from_core_3.astype(F32)).astype(BF16)
    dq, far, dh2_low = fence([dq, far, dh2_low], from_core_1)
    from_y = over_ctx(far, 2)
    if direct:
        away = [total.second() for total in early]
        (dh2_low,) = fence([dh2_low], *away)

    pair_out = pl.BlockSpec((4, 1, width // 8, 2 * head_cols), lambda i, *_: (0, i, 0, 0))
    pair_shape = shape_of((4, tp_size, width // 8, 2 * head_cols))
    first_grads = call(
        first_grads_kernel,
        (tp_size,),
        [
            mine,
            by_step((rows, head_cols)),
            whole((rows, width)),
            pl.BlockSpec((1, 1, rows // 2, 2 * head_cols), lambda i, scal: (i, scal[2], 0, 0)),
        ],
        [pair_out] * 2,
        [pair_shape] * 2,
    )(scal, n1, dq, dh2_low, o_all)

    if direct:
        sum_qo = Sum(first_grads[0], over_ctx(first_grads[1], 1), True)
        (from_y,) = fence([from_y], sum_qo.first())
    from_y, y_own = fence([from_y, y_own])
    activations = lax.all_gather((h2 + y_own[0].astype(F32)).astype(BF16), "tp", axis=0)
    dkv = call(
        swing_kernel,
        (tp_size,),
        [kv_block] * 3 + [whole((rows, packed))] * 2,
        kv_block,
        kv_shape,
        prefetch=0,
    )(e0, from_core_1, from_y, cos_table, sin_table)

    def by_group(shape):
        return pl.BlockSpec((1,) + shape, lambda i, *_: (i, 0, 0))

    gi, sums = call(
        end_kernel,
        (tp_size,),
        [by_group((rows, head_cols)), by_group((rows, 2 * head_cols))]
        + [by_group((packed // 4, width))] * 4
        + [whole((rows, width)), mine, whole((16, width)), whole((16, width))],
        [whole((rows, width)), whole((16, width))],
        [shape_of((rows, width)), shape_of((16, width), F32)],
        [pltpu.VMEM((packed, width), BF16), pltpu.VMEM((rows, width), F32)],
    )(scal, dq, dkv, *w_pieces, dh2, layer_input, small, sums)
    dkv_late, n1_late, sums, gi = fence([dkv, n1, sums, gi])
    if direct:
        dkv_late, sums_of[1].last = fence([dkv_late, sums_of[1].last])
    gi_all = lax.all_gather(gi, "tp", axis=0)
    last_shape = shape_of((4, tp_size + 1, width // 8, 2 * head_cols))
    second_grads = call(
        second_grads_kernel,
        (tp_size + 1,),
        [
            mine,
            pl.BlockSpec((1, rows, 2 * head_cols), lambda i, *_: (jnp.minimum(i, tp_size - 1), 0, 0)),
            whole((16, width)),
        ],
        [pair_out] * 2,
        [last_shape] * 2,
    )(scal, n1_late, dkv_late, sums)

    if direct:
        sum_kv = Sum(second_grads[0], over_ctx(second_grads[1], 1), False)
        (sums_of[3].far,) = fence([sums_of[3].far], *second_grads)
        sum_kv.fence(sums_of[3].far)
        (sums_of[2].far,) = fence([sums_of[2].far], sum_kv.first())
        (sum_qo.far,) = fence([sum_qo.far], sums_of[2].second(), sums_of[3].second())
        away = sum_qo.second()
        early = (1, 0)
        flat = fence([sums_of[index].last for index in early], away)
        for index, value in zip(early, flat):
            sums_of[index].last = value
        results = [sums_of[index].result() for index in (0, 1)]
        (sum_kv.far,) = fence([sum_kv.far], *results)
        away = sum_kv.second()
        (sums_of[3].last,) = fence([sums_of[3].last], away)
        shared_result = sums_of[3].result()
        (sums_of[2].last,) = fence([sums_of[2].last], away)
        results += [sums_of[2].result(), shared_result]
        sum_kv.last, sum_qo.last = fence([sum_kv.last, sum_qo.last], *results)
        grads_qo, grads_kv = sum_qo.result(), sum_kv.result()
    else:
        grads_qo, grads_kv = scatter_plain(*first_grads), scatter_plain(*second_grads)
        results = [scatter_plain(*expert_group), scatter_plain(*shared_group)]
    grads_all = jnp.concatenate(
        [grads_qo, grads_kv[:tp_size], jnp.broadcast_to(grads_kv[tp_size:, :, :128], (tp_size, part, 128))], axis=-1
    )
    grads_all, gi_all = fence([grads_all.astype(BF16), gi_all])
    grads_all = jnp.sum(lax.all_to_all(grads_all, "tp", 0, 0, tiled=True).astype(F32), 0)
    grads_qo, grads_kv = grads_all[:, :2 * head_cols], grads_all[:, 2 * head_cols:4 * head_cols]
    sums = jnp.transpose(grads_all[:, 4 * head_cols:4 * head_cols + 16])
    grad_input = gi_all.astype(F32)
    results = [value.reshape(value.shape[0], 3, part, hidden) for value in results]
    grads_shared = results[-1][0]
    results = results[:-1]
    grads_exp = [jnp.concatenate([value[:, i] for value in results], axis=0) for i in range(3)]

    return (
        activations.reshape(layer_input.shape),
        grad_input.reshape(layer_input.shape),
        sums[8],
        grads_qo[:, :head_cols],
        grads_kv[:, :head_cols],
        grads_kv[:, head_cols:],
        jnp.transpose(grads_qo[:, head_cols:]),
        sums[9],
        jnp.transpose(sums[0:8]),
        grads_exp[0],
        grads_exp[1],
        jnp.transpose(grads_exp[2], (0, 2, 1)),
        grads_shared[0],
        grads_shared[1],
        jnp.transpose(grads_shared[2]),
    )


def solution(mesh):
    placed = (
        P("fsdp", "ctx", None),
        P("fsdp"),
        P("fsdp", "tp"),
        P("fsdp", "tp"),
        P("fsdp", "tp"),
        P("tp", "fsdp"),
        P("fsdp"),
        P("fsdp", None),
        P(None, "fsdp", "tp"),
        P(None, "fsdp", "tp"),
        P(None, "tp", "fsdp"),
        P("fsdp", "tp"),
        P("fsdp", "tp"),
        P("tp", "fsdp"),
        P("fsdp", "ctx", None),
        P("fsdp"),
        P("fsdp", "ctx", None),
    )
    return jax.shard_map(
        functools.partial(body, mesh.shape["fsdp"]),
        mesh=mesh,
        in_specs=placed,
        out_specs=(
            P("fsdp", "ctx", None),
            P("fsdp", "ctx", None),
            P(("fsdp", "ctx")),
            P(("fsdp", "ctx"), "tp"),
            P(("fsdp", "ctx"), "tp"),
            P(("fsdp", "ctx"), "tp"),
            P("tp", ("fsdp", "ctx")),
            P(("fsdp", "ctx")),
            P(("fsdp", "ctx"), None),
            P(None, ("fsdp", "ctx"), "tp"),
            P(None, ("fsdp", "ctx"), "tp"),
            P(None, "tp", ("fsdp", "ctx")),
            P(("fsdp", "ctx"), "tp"),
            P(("fsdp", "ctx"), "tp"),
            P("tp", ("fsdp", "ctx")),
        ),
        check_vma=False,
    )
```

```python
import functools
import math

import jax
import jax.numpy as jnp
from jax import lax
from jax.experimental import pallas as pl
from jax.experimental.pallas import tpu as pltpu
from jax.sharding import PartitionSpec as P

HD = 64
SLOTS = 80
EPS = 1e-06
F32 = jnp.float32
BF16 = jnp.bfloat16
VMEM_BYTES = 56 * 1024 * 1024


def mm(a, b):
    return lax.dot_general(a, b, (((1,), (0,)), ((), ())), preferred_element_type=F32)


def mm_nt(a, b):
    return lax.dot_general(a, b, (((1,), (1,)), ((), ())), preferred_element_type=F32)


def mm_tn(a, b):
    return lax.dot_general(a, b, (((0,), (0,)), ((), ())), preferred_element_type=F32)


def params(steps=1):
    return pltpu.CompilerParams(
        dimension_semantics=("arbitrary",) * steps, vmem_limit_bytes=VMEM_BYTES
    )


def rotation(width):
    row = lax.broadcasted_iota(jnp.int32, (width, width), 0)
    col = lax.broadcasted_iota(jnp.int32, (width, width), 1)
    first = (col % HD) < HD // 2
    minus = first & (row == col + HD // 2)
    plus = jnp.logical_not(first) & (row == col - HD // 2)
    return jnp.where(minus, -1.0, jnp.where(plus, 1.0, 0.0)).astype(BF16)


def row_scale(value):
    return lax.rsqrt(jnp.mean(value * value, -1, keepdims=True) + EPS)


def qkv_kernel(scal, x_ref, own_ref, oth_ref, cos_ref, sin_ref, n1_ref, q_ref, kv_ref, all_ref, w_ref, small_ref, swap):
    half = own_ref.shape[1]
    packed = w_ref.shape[0]

    @pl.when(pl.program_id(0) == 0)
    def _():
        mine = pl.multiple_of(scal[0] * half, half)
        other = pl.multiple_of((1 - scal[0]) * half, half)
        w_ref[:, pl.ds(mine, half)] = own_ref[:packed, :]
        w_ref[:, pl.ds(other, half)] = oth_ref[:packed, :]
        swap[...] = jnp.zeros_like(swap)
        for head in list(range(0, 192, HD)) + list(range(256, 448, HD)):
            middle, end = head + HD // 2, head + HD
            swap[head:middle, :] = -w_ref[middle:end, :]
            swap[middle:end, :] = w_ref[head:middle, :]
        small_ref[...] = w_ref[192:208, :].astype(F32)

    x = x_ref[0].astype(F32)
    n1 = (x * row_scale(x) * small_ref[8:9, :]).astype(BF16)
    n1_ref[0] = n1
    turned = (mm_nt(n1, w_ref[...]) * cos_ref[...] + mm_nt(n1, swap[...]) * sin_ref[...]).astype(BF16)
    q_ref[0] = turned[:, :192]
    kv_ref[0] = turned[:, 256:640]
    all_ref[0] = turned


def visible(scal, prefix, keys, rows):
    key_pos = lax.broadcasted_iota(jnp.int32, (keys, rows), 0) ^ (scal[1] * rows)
    row_pos = lax.broadcasted_iota(jnp.int32, (keys, rows), 1) + scal[1] * rows
    return (key_pos <= row_pos) | (key_pos < prefix)


def only_head(rows, head):
    lane = lax.broadcasted_iota(jnp.int32, rows.shape, 1)
    return jnp.where((lane >= head * HD) & (lane < (head + 1) * HD), rows, jnp.zeros_like(rows))


def softmax(scores, seen):
    scores = jnp.where(seen, scores, -1e30)
    expo = jnp.exp(scores - jnp.max(scores, 0, keepdims=True))
    return expo, 1.0 / jnp.sum(expo, 0, keepdims=True)


def attn_fwd_kernel(scal, prefix, q_ref, kv0, kv1, kv2, kv3, o_ref):
    q = q_ref[0]
    rows, width = q.shape
    heads = width // HD
    kv = jnp.concatenate([kv0[0], kv1[0], kv2[0], kv3[0]], axis=0)
    k = kv[:, :width]
    value_t = jnp.transpose(kv[:, width:])
    seen = visible(scal, prefix[pl.program_id(0)], kv.shape[0], rows)
    outs = []
    for head in range(heads):
        expo, factor = softmax(mm_nt(k, only_head(q, head) * (HD ** -0.5)), seen)
        outs.append(mm(value_t[head * HD:(head + 1) * HD], expo.astype(BF16)) * factor)
    o = jnp.transpose(jnp.concatenate(outs, axis=0))
    o_ref[0] = jnp.concatenate([o[: rows // 2], o[rows // 2:]], axis=1).astype(BF16)


def fill_out_weights(scal, wo, wo_ref):
    pieces, _, width, half = wo_ref.shape
    for piece in range(pieces):
        for index, side in enumerate((scal[0], 1 - scal[0])):
            at = pl.ds(pl.multiple_of(side * half, half), half)
            wo[piece * width:(piece + 1) * width, at] = wo_ref[piece, index]


def post_kernel(scal, o_ref, wo_ref, x_ref, small_ref, routes_ref, n2_ref, h2_ref, gates_ref, slots_ref, wo):
    step = pl.program_id(0)
    width = wo_ref.shape[2]

    @pl.when(step == 0)
    def _():
        fill_out_weights(scal, wo, wo_ref)

    low = jnp.zeros((o_ref.shape[2], wo.shape[1]), F32)
    high = low
    for piece in range(o_ref.shape[0]):
        block = o_ref[piece, 0]
        weights = wo[piece * width:(piece + 1) * width, :]
        low += mm(block[:, :width], weights)
        high += mm(block[:, width:], weights)
    h2 = x_ref[0].astype(F32) + jnp.concatenate([low, high], axis=0)
    n2 = (h2 * row_scale(h2) * small_ref[9:10, :]).astype(BF16)
    n2_ref[0] = n2

    @pl.when(step == scal[2])
    def _():
        h2_ref[...] = h2

    expo = jnp.exp(mm_nt(small_ref[0:8, :].astype(BF16), n2))
    gates_ref[0] = expo / jnp.sum(expo, 0, keepdims=True)
    rows = n2.shape[0]
    expert = lax.broadcasted_iota(jnp.int32, (8, rows), 0)
    named = (routes_ref[0, 0:1, :] == expert) | (routes_ref[0, 1:2, :] == expert)
    before = lax.broadcasted_iota(jnp.int32, (rows, rows), 0) < lax.broadcasted_iota(jnp.int32, (rows, rows), 1)
    place = mm(named.astype(BF16), before.astype(BF16))
    slots_ref[0] = jnp.where(named, place.astype(jnp.int32), -1)


def silu_parts(value):
    sigma = 0.5 * jnp.tanh(0.5 * value) + 0.5
    return sigma, value * sigma


def split_blocks(core, value, blocks):
    rows = value.shape[0] // (2 * blocks)
    value = value.astype(BF16).reshape(blocks, 2, rows, value.shape[1])
    first = core == 0
    return jnp.where(first, value[:, 0], value[:, 1]), jnp.where(first, value[:, 1], value[:, 0])


def put_grads(core, keep_ref, send_ref, index, value):
    keep, send = split_blocks(core, value, keep_ref.shape[0])
    at = slice(index * keep.shape[1], (index + 1) * keep.shape[1])
    keep_ref[:, 0, at, :] = keep
    send_ref[:, 0, at, :] = send


def shared_kernel(
    scal, n2_ref, dy_ref, go_ref, uo_ref, do_ref, g0, g1, g2, g3, u0, u1, u2, u3, d0, d1, d2, d3,
    ys_ref, dn_ref, hid_ref, dab_ref, wgu, wd,
):
    step = pl.program_id(0)
    half = go_ref.shape[0]
    hidden = go_ref.shape[1]

    @pl.when(step == 0)
    def _():
        mine = pl.multiple_of(scal[0] * half, half)
        other = (1 - scal[0]) * half
        wgu[pl.ds(mine, half), :hidden] = go_ref[...]
        wgu[pl.ds(mine, half), hidden:] = uo_ref[...]
        wd[:, pl.ds(mine, half)] = do_ref[...]
        for piece, (g, u, d) in enumerate(((g0, u0, d0), (g1, u1, d1), (g2, u2, d2), (g3, u3, d3))):
            quarter = scal[3] ^ piece
            at = pl.multiple_of(other + quarter * (half // 4), half // 4)
            wgu[pl.ds(at, half // 4), :hidden] = g[...]
            wgu[pl.ds(at, half // 4), hidden:] = u[...]
            at = pl.multiple_of(quarter * (hidden // 4), hidden // 4)
            wd[pl.ds(at, hidden // 4), pl.ds(pl.multiple_of(other, half), half)] = d[...]

    shape = n2_ref.shape[:2]
    n2 = n2_ref[...].reshape(-1, n2_ref.shape[2])
    dy = dy_ref[...].reshape(-1, dy_ref.shape[2])

    def put(ref, value):
        ref[...] = value.astype(BF16).reshape(shape + (value.shape[1],))

    both = mm(n2, wgu[...])
    gate, up = both[:, :hidden], both[:, hidden:]
    sigma, silu = silu_parts(gate)
    hid = (silu * up).astype(BF16)
    put(ys_ref, mm(hid, wd[...]))
    back = mm_nt(dy, wd[...])
    da = (back * up * (sigma * (1.0 + gate * (1.0 - sigma)))).astype(BF16)
    db = (back * silu).astype(BF16)
    dab = jnp.concatenate([da, db], axis=1)
    put(dn_ref, mm_nt(dab, wgu[...]))
    put(hid_ref, hid)
    put(dab_ref, dab)


def put_all_grads(core, keep_ref, send_ref, value, upstream, hid, dab):
    wide = mm_tn(value, dab)
    hidden = hid.shape[1]
    put_grads(core, keep_ref, send_ref, 0, wide[:, :hidden])
    put_grads(core, keep_ref, send_ref, 1, wide[:, hidden:])
    put_grads(core, keep_ref, send_ref, 2, mm_tn(upstream, hid))


def shared_grads_kernel(scal, n2_ref, dy_ref, hid_ref, dab_ref, keep_ref, send_ref):
    values = [ref[...].reshape(-1, ref.shape[-1]) for ref in (n2_ref, dy_ref, hid_ref, dab_ref)]
    put_all_grads(scal[4], keep_ref, send_ref, *values)


def moe_kernel(
    scal, n2_ref, dy_ref, slots_ref, gates_ref, ys_ref, dn_in_ref, gate_own, up_own, down_own,
    w0, w1, w2, w3, r0, r1, r2, r3, d0, d1, d2, d3,
    y_ref, dn_ref, keep_ref, send_ref, wgu_s, wd_s, sems, pick_s, yd_s, xe_s, dy_s, de_s, gs_s, dprob_s,
):
    step = pl.program_id(0)
    seqs, rows, width = n2_ref.shape
    hidden, half = down_own.shape[1:]
    experts = slots_ref.shape[1]
    slot_now = step % 2
    mine = pl.multiple_of(scal[0] * half, half)
    other = pl.multiple_of((1 - scal[0]) * half, half)

    def expert_at(index):
        return 2 * ((index // 2) ^ scal[3]) + index % 2

    def place(slot, index):
        at = pl.ds(mine if index < 3 else other, half)
        if index % 3 == 2:
            return wd_s.at[slot, :, at]
        return wgu_s.at[slot, at, pl.ds(index % 3 * hidden, hidden)]

    def fetch(index):
        slot, piece, odd = index % 2, index // 2, index % 2

        def start(number, source):
            pltpu.make_async_copy(source, place(slot, number), sems.at[slot, number]).start()

        for number, ref in enumerate((gate_own, up_own, down_own)):
            start(number, ref.at[expert_at(index)])
        for number, (wide, rest, down) in enumerate(((w0, r0, d0), (w1, r1, d1), (w2, r2, d2), (w3, r3, d3))):
            @pl.when(piece == number)
            def _(wide=wide, rest=rest, down=down):
                start(3, wide.at[pl.ds(pl.multiple_of(odd * half, half), half), :])
                start(5, down.at[pl.ds(pl.multiple_of(odd * hidden, hidden), hidden), :])

                @pl.when(odd == 0)
                def _():
                    start(4, wide.at[pl.ds(2 * half, half), :])

                @pl.when(odd == 1)
                def _():
                    start(4, rest)

    @pl.when(step == 0)
    def _():
        fetch(step)

    @pl.when(step + 1 < experts)
    def _():
        fetch(step + 1)

    @pl.when(step < experts)
    def _():
        expert = expert_at(step)
        for number in range(6):
            source = down_own.at[0] if number % 3 == 2 else gate_own.at[0]
            pltpu.make_async_copy(source, place(slot_now, number), sems.at[slot_now, number]).wait()
        wgu, wd = wgu_s.at[slot_now], wd_s.at[slot_now]

        slot_at = pl.ds(pl.multiple_of(step * SLOTS, 16), SLOTS)
        slot = lax.broadcasted_iota(jnp.int32, (SLOTS, rows), 0)
        odd = step % 2

        @pl.when(odd == 0)
        def _():
            for s in range(seqs):
                at = slice(s * SLOTS, (s + 1) * SLOTS)
                hits = [slots_ref[s, pl.ds(expert + k, 1), :] == slot for k in range(2)]
                pick = jnp.concatenate([hit.astype(BF16) for hit in hits], axis=0)
                pick_s[s, pl.ds(pl.multiple_of(step * SLOTS, 16), 2 * SLOTS), :] = pick
                rows_in = mm(pick, n2_ref[s]).astype(BF16)
                upstream = mm(pick, dy_ref[s])
                for k, hit in enumerate(hits):
                    part = slice(k * SLOTS, (k + 1) * SLOTS)
                    gate_slot = jnp.sum(jnp.where(hit, gates_ref[s, pl.ds(expert + k, 1), :], 0.0), 1, keepdims=True)
                    xe_s[k, at, :] = rows_in[part]
                    dy_s[k, at, :] = upstream[part].astype(BF16)
                    de_s[k, at, :] = (gate_slot * upstream[part]).astype(BF16)
                    gs_s[k, at, :] = jnp.broadcast_to(gate_slot, (SLOTS, 128))

        xe = xe_s[odd]
        both = mm(xe, wgu[...])
        gate, up = both[:, :hidden], both[:, hidden:]
        sigma, silu = silu_parts(gate)
        hid = (silu * up).astype(BF16)
        ye = mm(hid, wd[...])
        dots = jnp.sum(ye * dy_s[odd].astype(F32), 1, keepdims=True)
        ye = (ye * gs_s[odd][:, 0:1]).astype(BF16)
        for s in range(seqs):
            at = slice(s * SLOTS, (s + 1) * SLOTS)
            yd_s[s, slot_at, :width] = ye[at]
            hit = slots_ref[s, pl.ds(expert, 1), :] == slot
            dprob_s[s, pl.ds(expert, 1), :] = jnp.sum(jnp.where(hit, dots[at], 0.0), 0, keepdims=True)
        back = mm_nt(de_s[odd], wd[...])
        da = (back * up * (sigma * (1.0 + gate * (1.0 - sigma)))).astype(BF16)
        db = (back * silu).astype(BF16)
        dab = jnp.concatenate([da, db], axis=1)
        dx = mm_nt(dab, wgu[...]).astype(BF16)
        for s in range(seqs):
            yd_s[s, slot_at, width:] = dx[s * SLOTS:(s + 1) * SLOTS]
        put_all_grads(scal[4], keep_ref, send_ref, xe, de_s[odd], hid, dab)

    @pl.when(step >= experts)
    def _():
        s = step - experts
        pick = pick_s[s]
        both = mm_tn(pick, yd_s[s])
        y_ref[0] = (ys_ref[0].astype(F32) + both[:, :width]).astype(BF16)
        dn_ref[0, 0:rows, :] = (dn_in_ref[0].astype(F32) + both[:, width:]).astype(BF16)
        tail = jnp.concatenate([dprob_s[s], jnp.zeros((dn_ref.shape[1] - rows - experts, rows), F32)], axis=0)
        tail = jnp.concatenate([tail, jnp.zeros((tail.shape[0], width - rows), F32)], axis=1)
        dn_ref[0, rows:, :] = tail.astype(BF16)


def norm_back(grad_out, value, scale, gain):
    weighted = grad_out * gain
    return scale * weighted - value * (scale * scale * scale) * jnp.mean(weighted * value, -1, keepdims=True)


def mid_kernel(scal, dn_ref, gates_ref, h2_ref, n2_ref, dy_ref, small_ref, wo_ref, dh2_ref, do_ref, low_ref, sums_ref, wo):
    rows = h2_ref.shape[0]
    pieces, _, width, _ = wo_ref.shape
    fill_out_weights(scal, wo, wo_ref)
    parts = dn_ref[0].astype(F32)
    gates = gates_ref[0]
    dprob = parts[rows:rows + 8, 0:rows]
    dlogits = (gates * (dprob - jnp.sum(dprob * gates, 0, keepdims=True))).astype(BF16)
    dn2 = parts[0:rows, :] + mm_tn(dlogits, small_ref[0:8, :].astype(BF16))
    h2 = h2_ref[...]
    scale = row_scale(h2)
    sums_ref[0:8, :] = mm(dlogits, n2_ref[0])
    sums_ref[8:16, :] = jnp.zeros((8, h2.shape[1]), F32)
    sums_ref[9:10, :] = jnp.sum(dn2 * h2 * scale, 0, keepdims=True)
    dh2 = dy_ref[0].astype(F32) + norm_back(dn2, h2, scale, small_ref[9:10, :])
    dh2_ref[...] = dh2
    low = dh2.astype(BF16)
    low_ref[...] = low
    for piece in range(pieces):
        do = mm_nt(low, wo[piece * width:(piece + 1) * width, :])
        do_ref[piece] = jnp.concatenate([do[: rows // 2], do[rows // 2:]], axis=1).astype(BF16)


def attn_bwd_kernel(
    scal, prefix, q_ref, kv0, kv1, kv2, kv3, do_ref, cos_ref, sin_ref, dq_ref, e0, e1, e2, e3
):
    rows, width = dq_ref.shape[1:]
    q = q_ref[0][:, :width]
    heads = width // HD
    kv = jnp.concatenate([kv0[0], kv1[0], kv2[0], kv3[0]], axis=0)
    k = kv[:, :width]
    v = kv[:, width:]
    key_t = jnp.transpose(k)
    do = jnp.concatenate([do_ref[0][:, :width], do_ref[0][:, width:]], axis=0)
    seen = visible(scal, prefix[scal[2]], kv.shape[0], rows)
    cosine, sine = cos_ref[...], sin_ref[...]
    turned, ds_all, probs_all, q_all, do_all = [], [], [], [], []
    for head in range(heads):
        q_head = only_head(q, head) * (HD ** -0.5)
        do_head = only_head(do, head)
        expo, factor = softmax(mm_nt(k, q_head), seen)
        probs = expo * factor
        dp = mm_nt(v, do_head)
        ds = (probs * (dp - jnp.sum(dp * probs, 0, keepdims=True))).astype(BF16)
        dq = mm(key_t[head * HD:(head + 1) * HD], ds) * (HD ** -0.5)
        first, second = dq[: HD // 2], dq[HD // 2:]
        turned += [first * cosine + second * sine, second * cosine - first * sine]
        ds_all.append(ds)
        probs_all.append(probs.astype(BF16))
        q_all.append(q_head)
        do_all.append(do_head)
    dq_ref[0] = jnp.transpose(jnp.concatenate(turned, axis=0)).astype(BF16)
    dk = mm(jnp.concatenate(ds_all, axis=1), jnp.concatenate(q_all, axis=0))
    dv = mm(jnp.concatenate(probs_all, axis=1), jnp.concatenate(do_all, axis=0))
    dkv = jnp.concatenate([dk, dv], axis=1).astype(BF16)
    for piece, out in enumerate((e0, e1, e2, e3)):
        out[0] = dkv[piece * rows:(piece + 1) * rows]


def swing_kernel(a_ref, b_ref, c_ref, cos_ref, sin_ref, out_ref):
    dkv = a_ref[0].astype(F32) + b_ref[0].astype(F32) + c_ref[0].astype(F32)
    swung = dkv * sin_ref[:, 256:]
    high = swung.astype(BF16)
    low = (swung - high.astype(F32)).astype(BF16)
    turn = rotation(dkv.shape[1])
    out_ref[0] = (dkv * cos_ref[:, 256:] + mm_nt(high, turn) + mm_nt(low, turn)).astype(BF16)


def end_kernel(scal, dq_ref, dkv_ref, w0, w1, w2, w3, dh2_ref, x_ref, small_ref, sums_in, gi_ref, sums_ref, w, total):
    step = pl.program_id(0)
    head_cols = dq_ref.shape[2]
    quarter = w.shape[0] // 4
    for piece, ref in enumerate((w0, w1, w2, w3)):
        at = pl.multiple_of((scal[1] ^ piece) * quarter, quarter)
        w[pl.ds(at, quarter), :] = ref[0]
    part = mm(dq_ref[0], w[:head_cols, :]) + mm(dkv_ref[0], w[256:, :])

    @pl.when(step == 0)
    def _():
        total[...] = part

    @pl.when(step > 0)
    def _():
        total[...] += part

    @pl.when(step == pl.num_programs(0) - 1)
    def _():
        x = x_ref[0].astype(F32)
        dn1 = total[...]
        scale = row_scale(x)
        sums_ref[...] = sums_in[...]
        sums_ref[8:9, :] = jnp.sum(dn1 * x * scale, 0, keepdims=True)
        gi_ref[...] = (dh2_ref[...] + norm_back(dn1, x, scale, small_ref[8:9, :])).astype(BF16)


def first_grads_kernel(scal, n1_ref, dq_ref, low_ref, o_ref, keep_ref, send_ref):
    head_cols = dq_ref.shape[2]
    block = o_ref[0, 0]
    o = jnp.concatenate([block[:, :head_cols], block[:, head_cols:]], axis=0)
    grads = jnp.concatenate([mm_tn(n1_ref[0], dq_ref[0]), mm_tn(low_ref[...], o)], axis=1)
    keep_ref[:, 0], send_ref[:, 0] = split_blocks(scal[4], grads, keep_ref.shape[0])


def second_grads_kernel(scal, n1_ref, dkv_ref, sums_ref, keep_ref, send_ref):
    step = pl.program_id(0)
    last = pl.num_programs(0) - 1

    @pl.when(step < last)
    def _():
        keep_ref[:, 0], send_ref[:, 0] = split_blocks(scal[4], mm_tn(n1_ref[0], dkv_ref[0]), keep_ref.shape[0])

    @pl.when(step == last)
    def _():
        sums = sums_ref[...]
        sums = jnp.concatenate([sums, jnp.zeros((keep_ref.shape[3] - sums.shape[0], sums.shape[1]), F32)], axis=0)
        keep_ref[:, 0], send_ref[:, 0] = split_blocks(scal[4], jnp.transpose(sums), keep_ref.shape[0])


def whole(shape):
    return pl.BlockSpec(shape, lambda *_: (0,) * len(shape))


def by_step(shape):
    return pl.BlockSpec((1,) + shape, lambda i, *_: (i,) + (0,) * len(shape))


def call(kernel, grid, in_specs, out_specs, out_shape, scratch=(), prefetch=1, aliases=None):
    return pl.pallas_call(
        kernel,
        grid_spec=pltpu.PrefetchScalarGridSpec(
            num_scalar_prefetch=prefetch,
            grid=grid,
            in_specs=in_specs,
            out_specs=out_specs,
            scratch_shapes=scratch,
        ),
        out_shape=out_shape,
        input_output_aliases=aliases or {},
        compiler_params=params(len(grid)),
        cost_estimate=pl.CostEstimate(flops=1, bytes_accessed=1, transcendentals=0),
    )


def fence(values, *others):
    values = list(values)
    return list(lax.optimization_barrier((*values, *others))[: len(values)])


def shape_of(shape, dtype=BF16):
    return jax.ShapeDtypeStruct(shape, dtype)


def body(
    fsdp_size,
    layer_input,
    gain_attn,
    query_weight,
    key_weight,
    value_weight,
    output_weight,
    gain_ffn,
    router,
    exp_gate,
    exp_up,
    exp_down,
    shared_gate_weight,
    shared_up_weight,
    shared_down_weight,
    routes,
    prefix,
    cotangent,
):
    seqs, rows, width = layer_input.shape
    experts = exp_gate.shape[0]
    hidden = exp_gate.shape[2]
    head_cols = query_weight.shape[1]
    half = width // 2
    paired = fsdp_size == 2
    ctx = lax.axis_index("ctx")
    tp = lax.axis_index("tp")
    ctx_size = lax.axis_size("ctx")
    tp_size = lax.axis_size("tp")
    side = lax.axis_index("fsdp") if paired else jnp.int32(0)
    weight_ctx = ctx if paired else jnp.int32(0)
    blocks = fsdp_size * ctx_size
    direct = paired and ctx_size == 4 and tp_size == 4
    core = ctx % 2 if direct else jnp.int32(0)
    scal = jnp.stack([side, ctx, tp, weight_ctx, core]).astype(jnp.int32)

    def over_x(value):
        return lax.ppermute(value, "fsdp", [(0, 1), (1, 0)])

    def over_tp(value, bit):
        return lax.ppermute(value, "tp", [(i, i ^ bit) for i in range(tp_size)])

    def over_ctx(value, bit):
        return lax.ppermute(value, "ctx", [(i, i ^ bit) for i in range(ctx_size)])

    columns = jnp.concatenate(
        [
            query_weight.T,
            router.T,
            gain_attn[None],
            gain_ffn[None],
            jnp.zeros((54, query_weight.shape[0]), BF16),
            key_weight.T,
            value_weight.T,
            output_weight,
        ],
        axis=0,
    )
    if paired:
        columns_own, columns_other = columns, over_x(columns)
    else:
        columns = lax.all_gather(columns, "fsdp", axis=1, tiled=True)
        columns_own, columns_other = columns[:, :half], columns[:, half:]

    shared_own = (shared_gate_weight, shared_up_weight, shared_down_weight)
    experts_own = (exp_gate, exp_up, exp_down)
    if paired:

        def quarter(value, parts):
            size = value.shape[0] // parts
            return lax.dynamic_slice_in_dim(value, size * ctx, size, 0).reshape(-1, value.shape[-1])

        gate, up, down = [quarter(stack, 4) for stack in experts_own]
        shared_gate, shared_up, shared_down = [quarter(stack, 4) for stack in shared_own]
        wide = jnp.concatenate([gate, up[:half], shared_gate, shared_up], axis=0)
        rest = up[half:]
        down = jnp.concatenate([down, shared_down], axis=0)
        own = experts_own + shared_own
    else:
        gate_all = lax.all_gather(exp_gate, "fsdp", axis=1, tiled=True)
        up_all = lax.all_gather(exp_up, "fsdp", axis=1, tiled=True)
        down_all = lax.all_gather(exp_down, "fsdp", axis=2, tiled=True)
        sg_all = lax.all_gather(shared_gate_weight, "fsdp", axis=0, tiled=True)
        su_all = lax.all_gather(shared_up_weight, "fsdp", axis=0, tiled=True)
        sd_all = lax.all_gather(shared_down_weight, "fsdp", axis=1, tiled=True)
        own = (gate_all[:, :half], up_all[:, :half], down_all[:, :, :half], sg_all[:half], su_all[:half], sd_all[:, :half])

        def split(value):
            return value.reshape((4, value.shape[0] // 4) + value.shape[1:])

        gate_all, up_all, sg_all, su_all = [
            split(value) for value in (gate_all[:, half:], up_all[:, half:], sg_all[half:], su_all[half:])
        ]
        down_all, sd_all = split(down_all[:, :, half:]), split(sd_all[:, half:])
        wide_p = [
            jnp.concatenate([gate_all[p, 0], gate_all[p, 1], up_all[p, 0], sg_all[p], su_all[p]], axis=0) for p in range(4)
        ]
        rest_p = [up_all[p, 1] for p in range(4)]
        down_p = [jnp.concatenate([down_all[p, 0], down_all[p, 1], sd_all[p]], axis=0) for p in range(4)]

    positions = (ctx * rows + jnp.arange(rows, dtype=jnp.int32)).astype(F32)
    inverse = jnp.exp(jnp.arange(HD // 2, dtype=F32) * (-math.log(10000.0) / (HD // 2)))
    angles = positions[:, None] * inverse[None, :]
    cosine, sine = jnp.cos(angles), jnp.sin(angles)
    heads = head_cols // HD

    def table(value, rest):
        turned = jnp.tile(value, (1, 2 * heads))
        plain = jnp.full((rows, head_cols), rest, F32)
        return jnp.concatenate([turned, plain[:, :64], turned, plain], axis=1)

    cos_table, sin_table = table(cosine, 1.0), table(sine, 0.0)
    routes_t = jnp.pad(jnp.transpose(routes, (0, 2, 1)), ((0, 0), (0, 6), (0, 0)))

    cos_t, sin_t = jnp.transpose(cosine), jnp.transpose(sine)
    columns_other, cos_table, sin_table, cos_t, sin_t = fence([columns_other, cos_table, sin_table, cos_t, sin_t], routes_t)
    if paired:
        columns_other, cos_table, wide, rest, down = fence([columns_other, cos_table, wide, rest, down])
        wide_0 = over_x(wide)
    out_pieces = jnp.stack([columns_own[-head_cols:], columns_other[-head_cols:]])
    out_pieces = lax.all_gather(out_pieces, "tp", axis=0)
    packed = cos_table.shape[1]

    n1, q, kv, qkv, w_qkv, small = call(
        qkv_kernel,
        (seqs,),
        [
            by_step((rows, width)),
            whole((packed + head_cols, half)),
            whole((packed + head_cols, half)),
            whole((rows, packed)),
            whole((rows, packed)),
        ],
        [
            by_step((rows, width)),
            by_step((rows, head_cols)),
            by_step((rows, 2 * head_cols)),
            by_step((rows, packed)),
            whole((packed, width)),
            whole((16, width)),
        ],
        [
            shape_of((seqs, rows, width)),
            shape_of((seqs, rows, head_cols)),
            shape_of((seqs, rows, 2 * head_cols)),
            shape_of((seqs, rows, packed)),
            shape_of((packed, width)),
            shape_of((16, width), F32),
        ],
        [pltpu.VMEM((packed, width), BF16)],
    )(scal, layer_input, columns_own, columns_other, cos_table, sin_table)

    kv_0 = kv
    kv_2 = over_ctx(kv_0, 2)
    kv_1 = over_ctx(kv_0, 1)
    q_now, kv_2 = fence([q, kv_2], kv_1)
    w_part = lax.dynamic_slice_in_dim(w_qkv, (packed // 4) * ctx, packed // 4, 0)
    w_part = jnp.pad(w_part, ((0, 16), (0, 0)))
    if paired:
        kv_2, wide_0, rest, down, w_part = fence([kv_2, wide_0, rest, down, w_part])
        wide_2 = over_ctx(wide_0, 2)
        rest_0 = over_x(rest)
        (down,) = fence([down], rest)
        down_0 = over_x(down)
    kv_3 = over_ctx(kv_2, 1)
    q_now, kv_3, out_pieces = fence([q_now, kv_3, out_pieces])

    o = call(
        attn_fwd_kernel,
        (seqs,),
        [by_step((rows, head_cols))] + [by_step((rows, 2 * head_cols))] * 4,
        by_step((rows // 2, 2 * head_cols)),
        shape_of((seqs, rows // 2, 2 * head_cols)),
        prefetch=2,
    )(scal, prefix, q_now, kv_0, kv_1, kv_2, kv_3)

    o_all = lax.all_gather(o, "tp", axis=0)
    if paired:
        wide_0, rest_0 = fence([wide_0, rest_0], o)
        rest_2, rest_1, wide_1 = over_ctx(rest_0, 2), over_ctx(rest_0, 1), over_ctx(wide_0, 1)
        down_0, wide_2, rest_1, wide_1 = fence([down_0, wide_2, rest_1, wide_1])
        down_2, down_1, wide_3 = over_ctx(down_0, 2), over_ctx(down_0, 1), over_ctx(wide_2, 1)
        (rest_2,) = fence([rest_2], down_0, wide_2)
        down_1, wide_3 = fence([down_1, wide_3], rest_2)
        rest_3 = over_ctx(rest_2, 1)
        o_all, down_1, wide_3 = fence([o_all, down_1, wide_3])
    w_0 = lax.all_gather(fence([w_part], o_all)[0], "tp", axis=0)
    n2, h2, gates, slots = call(
        post_kernel,
        (seqs,),
        [
            pl.BlockSpec((tp_size, 1, rows // 2, 2 * head_cols), lambda i, *_: (0, i, 0, 0)),
            whole((tp_size, 2, head_cols, half)),
            by_step((rows, width)),
            whole((16, width)),
            by_step((8, rows)),
        ],
        [by_step((rows, width)), whole((rows, width)), by_step((8, rows)), by_step((8, rows))],
        [
            shape_of((seqs, rows, width)),
            shape_of((rows, width), F32),
            shape_of((seqs, 8, rows), F32),
            shape_of((seqs, 8, rows), jnp.int32),
        ],
        [pltpu.VMEM((width, width), BF16)],
    )(scal, o_all, out_pieces, layer_input, small, routes_t)

    if paired:
        down_2, rest_3 = fence([down_2, rest_3], n2)
        down_3 = over_ctx(down_2, 1)
        wide_p = (wide_0, wide_1, wide_2, wide_3)
        rest_p = (rest_0, rest_1, rest_2, rest_3)
        down_p = (down_0, down_1, down_2, down_3)

    full = pl.BlockSpec((seqs, rows, width), lambda *_: (0, 0, 0), pipeline_mode=pl.Buffered(1))
    part_rows = 3 * (width // 8)
    upper = [pl.BlockSpec((half // 4, hidden), lambda *_, at=at: (at, 0)) for at in (12, 13)]
    lower = pl.BlockSpec((hidden // 4, half), lambda *_: (8, 0))
    weights = [pltpu.VMEM((width, 2 * hidden), BF16), pltpu.VMEM((hidden, width), BF16)]

    def by_pair(cols):
        return pl.BlockSpec((2, rows, cols), lambda i, *_: (i, 0, 0))

    ys, dn_shared, *shared_hidden = call(
        shared_kernel,
        (seqs // 2,),
        [by_pair(width)] * 2
        + [whole((half, hidden)), whole((half, hidden)), whole((hidden, half))]
        + [upper[0]] * 4
        + [upper[1]] * 4
        + [lower] * 4,
        [by_pair(width)] * 2 + [by_pair(hidden), by_pair(2 * hidden)],
        [shape_of((seqs, rows, width))] * 2 + [shape_of((seqs, rows, hidden)), shape_of((seqs, rows, 2 * hidden))],
        weights,
    )(scal, n2, cotangent, *own[3:], *wide_p, *wide_p, *down_p)

    qkv_late, w_0, ys = fence([qkv, w_0, ys])
    qkv_seq = lax.all_to_all(qkv_late, "tp", 0, 0, tiled=True)
    w_2, w_1 = over_ctx(w_0, 2), over_ctx(w_0, 1)

    def expert_of(i, scal):
        i = jnp.minimum(i, experts - 1)
        return 2 * ((i // 2) ^ scal[3]) + i % 2

    late = pl.BlockSpec((1, rows, width), lambda i, scal: (jnp.maximum(i - experts, 0), 0, 0))

    dn_rows = rows + 16
    slot_rows = seqs * SLOTS
    block = (4, 1, part_rows, hidden)

    expert_grads = pl.BlockSpec(block, lambda i, scal: (0, expert_of(i, scal), 0, 0))
    y, dn, *expert_group = call(
        moe_kernel,
        (experts + seqs,),
        [full, full, whole((seqs, 8, rows)), whole((seqs, 8, rows)), late, late]
        + [pl.BlockSpec(memory_space=pl.ANY)] * 15,
        [late, pl.BlockSpec((1, dn_rows, width), lambda i, *_: (jnp.maximum(i - experts, 0), 0, 0))]
        + [expert_grads] * 2,
        [shape_of((seqs, rows, width)), shape_of((seqs, dn_rows, width))]
        + [shape_of((4, experts, part_rows, hidden))] * 2,
        [pltpu.VMEM((2, width, 2 * hidden), BF16), pltpu.VMEM((2, hidden, width), BF16)]
        + [pltpu.SemaphoreType.DMA((2, 6))]
        + [pltpu.VMEM((seqs, experts * SLOTS, rows), BF16)]
        + [pltpu.VMEM((seqs, experts * SLOTS, 2 * width), BF16)]
        + [pltpu.VMEM((2, slot_rows, width), BF16)] * 3
        + [pltpu.VMEM((2, slot_rows, 128), F32), pltpu.VMEM((seqs, 8, rows), F32)],
    )(scal, n2, cotangent, slots, gates, ys, dn_shared, *own[:3], *wide_p, *rest_p, *down_p)

    dn, qkv_seq, w_2, w_1, n2_late, *expert_group = fence([dn, qkv_seq, w_2, w_1, n2, *expert_group])
    w_pieces = (w_0, w_1, w_2, over_ctx(w_2, 1))
    dn_own = lax.psum_scatter(dn, "tp", scatter_dimension=0, tiled=True)
    kv_seq = qkv_seq[:, :, 256:]
    kv_seq_2, kv_seq_1 = over_ctx(kv_seq, 2), over_ctx(kv_seq, 1)

    shared_group = call(
        shared_grads_kernel,
        (1,),
        [full] * 2 + [whole((seqs, rows, hidden)), whole((seqs, rows, 2 * hidden))],
        [whole(block)] * 2,
        [shape_of(block)] * 2,
    )(scal, n2_late, cotangent, *shared_hidden)

    part = width // blocks
    along_x, along_y = side, ctx // 2

    def pick(value, x, y, first, count):
        value = value.reshape((2, 2) + value.shape[1:])
        sizes = (2 if x is None else 1, 2 if y is None else 1, count) + value.shape[3:]
        begin = (0 if x is None else x, 0 if y is None else y, first, 0, 0)
        value = lax.dynamic_slice(value, begin, sizes)
        value = value.reshape(tuple(n for n, at in zip(sizes[:2], (x, y)) if at is None) + sizes[2:])
        return value.astype(F32)

    def indexed(value, index):
        return lax.dynamic_index_in_dim(value, index, 0, False).astype(F32)

    class Sum:
        def __init__(self, keep, got, y_first, first=0, count=None):
            self.keep, self.got, self.y_first = keep, got, y_first
            self.range = (first, count or keep.shape[1])

        def fence(self, *others):
            (self.got,) = fence([self.got], *others)

        def both(self, x, y):
            return pick(self.keep, x, y, *self.range) + pick(self.got, x, y, *self.range)

        def first(self):
            if self.y_first:
                self.sent = self.both(None, 1 - along_y).astype(BF16)
            else:
                self.sent = self.both(1 - along_x, None).astype(BF16)
            self.far = over_ctx(self.sent, 2) if self.y_first else over_x(self.sent)
            return self.sent

        def second(self):
            if self.y_first:
                self.away = (self.both(1 - along_x, along_y) + indexed(self.far, 1 - along_x)).astype(BF16)
                self.last = over_x(self.away)
            else:
                self.away = (self.both(along_x, 1 - along_y) + indexed(self.far, 1 - along_y)).astype(BF16)
                self.last = over_ctx(self.away, 2)
            return self.away

        def result(self):
            mine = indexed(self.far, along_x if self.y_first else along_y)
            return self.both(along_x, along_y) + mine + self.last.astype(F32)

    def scatter_plain(keep, send):
        count, cols = keep.shape[1], keep.shape[3]
        triples = keep.shape[2] // (width // 8)
        both = jnp.stack([keep, send], axis=1).reshape(8, count, triples, width // 8, cols)
        both = jnp.transpose(both, (0, 3, 1, 2, 4)).reshape(blocks, part, count * triples, cols)
        both = jnp.transpose(both, (0, 2, 1, 3)).reshape(blocks, count * triples * part, cols)
        both = lax.psum_scatter(both, ("fsdp", "ctx"), scatter_dimension=0, tiled=True)
        return both.reshape(count, triples * part, cols).astype(F32)

    if direct:
        got, shared_got = over_ctx(expert_group[1], 1), over_ctx(shared_group[1], 1)
        cuts = ((0, 2, True), (2, 2, False), (4, 4, False))
        sums_of = [Sum(expert_group[0], got, y_first, first, count) for first, count, y_first in cuts]
        sums_of.append(Sum(shared_group[0], shared_got, True))
        sent = [sums_of[0].first(), sums_of[1].first()]
        sums_of[2].fence(*sent)
        sent.append(sums_of[2].first())
        (kv_seq_2,) = fence([kv_seq_2], *sent)
    kv_seq_3 = over_ctx(kv_seq_2, 1)
    if direct:
        sums_of[3].fence(*sent, kv_seq_2)
        kv_seq_1, kv_seq_3 = fence([kv_seq_1, kv_seq_3], sums_of[3].first())
    kv_seqs = (kv_seq, kv_seq_1, kv_seq_2, kv_seq_3)
    (dn_own,) = fence([dn_own], kv_seq_1, kv_seq_3)
    (y_late,) = fence([y], dn_own)
    y_own = lax.psum_scatter(y_late, "tp", scatter_dimension=0, tiled=True)

    mine = pl.BlockSpec((1, rows, width), lambda i, scal: (scal[2], 0, 0))
    dh2, do, dh2_low, sums = call(
        mid_kernel,
        (1,),
        [
            whole((1, dn_rows, width)),
            pl.BlockSpec((1, 8, rows), lambda i, scal: (scal[2], 0, 0)),
            whole((rows, width)),
            mine,
            mine,
            whole((16, width)),
            whole((tp_size, 2, head_cols, half)),
        ],
        [
            whole((rows, width)),
            whole((tp_size, rows // 2, 2 * head_cols)),
            whole((rows, width)),
            whole((16, width)),
        ],
        [
            shape_of((rows, width), F32),
            shape_of((tp_size, rows // 2, 2 * head_cols)),
            shape_of((rows, width)),
            shape_of((16, width), F32),
        ],
        [pltpu.VMEM((width, width), BF16)],
    )(scal, dn_own, gates, h2, n2, cotangent, small, out_pieces)

    kv_block = by_step((rows, 2 * head_cols))
    kv_shape = shape_of((tp_size, rows, 2 * head_cols))
    dq, e0, e1, e2, e3 = call(
        attn_bwd_kernel,
        (tp_size,),
        [by_step((rows, packed))]
        + [kv_block] * 4
        + [by_step((rows // 2, 2 * head_cols)), whole((HD // 2, rows)), whole((HD // 2, rows))],
        [by_step((rows, head_cols))] + [kv_block] * 4,
        [shape_of((tp_size, rows, head_cols))] + [kv_shape] * 4,
        prefetch=2,
    )(scal, prefix, qkv_seq, *kv_seqs, do, cos_t, sin_t)
    if direct:
        early = [sums_of[index] for index in (1, 0)]
        flat = fence([total.far for total in early] + [e1, e3])
        for total, value in zip(early, flat):
            total.far = value
        e1, e3 = flat[2:]
    from_core_1 = over_ctx(e1, 1)
    from_core_3 = over_ctx(e3, 1)
    far = (e2.astype(F32) + from_core_3.astype(F32)).astype(BF16)
    dq, far, dh2_low = fence([dq, far, dh2_low], from_core_1)
    from_y = over_ctx(far, 2)
    if direct:
        away = [total.second() for total in early]
        (dh2_low,) = fence([dh2_low], *away)

    pair_out = pl.BlockSpec((4, 1, width // 8, 2 * head_cols), lambda i, *_: (0, i, 0, 0))
    pair_shape = shape_of((4, tp_size, width // 8, 2 * head_cols))
    first_grads = call(
        first_grads_kernel,
        (tp_size,),
        [
            mine,
            by_step((rows, head_cols)),
            whole((rows, width)),
            pl.BlockSpec((1, 1, rows // 2, 2 * head_cols), lambda i, scal: (i, scal[2], 0, 0)),
        ],
        [pair_out] * 2,
        [pair_shape] * 2,
    )(scal, n1, dq, dh2_low, o_all)

    if direct:
        sum_qo = Sum(first_grads[0], over_ctx(first_grads[1], 1), True)
        (from_y,) = fence([from_y], sum_qo.first())
    from_y, y_own = fence([from_y, y_own])
    activations = lax.all_gather((h2 + y_own[0].astype(F32)).astype(BF16), "tp", axis=0)
    dkv = call(
        swing_kernel,
        (tp_size,),
        [kv_block] * 3 + [whole((rows, packed))] * 2,
        kv_block,
        kv_shape,
        prefetch=0,
    )(e0, from_core_1, from_y, cos_table, sin_table)

    def by_group(shape):
        return pl.BlockSpec((1,) + shape, lambda i, *_: (i, 0, 0))

    gi, sums = call(
        end_kernel,
        (tp_size,),
        [by_group((rows, head_cols)), by_group((rows, 2 * head_cols))]
        + [by_group((packed // 4, width))] * 4
        + [whole((rows, width)), mine, whole((16, width)), whole((16, width))],
        [whole((rows, width)), whole((16, width))],
        [shape_of((rows, width)), shape_of((16, width), F32)],
        [pltpu.VMEM((packed, width), BF16), pltpu.VMEM((rows, width), F32)],
    )(scal, dq, dkv, *w_pieces, dh2, layer_input, small, sums)
    dkv_late, n1_late, sums, gi = fence([dkv, n1, sums, gi])
    if direct:
        dkv_late, sums_of[1].last = fence([dkv_late, sums_of[1].last])
    gi_all = lax.all_gather(gi, "tp", axis=0)
    last_shape = shape_of((4, tp_size + 1, width // 8, 2 * head_cols))
    second_grads = call(
        second_grads_kernel,
        (tp_size + 1,),
        [
            mine,
            pl.BlockSpec((1, rows, 2 * head_cols), lambda i, *_: (jnp.minimum(i, tp_size - 1), 0, 0)),
            whole((16, width)),
        ],
        [pair_out] * 2,
        [last_shape] * 2,
    )(scal, n1_late, dkv_late, sums)

    if direct:
        sum_kv = Sum(second_grads[0], over_ctx(second_grads[1], 1), False)
        (sums_of[3].far,) = fence([sums_of[3].far], *second_grads)
        sum_kv.fence(sums_of[3].far)
        (sums_of[2].far,) = fence([sums_of[2].far], sum_kv.first())
        (sum_qo.far,) = fence([sum_qo.far], sums_of[2].second(), sums_of[3].second())
        away = sum_qo.second()
        early = (1, 0)
        flat = fence([sums_of[index].last for index in early], away)
        for index, value in zip(early, flat):
            sums_of[index].last = value
        results = [sums_of[index].result() for index in (0, 1)]
        (sum_kv.far,) = fence([sum_kv.far], *results)
        away = sum_kv.second()
        (sums_of[3].last,) = fence([sums_of[3].last], away)
        shared_result = sums_of[3].result()
        (sums_of[2].last,) = fence([sums_of[2].last], away)
        results += [sums_of[2].result(), shared_result]
        sum_kv.last, sum_qo.last = fence([sum_kv.last, sum_qo.last], *results)
        grads_qo, grads_kv = sum_qo.result(), sum_kv.result()
    else:
        grads_qo, grads_kv = scatter_plain(*first_grads), scatter_plain(*second_grads)
        results = [scatter_plain(*expert_group), scatter_plain(*shared_group)]
    grads_all = jnp.concatenate(
        [grads_qo, grads_kv[:tp_size], jnp.broadcast_to(grads_kv[tp_size:, :, :128], (tp_size, part, 128))], axis=-1
    )
    grads_all, gi_all = fence([grads_all.astype(BF16), gi_all])
    grads_all = jnp.sum(lax.all_to_all(grads_all, "tp", 0, 0, tiled=True).astype(F32), 0)
    grads_qo, grads_kv = grads_all[:, :2 * head_cols], grads_all[:, 2 * head_cols:4 * head_cols]
    sums = jnp.transpose(grads_all[:, 4 * head_cols:4 * head_cols + 16])
    grad_input = gi_all.astype(F32)
    results = [value.reshape(value.shape[0], 3, part, hidden) for value in results]
    grads_shared = results[-1][0]
    results = results[:-1]
    grads_exp = [jnp.concatenate([value[:, i] for value in results], axis=0) for i in range(3)]

    return (
        activations.reshape(layer_input.shape),
        grad_input.reshape(layer_input.shape),
        sums[8],
        grads_qo[:, :head_cols],
        grads_kv[:, :head_cols],
        grads_kv[:, head_cols:],
        jnp.transpose(grads_qo[:, head_cols:]),
        sums[9],
        jnp.transpose(sums[0:8]),
        grads_exp[0],
        grads_exp[1],
        jnp.transpose(grads_exp[2], (0, 2, 1)),
        grads_shared[0],
        grads_shared[1],
        jnp.transpose(grads_shared[2]),
    )


def solution(mesh):
    placed = (
        P("fsdp", "ctx", None),
        P("fsdp"),
        P("fsdp", "tp"),
        P("fsdp", "tp"),
        P("fsdp", "tp"),
        P("tp", "fsdp"),
        P("fsdp"),
        P("fsdp", None),
        P(None, "fsdp", "tp"),
        P(None, "fsdp", "tp"),
        P(None, "tp", "fsdp"),
        P("fsdp", "tp"),
        P("fsdp", "tp"),
        P("tp", "fsdp"),
        P("fsdp", "ctx", None),
        P("fsdp"),
        P("fsdp", "ctx", None),
    )
    return jax.shard_map(
        functools.partial(body, mesh.shape["fsdp"]),
        mesh=mesh,
        in_specs=placed,
        out_specs=(
            P("fsdp", "ctx", None),
            P("fsdp", "ctx", None),
            P(("fsdp", "ctx")),
            P(("fsdp", "ctx"), "tp"),
            P(("fsdp", "ctx"), "tp"),
            P(("fsdp", "ctx"), "tp"),
            P("tp", ("fsdp", "ctx")),
            P(("fsdp", "ctx")),
            P(("fsdp", "ctx"), None),
            P(None, ("fsdp", "ctx"), "tp"),
            P(None, ("fsdp", "ctx"), "tp"),
            P(None, "tp", ("fsdp", "ctx")),
            P(("fsdp", "ctx"), "tp"),
            P(("fsdp", "ctx"), "tp"),
            P("tp", ("fsdp", "ctx")),
        ),
        check_vma=False,
    )
```
